32 devices in a mesh: ha: 4 (over y, x), wa: 2 (over core), col: 4 (over z).
Axes of the slice: x: 2, y: 2, z: 4, core: 2. Of those that a mesh axis runs over, the one named last changes fastest.
Arguments:
- features: bfloat16 [8, 32, 16, 2048], P('col', 'ha', 'wa'), may hold values from -60 to 60
- region_boxes: int32 [8, 3, 4], replicated, may hold values from 0 to 32, as said below
- branch_weight: bfloat16 [4, 2048, 512], P(None, None, 'col'), may hold values from -0.125 to 0.125
- branch_gain: float32 [4, 512], P(None, 'col'), may hold values from 0.5 to 1.5
- branch_bias: float32 [4, 512], P(None, 'col'), may hold values from -3 to 3
- conv_weight: bfloat16 [9, 4096, 512], P(None, None, 'col'), may hold values from -0.03125 to 0.03125
- norm_gain: float32 [512], P('col'), may hold values from 0.1 to 1.9
- norm_bias: float32 [512], P('col'), may hold values from -3 to 3
- class_weight: float32 [512, 19], P('col'), may hold values from -0.25 to 0.25
- class_bias: float32 [19], replicated, may hold values from -4 to 4
- cotangent: float32 [8, 32, 16, 19], P('col', 'ha', 'wa'), may hold values from -6 to 6
Outputs:
- logits: float32 [8, 32, 16, 19], P('col', 'ha', 'wa')
- feature_grad: float32 [8, 32, 16, 2048], P('col', 'ha', 'wa')
- branch_grad: float32 [4, 2048, 512], P(None, None, 'col')
- branch_gain_grad: float32 [4, 512], P(None, 'col')
- branch_bias_grad: float32 [4, 512], P(None, 'col')
- conv_grad: float32 [9, 4096, 512], P(None, ('ha', 'wa'), 'col')
- norm_gain_grad: float32 [512], P('col')
- norm_bias_grad: float32 [512], P('col')
- class_weight_grad: float32 [512, 19], P('col')
- class_bias_grad: float32 [19], replicated
The draws below stay inside these ranges and needn't reach their ends.
Inputs may be any that keep to these rules, and one draw needn't show every extreme that they name: `region_boxes`: each canvas holds three disjoint boxes (first row, first column, end row, end column; ends excluded): box 0 = rows [0, 32), columns [0, c); box 1 = rows [0, r), columns [c, 16); box 2 = rows [r, 32), columns [c, 16 - p); with 2 <= c < 8, 2 <= r <= 30, 0 <= p < 8. Pixels outside the boxes are padding.
All inputs are finite; a program needn't handle non-finite values.
Results may differ from the reference program's by a relative error of at most 0.0095.
The reference program's roundings to bfloat16 on the way count: a program that leaves them out, or rounds other values in their place, can miss the bound.
Values may be sent and summed in bfloat16 or wider, within the bound.
A program may use at most 256 MiB of HBM per device.

```python
import math
import jax
import jax.numpy as jnp
from jax import lax

C_IN = 2048
FEAT = 512
CLASSES = 19
NREG = 3
MICRO = 2
TW = 8
C_CAT = 4096
CANVASES = 8
CH = 32
CW = 16
N_COL = 4


def draw_features(key, part):
    key = jax.random.fold_in(key, 11)
    subkeys = jax.random.split(key, 4)
    full_shape = (CANVASES, CH, CW, C_IN)
    pixel_scale = jnp.exp(jax.random.uniform(subkeys[0], (CANVASES, CH, CW, 1), jnp.float32, math.log(0.3), math.log(3.0)))
    channel_scale = jnp.exp(jax.random.uniform(subkeys[1], (1, 1, 1, C_IN), jnp.float32, math.log(0.3), math.log(3.0)))
    values = jnp.clip(jax.random.normal(subkeys[3], full_shape, jnp.float32), -4.0, 4.0)
    return (values * pixel_scale * channel_scale).astype(jnp.bfloat16)


def draw_region_boxes(key, part):
    key = jax.random.fold_in(key, 23)
    subkeys = jax.random.split(key, 3)
    cut_row = jax.random.randint(subkeys[0], (CANVASES,), 2, CH - 1, jnp.int32)
    cut_col = jax.random.randint(subkeys[1], (CANVASES,), 2, TW, jnp.int32)
    padding = jax.random.randint(subkeys[2], (CANVASES,), 0, TW, jnp.int32)
    zeros_now = jnp.zeros((CANVASES,), jnp.int32)
    full_rows = zeros_now + CH
    full_cols = zeros_now + CW
    first = jnp.stack([zeros_now, zeros_now, full_rows, cut_col], -1)
    second = jnp.stack([zeros_now, cut_col, cut_row, full_cols], -1)
    third = jnp.stack([cut_row, cut_col, full_rows, full_cols - padding], -1)
    return jnp.stack([first, second, third], 1).astype(jnp.int32)


def levels(stream_key, shape, shards, smallest, top_value):
    level = 1.0
    for axis_at, parts in shards:
        draws = jax.random.uniform(jax.random.fold_in(jax.random.fold_in(stream_key, 6), axis_at), (parts,), jnp.float32, smallest / len(shards), top_value / len(shards))
        level = level * jnp.repeat(jnp.exp(draws), shape[axis_at] // parts).reshape((-1,) + (1,) * (len(shape) - 1 - axis_at))
    return level


def scatter_about(own_key, shape, scale, reach, pieces=(), held_as=jnp.bfloat16):
    values = scale * jax.random.normal(own_key, shape, jnp.float32)
    if pieces:
        values = values * levels(own_key, shape, pieces, -0.22, 0.18)
    return jnp.clip(values, -reach, reach).astype(held_as)


def setup_inputs(seed: int = 0) -> dict:
    keys = jax.random.split(jax.random.key(seed), 12)
    return {
        "features": draw_features(jax.random.fold_in(keys[11], 71), 0),
        "region_boxes": draw_region_boxes(jax.random.fold_in(keys[11], 71), 0),
        "branch_weight": scatter_about(keys[2], (4, C_IN, FEAT), C_IN ** -0.5, 0.125, ((2, 4),)),
        "branch_gain": jnp.clip(1.0 + 0.1 * jax.random.normal(keys[3], (4, FEAT), jnp.float32), 0.5, 1.5),
        "branch_bias": scatter_about(keys[4], (4, FEAT), 0.5, 3.0, ((1, 4),), jnp.float32),
        "conv_weight": scatter_about(keys[5], (9, C_CAT, FEAT), (9 * C_CAT) ** -0.5, 0.03125, ((2, 4),)),
        "norm_gain": jnp.clip(1.0 + 0.18 * jax.random.normal(keys[6], (FEAT,), jnp.float32), 0.1, 1.9),
        "norm_bias": scatter_about(keys[7], (FEAT,), 0.5, 3.0, ((0, 4),), jnp.float32),
        "class_weight": scatter_about(keys[8], (FEAT, CLASSES), FEAT ** -0.5, 0.25, ((0, 4),), jnp.float32),
        "class_bias": scatter_about(keys[9], (CLASSES,), 1.0, 4.0, (), jnp.float32),
        "cotangent": scatter_about(keys[10], (CANVASES, CH, CW, CLASSES), 1.0, 6.0, ((0, 4), (1, 4), (2, 2)), jnp.float32),
    }


EPSILON = 1e-05
LEVELS = (1, 2, 3, 6)
FULL_ACCURACY = lax.Precision.HIGHEST

@jax.custom_vjp
def low(v):
    return lax.optimization_barrier(v.astype(jnp.bfloat16)).astype(jnp.float32)

@jax.custom_vjp
def low_back(v):
    return v

def low_keep(v):
    return (low(v), None)

def low_pass(kept, grad):
    return (grad,)

def back_keep(v):
    return (v, None)

def back_low(kept, grad):
    return (low(grad),)
low.defvjp(low_keep, low_pass)
low_back.defvjp(back_keep, back_low)

def interpolate(offset, extent, n, bin_ids):
    scaled = offset * (n - 1)
    lower_bin = scaled // (extent - 1)
    fraction = (scaled - lower_bin * (extent - 1)).astype(jnp.float32) / (extent - 1).astype(jnp.float32)
    upper_bin = jnp.minimum(lower_bin + 1, n - 1)
    lower_hit = (bin_ids[None, :] == lower_bin[:, None]).astype(jnp.float32)
    upper_hit = (bin_ids[None, :] == upper_bin[:, None]).astype(jnp.float32)
    return (1.0 - fraction)[:, None] * lower_hit + fraction[:, None] * upper_hit

def layout(region, row_ids, col_ids):
    member_cols = []
    count_cols = []
    weight_per_level = []
    validity = jnp.zeros(row_ids.shape, jnp.float32)
    for n in LEVELS:
        bin_ids = jnp.arange(n, dtype=jnp.int32)
        level_weights = []
        for k in range(region.shape[0]):
            row_start = region[k, 0]
            col_start = region[k, 1]
            height = region[k, 2] - row_start
            width = region[k, 3] - col_start
            row_offset = row_ids - row_start
            col_offset = col_ids - col_start
            inside = (row_offset >= 0) & (row_offset < height) & (col_offset >= 0) & (col_offset < width)
            row_low = bin_ids * height // n
            row_high = ((bin_ids + 1) * height + n - 1) // n
            col_low = bin_ids * width // n
            col_high = ((bin_ids + 1) * width + n - 1) // n
            row_in = (row_offset[:, None] >= row_low[None, :]) & (row_offset[:, None] < row_high[None, :])
            col_in = (col_offset[:, None] >= col_low[None, :]) & (col_offset[:, None] < col_high[None, :])
            member = row_in[:, :, None] & col_in[:, None, :] & inside[:, None, None]
            member_cols.append(member.reshape(-1, n * n).astype(jnp.float32))
            count_cols.append(((row_high - row_low)[:, None] * (col_high - col_low)[None, :]).reshape(n * n))
            row_weight = interpolate(row_offset, height, n, bin_ids)
            col_weight = interpolate(col_offset, width, n, bin_ids)
            bilinear = row_weight[:, :, None] * col_weight[:, None, :] * inside.astype(jnp.float32)[:, None, None]
            level_weights.append(bilinear.reshape(-1, n * n))
            if n == 1:
                validity = validity + inside.astype(jnp.float32)
        weight_per_level.append(jnp.concatenate(level_weights, 1))
    counts = jnp.concatenate(count_cols).astype(jnp.float32)
    return (jnp.concatenate(member_cols, 1), weight_per_level, counts, validity)

def micro_batch(inputs, boxes_now, weights_all):
    branch_weight, branch_gain, branch_bias, conv_weight, norm_gain, norm_bias, class_weight, class_bias = weights_all
    groups, rows_all, cols_all, channels = inputs.shape
    regions = boxes_now.shape[1]
    row_ids = jnp.repeat(jnp.arange(rows_all, dtype=jnp.int32), cols_all)
    col_ids = jnp.tile(jnp.arange(cols_all, dtype=jnp.int32), rows_all)
    member_pixels, weight_per_level, counts, validity = jax.vmap(lambda region: layout(region, row_ids, col_ids))(boxes_now)
    flat_layout = inputs.reshape(groups, rows_all * cols_all, channels)
    partial_sums = jnp.einsum('ger,gek->grk', member_pixels, flat_layout, precision=FULL_ACCURACY)
    pooled = low(partial_sums / counts[:, :, None])
    enlarged_map = []
    offset = 0
    for level_number, n in enumerate(LEVELS):
        span = regions * n * n
        pre = jnp.einsum('cbd,de->cbe', pooled[:, offset:offset + span], branch_weight[level_number], precision=FULL_ACCURACY)
        average = lax.optimization_barrier(jnp.mean(pre, (0, 1)))
        spread = lax.optimization_barrier(jnp.mean(pre * pre, (0, 1))) - average * average
        affine = branch_gain[level_number] * (pre - average) * lax.rsqrt(spread + EPSILON) + branch_bias[level_number]
        branch_result = low(jax.nn.silu(affine))
        enlarged_map.append(jnp.einsum('zdw,zwk->zdk', weight_per_level[level_number], branch_result, precision=FULL_ACCURACY))
        offset = offset + span
    stacked = low(jnp.concatenate([flat_layout * validity[:, :, None]] + enlarged_map, -1))
    stacked = stacked.reshape(groups, rows_all, cols_all, -1)
    padded = jnp.pad(stacked, ((0, 0), (1, 1), (1, 1), (0, 0)))
    convolved = jnp.zeros((groups, rows_all, cols_all, conv_weight.shape[2]), jnp.float32)
    for row_tap in range(3):
        for col_tap in range(3):
            window = padded[:, row_tap:row_tap + rows_all, col_tap:col_tap + cols_all]
            convolved = convolved + jnp.einsum('chwk,ke->chwe', window, conv_weight[3 * row_tap + col_tap], precision=FULL_ACCURACY)
    convolved = low_back(convolved)
    valid_grid = validity.reshape(groups, rows_all, cols_all, 1)
    valid_total = jnp.sum(valid_grid)
    average = lax.optimization_barrier(jnp.sum(convolved * valid_grid, (0, 1, 2))) / valid_total
    spread = lax.optimization_barrier(jnp.sum(convolved * convolved * valid_grid, (0, 1, 2))) / valid_total - average * average
    hidden = jax.nn.silu(norm_gain * (convolved - average) * lax.rsqrt(spread + EPSILON) + norm_bias)
    scores = jnp.einsum('chwe,ek->chwk', hidden, class_weight, precision=FULL_ACCURACY)
    return (scores + class_bias) * valid_grid

def reference(features, region_boxes, branch_weight, branch_gain, branch_bias, conv_weight, norm_gain, norm_bias, class_weight, class_bias, cotangent):
    grouped_boxes = region_boxes.reshape(N_COL, MICRO, NREG, 4).swapaxes(0, 1)

    def forward(inputs, *weights_all):
        grouped = inputs.reshape(N_COL, MICRO, CH, CW, C_IN).swapaxes(0, 1)
        runner = jax.checkpoint(lambda batch_pair: micro_batch(batch_pair[0], batch_pair[1], weights_all))
        result = lax.map(runner, (grouped, grouped_boxes))
        return result.swapaxes(0, 1).reshape(CANVASES, CH, CW, CLASSES)
    primals = (features.astype(jnp.float32), branch_weight.astype(jnp.float32), branch_gain, branch_bias, conv_weight.astype(jnp.float32), norm_gain, norm_bias, class_weight, class_bias)
    logits, pullback = jax.vjp(forward, *primals)
    grads = pullback(cotangent)
    return (logits, grads[0], grads[1], grads[2], grads[3], grads[4], grads[5], grads[6], grads[7], grads[8])
```

```python
import functools

import jax
import jax.numpy as jnp
import numpy as np
from jax import lax
from jax.experimental import pallas as pl
from jax.experimental.pallas import tpu as pltpu
from jax.sharding import PartitionSpec as P

EPSILON = 1e-05
LEVELS = (1, 2, 3, 6)
FULL_ACCURACY = lax.Precision.HIGHEST
MESH = pl.DeviceIdType.MESH


SPANS = (16, 16, 32, 112)
STARTS = (0, 16, 32, 64)
BINS = 176
WIDE = 112
TAPS = 9


def whole_canvas_plan(mesh):
    return mesh.shape["ha"] == 4 and mesh.shape["wa"] == 2 and mesh.shape["col"] == 4


def bin_tables():
    lanes = np.zeros((4, 8, 128), np.float32)
    rows = np.zeros((5, BINS, 128), np.float32)
    rows[3] = 1.0
    for level, n in enumerate(LEVELS):
        lanes[level, 3, :] = n - 1
        for k in range(3):
            for i in range(n):
                for j in range(n):
                    b = (k * n + i) * n + j
                    lanes[level, :3, b] = (k, i, j)
                    lanes[level, 4, b] = 1.0
                    row = STARTS[level] + b
                    for at, value in enumerate((k, i, j, n, 1.0)):
                        rows[at, row] = value
    return lanes, rows


def dot(a, b, dims=((1,), (0,)), precision=None):
    return lax.dot_general(a, b, (dims, ((), ())), precision=precision, preferred_element_type=jnp.float32)


ROWS_T = ((0,), (0,))
BOTH_LAST = ((1,), (1,))


def halves(value):
    high = value.astype(jnp.bfloat16)
    return high, (value - high.astype(jnp.float32)).astype(jnp.bfloat16)


def pick3(index, values):
    return jnp.where(index == 0.0, values[0], jnp.where(index == 1.0, values[1], values[2]))


class Sems:
    def __init__(self):
        self.count = 0

    def take(self, n=1):
        at = self.count
        self.count += n
        return at


def head_kernel(
    boxes, lane_table, row_table, feat, seeds, wconv, wbranch, bgain, bbias, ngain, nbias, cwt,
    logits_out, fgrad_out, bgrad_out, small_out, cgrad_out,
    x, lv, wall, wb, uh, ul, mt, cnt, po, pre, prr, bos, bo, val, yp, p, cr, gc, g9, gp3,
    dxf, sbu, sbd, rxu, rxd, gb, grr, gpre, gpa, gps, gpr, dw, dwr, bg, bgr, bgh, seed_in, sd, lt, ltr, lts,
    st, str_, small, smr, nb_s, af_s, cn_s, bga, fg, sems,
):
    f32, bf16 = jnp.float32, jnp.bfloat16
    q, w, z = lax.axis_index("ha"), lax.axis_index("wa"), lax.axis_index("col")
    xq, yq = lax.rem(q, 2), lax.div(q, 2)
    g = 2 * xq + yq
    zm = lax.div(z, 2)
    zz = z * (1 - zm) + (3 - z) * zm
    names = Sems()
    later = []

    def peer(kx, ky, kw):
        px = xq + kx - 2 * kx * xq
        py = yq + ky - 2 * ky * yq
        return {"ha": 2 * py + px, "wa": w + kw - 2 * kw * w}, 2 * px + py

    def copy(src, dst, ss, rs, dev):
        return pltpu.make_async_remote_copy(
            src_ref=src, dst_ref=dst, send_sem=sems.at[ss], recv_sem=sems.at[rs], device_id=dev, device_id_type=MESH
        )

    def zpeer(j):
        return {"col": lax.rem(z + j, 4)}

    plane = [(kx, ky, kw) for kw in (0, 1) for ky in (0, 1) for kx in (0, 1) if kx + ky + kw]
    chips = [(1, 0), (0, 1), (1, 1)]

    g512 = pl.multiple_of(g * 512, 512)
    weight_copies = []
    for t in range(TAPS):
        for part in range(2):
            s = names.take()
            weight_copies.append(
                pltpu.make_async_copy(
                    wconv.at[t, pl.ds(2048 * part + g512, 512), :],
                    wall.at[pl.ds(512 * part, 512), pl.ds(128 * t, 128)],
                    sems.at[s],
                )
            )
    s = names.take()
    weight_copies.append(pltpu.make_async_copy(wbranch.at[:, pl.ds(g512, 512), :], wb, sems.at[s]))
    for c in weight_copies:
        c.start()

    prr[...] = jnp.zeros(prr.shape, f32)
    grr[...] = jnp.zeros(grr.shape, bf16)
    bo[...] = jnp.zeros(bo.shape, bf16)
    yp[:, 0:8, :] = jnp.zeros((2, 8, 1152), f32)
    yp[:, 264:272, :] = jnp.zeros((2, 8, 1152), f32)
    gp3[:, :, 0:8, :] = jnp.zeros((3, 2, 8, 128), f32)
    gp3[:, :, 264:272, :] = jnp.zeros((3, 2, 8, 128), f32)
    small[...] = jnp.zeros(small.shape, f32)
    st[...] = jnp.zeros(st.shape, f32)

    barrier = pltpu.get_barrier_semaphore()
    for kx, ky, kw in plane:
        pl.semaphore_signal(barrier, 1, device_id=peer(kx, ky, kw)[0], device_id_type=MESH)
    for j in (1, 2, 3):
        pl.semaphore_signal(barrier, 1, device_id=zpeer(j), device_id_type=MESH)
    pl.semaphore_wait(barrier, 10)

    q64 = pl.multiple_of(64 * q, 64)
    a_send, a_recv = names.take(8), names.take(8)
    a_copies = []
    own_row = pl.multiple_of(256 * w + 64 * q, 64)
    for n, (kx, ky, kw) in enumerate(plane):
        dev, block = peer(kx, ky, kw)
        c = copy(
            feat.at[dev["wa"], :, pl.ds(pl.multiple_of(512 * block, 512), 512)],
            x.at[z, pl.ds(own_row, 64), :],
            a_send + n, a_recv + n, dev,
        )
        c.start()
        a_copies.append(c)
    own = pltpu.make_async_copy(feat.at[w, :, pl.ds(g512, 512)], x.at[z, pl.ds(own_row, 64), :], sems.at[a_send + 7])
    own.start()
    sc_send, sc_recv = names.take(), names.take()
    seed_copy = copy(seeds.at[1 - w], seed_in.at[0], sc_send, sc_recv, peer(0, 0, 1)[0])
    seed_copy.start()

    def scalars(canvas):
        index = 2 * canvas + w
        return [[boxes[index * 12 + 4 * k + e] for k in range(3)] for e in range(4)]

    def px(rows, lanes, axis, start=0):
        at = lax.broadcasted_iota(jnp.int32, (rows, lanes), axis) + start
        half = at // 256
        return (at // 8 % 32).astype(f32), (half * 8 + at % 8).astype(f32)

    def layout(c):
        top, left, bottom, right = [[v.astype(f32) for v in values] for values in scalars(c)]
        y, xx = px(512, 128, 0)
        ok = jnp.zeros((512, 128), f32)
        for k in range(3):
            ok = jnp.where((y >= top[k]) & (y < bottom[k]) & (xx >= left[k]) & (xx < right[k]), 1.0, ok)
        val[c] = ok
        table = lane_table[g]
        box, bi, bj, n1, real = [table[e:e + 1] for e in range(5)]
        t_, l_, b_, r_ = [pick3(box, v) for v in (top, left, bottom, right)]
        h1, w1 = b_ - t_ - 1.0, r_ - l_ - 1.0
        rw = jnp.maximum(1.0 - jnp.abs((y - t_) * n1 - bi * h1) / h1, 0.0)
        cw = jnp.maximum(1.0 - jnp.abs((xx - l_) * n1 - bj * w1) / w1, 0.0)
        inside = (y >= t_) & (y < b_) & (xx >= l_) & (xx < r_) & (real > 0.0)
        weights = jnp.where(inside, rw * cw, 0.0)
        high, low = halves(weights)
        uh[c] = high
        ul[c] = low
        box, bi, bj, n, real = [row_table[e] for e in range(5)]
        t_, l_, b_, r_ = [pick3(box, v) for v in (top, left, bottom, right)]
        h, wd = b_ - t_, r_ - l_
        row_low = jnp.floor((bi * h + 0.5) / n)
        row_high = jnp.floor(((bi + 1.0) * h + n - 0.5) / n)
        col_low = jnp.floor((bj * wd + 0.5) / n)
        col_high = jnp.floor(((bj + 1.0) * wd + n - 0.5) / n)
        cnt[c] = jnp.where(real > 0.0, (row_high - row_low) * (col_high - col_low), 1.0)
        for chunk in range(4):
            y, xx = px(BINS, 128, 1, 128 * chunk)
            u, v = y - t_, xx - l_
            member = (u >= row_low) & (u < row_high) & (v >= col_low) & (v < col_high) & (real > 0.0)
            mt[c, :, 128 * chunk:128 * chunk + 128] = jnp.where(member, 1.0, 0.0).astype(bf16)

    def combine():
        out = []
        zs = []
        for b in range(3):
            acc = [None, None]
            for h in range(2):
                for a in range(3):
                    t = 3 * a + b
                    piece = yp[h, 8 * a:8 * a + 256, 128 * t:128 * t + 128]
                    acc[h] = piece if acc[h] is None else acc[h] + piece
            zs.append(acc)
        col = lax.broadcasted_iota(jnp.int32, (256, 128), 0) % 8
        first, last = col == 0, col == 7
        out0 = zs[1][0] + jnp.where(first, 0.0, pltpu.roll(zs[0][0], 1, 0))
        out0 = out0 + jnp.where(last, pltpu.roll(zs[2][1], 7, 0), pltpu.roll(zs[2][0], 255, 0))
        out1 = zs[1][1] + jnp.where(first, pltpu.roll(zs[0][0], 249, 0), pltpu.roll(zs[0][1], 1, 0))
        out1 = out1 + jnp.where(last, 0.0, pltpu.roll(zs[2][1], 255, 0))
        return out0, out1

    def conv_part(operand, part):
        for h in range(2):
            yp[h, 8:264, :] = dot(operand[256 * h:256 * h + 256], wall[512 * part:512 * part + 512, :])
        return combine()

    e_send, e_recv = names.take(16), names.take(12)

    def pre_copy(level, c, kx, ky):
        slot = kx + 2 * ky - 1
        return copy(
            pre.at[c, pl.ds(STARTS[level], SPANS[level]), :],
            prr.at[slot, c, pl.ds(0, SPANS[level]), :],
            e_send + 4 * level + c, e_recv + 4 * slot + c, peer(kx, ky, 0)[0],
        )

    def to_level_owner(level, action):
        lx, ly = level // 2, level % 2
        for kx, ky in chips:
            wanted = (xq + kx - 2 * kx * xq == lx) & (yq + ky - 2 * ky * yq == ly)
            pl.when(wanted)(functools.partial(action, kx, ky))

    def process(c):
        po_sum = dot(mt[c], x[c])
        for chunk in range(4):
            po[c, :, 128 * chunk:128 * chunk + 128] = (po_sum[:, 128 * chunk:128 * chunk + 128] / cnt[c]).astype(bf16)
        for level in range(4):
            rows = slice(STARTS[level], STARTS[level] + SPANS[level])
            pre[c, rows, :] = dot(po[c, rows, :], wb[level])
        for level in range(4):
            to_level_owner(level, lambda kx, ky, level=level: pre_copy(level, c, kx, ky).start())
        out0, out1 = conv_part(x[c], 0)
        p[c, 0] = out0
        p[c, 1] = out1

    for c in range(4):
        layout(c)

    for c in weight_copies:
        c.wait()
    for c in a_copies:
        c.wait_recv()
    own.wait()
    ok = val[z]
    for chunk in range(4):
        cols = slice(128 * chunk, 128 * chunk + 128)
        x[z, :, cols] = (x[z, :, cols].astype(f32) * ok).astype(bf16)

    up_send, up_recv, dn_send, dn_recv = names.take(3), names.take(3), names.take(3), names.take(3)

    def up_copy(k):
        return copy(x.at[z - k], x.at[z - k], up_send + k, up_recv + k, {"col": z + 1})

    def dn_copy(k):
        return copy(x.at[z + k], x.at[z + k], dn_send + k, dn_recv + k, {"col": z - 1})

    def up_wait(k):
        copy(x.at[z - k], x.at[z - k], up_send + k - 1, up_recv + k - 1, {"col": z}).wait_recv()

    def dn_wait(k):
        copy(x.at[z + k], x.at[z + k], dn_send + k - 1, dn_recv + k - 1, {"col": z}).wait_recv()

    pl.when(z < 3)(lambda: up_copy(0).start())
    pl.when(z > 0)(lambda: dn_copy(0).start())

    seed_copy.wait_recv()
    sd[z] = seeds[w] + seed_in[0]
    sz_send, sz_recv = names.take(3), names.take(3)
    for j in (1, 2, 3):
        copy(sd.at[z], sd.at[z], sz_send + j - 1, sz_recv + j - 1, zpeer(j)).start()

    process(z)
    for k in (1, 2, 3):

        @pl.when(z >= k)
        def _():
            up_wait(k)
            if k < 3:
                pl.when(z < 3)(lambda: up_copy(k).start())

        @pl.when(z + k <= 3)
        def _():
            dn_wait(k)
            if k < 3:
                pl.when(z > 0)(lambda: dn_copy(k).start())

        pl.when(z >= k)(lambda: process(z - k))
        pl.when(z + k <= 3)(lambda: process(z + k))

    for c in range(4):
        for kx, ky in chips:
            slot = kx + 2 * ky - 1
            for level in range(4):

                @pl.when(g == level)
                def _():
                    copy(
                        pre.at[c, pl.ds(STARTS[level], SPANS[level]), :],
                        prr.at[slot, c, pl.ds(0, SPANS[level]), :],
                        e_send, e_recv + 4 * slot + c, peer(0, 0, 1)[0],
                    ).wait_recv()

    nb_s[...] = jnp.zeros(nb_s.shape, f32)
    for level in range(4):

        @pl.when(g == level)
        def _():
            for c in range(4):
                nb_s[c, 0:SPANS[level], :] = pre[c, STARTS[level]:STARTS[level] + SPANS[level], :]

    level_n = jnp.where(g == 0, 1.0, jnp.where(g == 1, 2.0, jnp.where(g == 2, 3.0, 6.0)))
    samples = 12.0 * level_n * level_n

    def rows_of(value):
        return value.reshape(4 * WIDE, 128)

    pre_all = rows_of(nb_s[...] + prr[0] + prr[1] + prr[2])
    average = jnp.sum(pre_all, 0, keepdims=True) / samples
    spread = jnp.sum(pre_all * pre_all, 0, keepdims=True) / samples - average * average
    b_inverse = lax.rsqrt(spread + EPSILON)
    b_gain = bgain[pl.ds(g, 1), :]
    b_norm = (pre_all - average) * b_inverse
    b_act = b_gain * b_norm + bbias[pl.ds(g, 1), :]
    nb_s[...] = b_norm.reshape(4, WIDE, 128)
    logistic = jax.nn.sigmoid(b_act)
    af_s[...] = (logistic * (1.0 + b_act * (1.0 - logistic))).reshape(4, WIDE, 128)
    bos[...] = (b_act * logistic).astype(bf16).reshape(4, WIDE, 128)

    f_send, f_recv = names.take(3), names.take(3)

    def share(ref, at):
        return ref.at[:, pl.ds(0, WIDE), pl.ds(pl.multiple_of(128 * at, 128), 128)]

    for j in (1, 2, 3):
        copy(bos, share(bo, z), f_send + j - 1, f_recv + j - 1, zpeer(j)).start()
    bo[:, 0:WIDE, pl.ds(pl.multiple_of(128 * z, 128), 128)] = bos[...]
    for j in (1, 2, 3):
        copy(bos, share(bo, lax.rem(z + 4 - j, 4)), f_send + j - 1, f_recv + j - 1, zpeer(j)).wait_recv()

    i_send, i_recv = names.take(12), names.take(12)

    def chip_rows(at):
        return pl.ds(pl.multiple_of(64 * at, 64), 64)

    def conv_copy(c, kx, ky):
        slot = kx + 2 * ky - 1
        dev, _ = peer(kx, ky, 0)
        return copy(p.at[c, :, chip_rows(dev["ha"]), :], cr.at[slot, c], i_send + 4 * slot + c, i_recv + 4 * slot + c, dev)

    def level_conv(c, carry):
        lv[c] = (dot(uh[c], bo[c]) + dot(ul[c], bo[c])).astype(bf16)
        out0, out1 = conv_part(lv[c], 1)
        p[c, 0] = p[c, 0] + out0
        p[c, 1] = p[c, 1] + out1
        for kx, ky in chips:
            conv_copy(c, kx, ky).start()
        return carry

    lax.fori_loop(0, 4, level_conv, 0)

    for j in (1, 2, 3):
        src = lax.rem(z + 4 - j, 4)
        copy(sd.at[src], sd.at[src], sz_send + j - 1, sz_recv + j - 1, zpeer(j)).wait_recv()
    for c in range(4):
        cn_s[0, 128 * c:128 * c + 128, :] = dot(sd[c], cwt[...], ROWS_T, FULL_ACCURACY)

    for c in range(4):
        for kx, ky in chips:
            conv_copy(c, kx, ky).wait_recv()
    convolved = (p[:, :, pl.ds(q64, 64), :] + cr[0] + cr[1] + cr[2]).reshape(512, 128)
    ok = val.at[...].reshape(4, 2, 256, 128)[:, :, pl.ds(q64, 64), :].reshape(512, 128)

    j_send, j_recv = names.take(6), names.take(6)

    def stat_copy(stage, kx, ky):
        slot = kx + 2 * ky - 1
        return copy(
            st.at[stage], str_.at[stage, slot], j_send + 3 * stage + slot, j_recv + 3 * stage + slot, peer(kx, ky, 0)[0]
        )

    def plane_sum(stage, first, second):
        st[stage, 0:1, :] = first
        st[stage, 1:2, :] = second
        for kx, ky in chips:
            stat_copy(stage, kx, ky).start()
        for kx, ky in chips:
            stat_copy(stage, kx, ky).wait_recv()
        total = st[stage] + str_[stage, 0] + str_[stage, 1] + str_[stage, 2]
        return total[0:1], total[1:2]

    masked = convolved * ok
    first, second = plane_sum(0, jnp.sum(masked, 0, keepdims=True), jnp.sum(convolved * masked, 0, keepdims=True))
    area = jnp.int32(0)
    for c in range(4):
        top, left, bottom, right = scalars(c)
        for k in range(3):
            area = area + (bottom[k] - top[k]) * (right[k] - left[k])
    valid_total = area.astype(f32)
    average = first / valid_total
    spread = second / valid_total - average * average
    inverse = lax.rsqrt(spread + EPSILON)
    normed = (convolved - average) * inverse
    gain = ngain[...]
    affine = gain * normed + nbias[...]
    logistic = jax.nn.sigmoid(affine)
    hidden = affine * logistic
    grad_affine = cn_s[0] * (logistic * (1.0 + affine * (1.0 - logistic)))
    part_bias = jnp.sum(grad_affine, 0, keepdims=True)
    part_gain = jnp.sum(grad_affine * normed, 0, keepdims=True)
    cn_s[1] = hidden
    small[48:49, :] = part_bias
    small[49:50, :] = part_gain
    bias_sum, gain_sum = plane_sum(1, part_bias, part_gain)
    grad_conv = ok * inverse * (
        grad_affine * gain - gain * bias_sum / valid_total - normed * gain * gain_sum / valid_total
    )
    gc[:, :, pl.ds(q64, 64), :] = grad_conv.astype(bf16).reshape(4, 2, 64, 128)
    k_send, k_recv = names.take(3), names.take(3)

    def gc_copy(kx, ky, at):
        slot = kx + 2 * ky - 1
        block = gc.at[:, :, chip_rows(at), :]
        return copy(block, block, k_send + slot, k_recv + slot, peer(kx, ky, 0)[0])

    for kx, ky in chips:
        gc_copy(kx, ky, q).start()

    lt_send, lt_recv = names.take(3), names.take(3)
    weight_part = jnp.zeros((24, 128), f32)
    bias_part = jnp.zeros((24, 1), f32)
    for c in range(4):
        hidden_c = cn_s[1, 128 * c:128 * c + 128, :]
        lt[c] = dot(cwt[...], hidden_c, BOTH_LAST, FULL_ACCURACY)
        weight_part = weight_part + dot(sd[c], hidden_c, precision=FULL_ACCURACY)
        bias_part = bias_part + jnp.sum(sd[c], 1, keepdims=True)
    small[0:24, :] = weight_part
    small[24:48, :] = jnp.broadcast_to(bias_part, (24, 128))
    for j in (1, 2, 3):
        copy(lt.at[lax.rem(z + j, 4)], ltr.at[j - 1], lt_send + j - 1, lt_recv + j - 1, zpeer(j)).start()

    for kx, ky in chips:
        gc_copy(kx, ky, peer(kx, ky, 0)[0]["ha"]).wait_recv()

    def shifted(c):
        col = lax.broadcasted_iota(jnp.int32, (256, 128), 0) % 8
        first, last = col == 0, col == 7
        g0, g1 = gc[c, 0].astype(f32), gc[c, 1].astype(f32)
        gp3[1, 0, 8:264, :] = g0
        gp3[1, 1, 8:264, :] = g1
        gp3[0, 0, 8:264, :] = jnp.where(last, pltpu.roll(g1, 7, 0), pltpu.roll(g0, 255, 0))
        gp3[0, 1, 8:264, :] = jnp.where(last, 0.0, pltpu.roll(g1, 255, 0))
        gp3[2, 0, 8:264, :] = jnp.where(first, 0.0, pltpu.roll(g0, 1, 0))
        gp3[2, 1, 8:264, :] = jnp.where(first, pltpu.roll(g0, 249, 0), pltpu.roll(g1, 1, 0))
        for a in range(3):
            for b in range(3):
                t = 3 * a + b
                for h in range(2):
                    start = 8 * (2 - a)
                    g9[c, 256 * h:256 * h + 256, 128 * t:128 * t + 128] = gp3[b, h, start:start + 256, :].astype(bf16)

    def data_grad(c):
        shifted(c)
        for h in range(2):
            dxf[c, 256 * h:256 * h + 256, :] = dot(g9[c, 256 * h:256 * h + 256, :], wall[0:512, :], BOTH_LAST)
        back = dot(g9[c], wall[512:1024, :], BOTH_LAST)
        high, low = halves(back)
        total = dot(uh[c], high, ROWS_T) + dot(uh[c], low, ROWS_T) + dot(ul[c], high, ROWS_T)
        gb[c] = total[0:WIDE].astype(bf16)

    ru_send, ru_recv, rd_send, rd_recv = names.take(3), names.take(3), names.take(3), names.take(3)

    def ru_copy(k):
        return copy(sbu.at[k], rxu.at[k], ru_send + k, ru_recv + k, {"col": z + 1})

    def rd_copy(k):
        return copy(sbd.at[k], rxd.at[k], rd_send + k, rd_recv + k, {"col": z - 1})

    def up_on(k):
        return (z + 3 - k <= 3) & (z < 3)

    def dn_on(k):
        return (z - 3 + k >= 0) & (z > 0)

    def scatter_step(k):
        @pl.when(up_on(k))
        def _():
            value = dxf[z + 3 - k]
            if k:
                sbu[k] = value.astype(bf16)

                @pl.when(z > 0)
                def _():
                    ru_copy(k - 1).wait_recv()
                    sbu[k] = (value + rxu[k - 1].astype(f32)).astype(bf16)
            else:
                sbu[k] = value.astype(bf16)
            ru_copy(k).start()

        @pl.when(dn_on(k))
        def _():
            value = dxf[z - 3 + k]
            if k:
                sbd[k] = value.astype(bf16)

                @pl.when(z < 3)
                def _():
                    rd_copy(k - 1).wait_recv()
                    sbd[k] = (value + rxd[k - 1].astype(f32)).astype(bf16)
            else:
                sbd[k] = value.astype(bf16)
            rd_copy(k).start()

    def canvas_at(i):
        low = (3 - i) if i < 2 else zz * (i - 2) + (1 - zz) * (3 - i)
        return (1 - zm) * low + zm * (3 - low)

    for i in range(4):
        data_grad(canvas_at(i))
        if i == 0:
            scatter_step(0)

    n_send, n_recv = names.take(3), names.take(3)
    for level in range(4):

        @pl.when(g == level)
        def _():
            for j in (1, 2, 3):
                at = lax.rem(z + j, 4)
                copy(
                    gb.at[:, pl.ds(0, SPANS[level]), pl.ds(pl.multiple_of(128 * at, 128), 128)],
                    grr.at[j - 1, :, pl.ds(0, SPANS[level]), :],
                    n_send + j - 1, n_recv + j - 1, zpeer(j),
                ).start()

    scatter_step(1)

    def weight_grad(part, store):
        for tile in range(2):
            cols = slice(256 * tile, 256 * tile + 256)

            def of(operand):
                total = None
                for c in range(4):
                    piece = dot(operand[c, :, cols], g9[c], ROWS_T)
                    total = piece if total is None else total + piece
                store(tile, total)

            pl.when(part == 0)(lambda: of(x))
            pl.when(part == 1)(lambda: of(lv))

    def store_out(tile, total):
        dw[0, 256 * tile:256 * tile + 256, :] = total

    def store_own(tile, total):
        dw[1, 256 * tile:256 * tile + 256, :] = total

    weight_grad(1 - w, store_out)
    w_send, w_recv = names.take(), names.take()
    dw_copy = copy(dw.at[0], dwr, w_send, w_recv, peer(0, 0, 1)[0])
    dw_copy.start()
    weight_grad(w, store_own)

    for level in range(4):

        @pl.when(g == level)
        def _():
            for j in (1, 2, 3):
                copy(
                    gb.at[:, pl.ds(0, SPANS[level]), pl.ds(0, 128)],
                    grr.at[j - 1, :, pl.ds(0, SPANS[level]), :],
                    n_send + j - 1, n_recv + j - 1, zpeer(j),
                ).wait_recv()

    own_grad = gb[:, :, pl.ds(pl.multiple_of(128 * z, 128), 128)].astype(f32)
    for j in range(3):
        own_grad = own_grad + grr[j].astype(f32)
    grad_act = rows_of(own_grad) * rows_of(af_s[...])
    b_norm = rows_of(nb_s[...])
    act_sum = jnp.sum(grad_act, 0, keepdims=True)
    act_norm_sum = jnp.sum(grad_act * b_norm, 0, keepdims=True)
    small[50:51, :] = act_norm_sum
    small[51:52, :] = act_sum
    grad_pre = b_inverse * (
        b_gain * grad_act - b_gain * act_sum / samples - b_norm * b_gain * act_norm_sum / samples
    )
    gpre[...] = grad_pre.reshape(4, WIDE, 128)
    o_send, o_recv = names.take(3), names.take(12)
    for level in range(4):

        @pl.when(g == level)
        def _():
            rows = pl.ds(STARTS[level], SPANS[level])
            for kx, ky in chips:
                slot = kx + 2 * ky - 1
                copy(
                    gpre.at[:, pl.ds(0, SPANS[level]), :], gpa.at[:, rows, :],
                    o_send + slot, o_recv + 3 * level + slot, peer(kx, ky, 0)[0],
                ).start()
            gpa[:, STARTS[level]:STARTS[level] + SPANS[level], :] = gpre[:, 0:SPANS[level], :]

    s_send, s_recv = names.take(7), names.take(7)

    def small_copy(n):
        return copy(small, smr.at[n], s_send + n, s_recv + n, peer(*plane[n])[0])

    for n in range(7):
        small_copy(n).start()

    dw_copy.wait_recv()
    dw[1] = dw[1] + dwr[...]
    y_send, y_recv = names.take(9), names.take(9)
    y_dev = peer(0, 1, 1)[0]

    def tap_copy(t):
        return copy(dw.at[1, :, pl.ds(128 * t, 128)], cgrad_out.at[t], y_send + t, y_recv + t, y_dev)

    def tap_own(t):
        return pltpu.make_async_copy(dw.at[1, :, pl.ds(128 * t, 128)], cgrad_out.at[t], sems.at[y_send + t])

    @pl.when(w == yq)
    def _():
        for t in range(TAPS):
            tap_own(t).start()

    @pl.when(w != yq)
    def _():
        for t in range(TAPS):
            tap_copy(t).start()

    for level in range(4):
        lx, ly = level // 2, level % 2
        for kx, ky in chips:

            @pl.when((xq + kx - 2 * kx * xq == lx) & (yq + ky - 2 * ky * yq == ly))
            def _():
                slot = kx + 2 * ky - 1
                copy(
                    gpre.at[:, pl.ds(0, SPANS[level]), :],
                    gpa.at[:, pl.ds(STARTS[level], SPANS[level]), :],
                    o_send + slot, o_recv + 3 * level + slot, peer(kx, ky, 0)[0],
                ).wait_recv()

    def pooled_grad(c, carry):
        for level in range(4):
            rows = slice(STARTS[level], STARTS[level] + SPANS[level])
            high, low = halves(gpa[c, rows, :])
            gps[c, rows, :] = (dot(high, wb[level], BOTH_LAST) + dot(low, wb[level], BOTH_LAST)).astype(bf16)
        return carry

    lax.fori_loop(0, 4, pooled_grad, 0)
    p_send, p_recv = names.take(3), names.take(3)
    for j in (1, 2, 3):
        copy(gps.at[lax.rem(z + j, 4)], gpr.at[j - 1], p_send + j - 1, p_recv + j - 1, zpeer(j)).start()

    scatter_step(2)

    for level in range(4):
        rows = slice(STARTS[level], STARTS[level] + SPANS[level])
        total = None
        for c in range(4):
            high, low = halves(gpa[c, rows, :])
            piece = dot(po[c, rows, :], high, ROWS_T) + dot(po[c, rows, :], low, ROWS_T)
            total = piece if total is None else total + piece
        bg[level] = total
    bc_send, bc_recv = names.take(), names.take()
    w256 = pl.multiple_of(256 * w, 256)
    v256 = pl.multiple_of(256 * (1 - w), 256)
    bg_copy = copy(bg.at[:, pl.ds(v256, 256), :], bgr, bc_send, bc_recv, peer(0, 0, 1)[0])
    bg_copy.start()
    bg_copy.wait_recv()
    bgh[...] = (bg[:, pl.ds(w256, 256), :] + bgr[...]).astype(bf16)
    own_channels = pl.ds(pl.multiple_of(512 * g + 256 * w, 256), 256)
    bx_send, bx_recv = names.take(3), names.take(3)
    by_send, by_recv = names.take(4), names.take(4)

    def bga_of(block, core):
        return bga.at[:, pl.ds(pl.multiple_of(512 * block + 256 * core, 256), 256), :]

    def bg_chip(kx, ky):
        slot = kx + 2 * ky - 1
        return copy(bgh, bga_of(g, w), bx_send + slot, bx_recv + slot, peer(kx, ky, 0)[0])

    def bg_core(n, block):
        return copy(bga_of(block, w), bga_of(block, w), by_send + n, by_recv + n, peer(0, 0, 1)[0])

    for kx, ky in chips:
        bg_chip(kx, ky).start()
    bga[:, own_channels, :] = bgh[...]
    bg_core(3, g).start()

    for j in (1, 2, 3):
        copy(lt.at[0], ltr.at[j - 1], lt_send + j - 1, lt_recv + j - 1, zpeer(j)).wait_recv()
    lts[w] = lt[z] + ltr[0] + ltr[1] + ltr[2]
    ls_send, ls_recv = names.take(), names.take()
    logits_copy = copy(lts.at[w], lts.at[w], ls_send, ls_recv, peer(0, 0, 1)[0])
    logits_copy.start()

    for j in (1, 2, 3):
        copy(gps.at[0], gpr.at[j - 1], p_send + j - 1, p_recv + j - 1, zpeer(j)).wait_recv()
    pooled_back = gps[z].astype(f32)
    for j in range(3):
        pooled_back = pooled_back + gpr[j].astype(f32)
    count = cnt[z]
    pieces = [pooled_back[:, 128 * chunk:128 * chunk + 128] / count for chunk in range(4)]
    high, low = halves(jnp.concatenate(pieces, 1))
    fg[...] = dot(mt[z], high, ROWS_T) + dot(mt[z], low, ROWS_T)
    ok = val[z]

    @pl.when(z > 0)
    def _():
        ru_copy(2).wait_recv()
        dxf[z] = dxf[z] + rxu[2].astype(f32)

    @pl.when(z < 3)
    def _():
        rd_copy(2).wait_recv()
        dxf[z] = dxf[z] + rxd[2].astype(f32)

    for chunk in range(4):
        cols = slice(128 * chunk, 128 * chunk + 128)
        fg[:, cols] = fg[:, cols] + dxf[z, :, cols] * ok
    q_send, q_recv = names.take(8), names.take(8)

    def fg_copy(n):
        dev, _ = peer(*plane[n])
        rows = pl.ds(pl.multiple_of(256 * dev["wa"] + 64 * dev["ha"], 64), 64)
        return copy(fg.at[rows, :], fgrad_out.at[w, :, pl.ds(g512, 512)], q_send + n, q_recv + n, dev)

    for n in range(7):
        fg_copy(n).start()
    fg_own = pltpu.make_async_copy(
        fg.at[pl.ds(own_row, 64), :], fgrad_out.at[w, :, pl.ds(g512, 512)], sems.at[q_send + 7]
    )
    fg_own.start()

    for n, (kx, ky) in enumerate(chips):
        dev, block = peer(kx, ky, 0)
        copy(bgh, bga_of(block, w), bx_send + n, bx_recv + n, dev).wait_recv()
        bg_core(n, block).start()

    for n in range(7):
        small_copy(n).wait_recv()
    total = small[...]
    for n in range(7):
        total = total + smr[n]
    small_out[0:48, :] = total[0:48]
    small_out[48:56, :] = total[48:56]
    for kx, ky in [(0, 0)] + chips:
        dev, block = peer(kx, ky, 0)
        mine = small[...] if kx + ky == 0 else smr[plane.index((kx, ky, 0))]
        both = mine + smr[plane.index((kx, ky, 1))]
        small_out[pl.ds(56 + block, 1), :] = both[50:51]
        small_out[pl.ds(60 + block, 1), :] = both[51:52]

    logits_other = copy(lts.at[1 - w], lts.at[1 - w], ls_send, ls_recv, peer(0, 0, 1)[0])
    logits_other.wait_recv()
    logits_out[...] = lts[...]

    for n, (kx, ky) in enumerate([*chips, (0, 0)]):
        block = peer(kx, ky, 0)[1]
        copy(bga_of(block, 1 - w), bga_of(block, 1 - w), by_send + n, by_recv + n, peer(0, 0, 1)[0]).wait_recv()
    out_sem = names.take()
    bg_out = pltpu.make_async_copy(bga, bgrad_out, sems.at[out_sem])
    bg_out.start()

    for n in range(7):
        dev, block = peer(*plane[n])
        copy(
            fg.at[pl.ds(0, 64), :],
            fgrad_out.at[dev["wa"], :, pl.ds(pl.multiple_of(512 * block, 512), 512)],
            q_send + n, q_recv + n, dev,
        ).wait_recv()
    fg_own.wait()

    @pl.when(w == yq)
    def _():
        for t in range(TAPS):
            tap_own(t).wait()

    @pl.when(w != yq)
    def _():
        for t in range(TAPS):
            tap_copy(t).wait()

    for c in a_copies:
        c.wait_send()
    seed_copy.wait_send()
    for k in range(3):
        pl.when((z >= k) & (z < 3))(lambda: up_copy(k).wait_send())
        pl.when((z + k <= 3) & (z > 0))(lambda: dn_copy(k).wait_send())
        pl.when(up_on(k))(lambda: ru_copy(k).wait_send())
        pl.when(dn_on(k))(lambda: rd_copy(k).wait_send())
    for j in (1, 2, 3):
        copy(sd.at[z], sd.at[z], sz_send + j - 1, sz_recv + j - 1, zpeer(j)).wait_send()
        copy(bos, share(bo, z), f_send + j - 1, f_recv + j - 1, zpeer(j)).wait_send()
        copy(lt.at[0], ltr.at[j - 1], lt_send + j - 1, lt_recv + j - 1, zpeer(j)).wait_send()
        copy(gps.at[0], gpr.at[j - 1], p_send + j - 1, p_recv + j - 1, zpeer(j)).wait_send()
    for level in range(4):
        for c in range(4):
            to_level_owner(level, lambda kx, ky: pre_copy(level, c, kx, ky).wait_send())

        @pl.when(g == level)
        def _():
            for j in (1, 2, 3):
                copy(
                    gb.at[:, pl.ds(0, SPANS[level]), pl.ds(0, 128)],
                    grr.at[j - 1, :, pl.ds(0, SPANS[level]), :],
                    n_send + j - 1, n_recv + j - 1, zpeer(j),
                ).wait_send()
            for kx, ky in chips:
                slot = kx + 2 * ky - 1
                copy(
                    gpre.at[:, pl.ds(0, SPANS[level]), :], gpa.at[:, pl.ds(STARTS[level], SPANS[level]), :],
                    o_send + slot, o_recv + 3 * level + slot, peer(kx, ky, 0)[0],
                ).wait_send()
    for kx, ky in chips:
        for c in range(4):
            conv_copy(c, kx, ky).wait_send()
        for stage in range(2):
            stat_copy(stage, kx, ky).wait_send()
        gc_copy(kx, ky, q).wait_send()
        bg_chip(kx, ky).wait_send()
    dw_copy.wait_send()
    bg_copy.wait_send()
    logits_copy.wait_send()
    for n in range(7):
        small_copy(n).wait_send()
        fg_copy(n).wait_send()
    for n in range(4):
        bg_core(n, g).wait_send()
    bg_out.wait()
    assert names.count <= SEMAPHORES


SEMAPHORES = 256


def canvas_body(
    mesh, features, region_boxes, branch_weight, branch_gain, branch_bias, conv_weight, norm_gain, norm_bias,
    class_weight, class_bias, cotangent,
):
    f32, bf16 = jnp.float32, jnp.bfloat16
    micros, tile_rows, tile_cols, channels = features.shape
    pixels = tile_rows * tile_cols
    classes = class_bias.shape[0]
    z, w = lax.axis_index("col"), lax.axis_index("wa")
    own_boxes = lax.dynamic_slice_in_dim(region_boxes, micros * z, micros, 0)
    at = jnp.arange(pixels, dtype=jnp.int32)
    y = (lax.axis_index("ha") * tile_rows + at // tile_cols)[None, None]
    xx = (w * tile_cols + at % tile_cols)[None, None]
    top, left, bottom, right = [own_boxes[:, :, e, None] for e in range(4)]
    valid = jnp.any((y >= top) & (y < bottom) & (xx >= left) & (xx < right), 1).astype(f32)
    seeds = jnp.transpose((cotangent.reshape(micros, pixels, classes) * valid[:, :, None]), (0, 2, 1))
    seeds = jnp.pad(seeds, ((0, 0), (0, 24 - classes), (0, 0)))
    blank = jnp.zeros_like(seeds)
    seeds = jnp.where(w == 0, jnp.concatenate([seeds, blank], 2), jnp.concatenate([blank, seeds], 2))
    cwt = jnp.pad(class_weight.T, ((0, 24 - classes), (0, 0)))
    lane_table, row_table = bin_tables()

    vmem = pl.BlockSpec(memory_space=pltpu.VMEM)
    hbm = pl.BlockSpec(memory_space=pl.ANY)
    smem = pl.BlockSpec(memory_space=pltpu.SMEM)
    V = pltpu.VMEM
    scratch = [
        V((4, 512, 512), bf16),
        V((4, 512, 512), bf16),
        V((1024, 1152), bf16),
        V((4, 512, 128), bf16),
        V((4, 512, 128), bf16),
        V((4, 512, 128), bf16),
        V((4, BINS, 512), bf16),
        V((4, BINS, 128), f32),
        V((4, BINS, 512), bf16),
        V((4, BINS, 128), f32),
        V((3, 4, WIDE, 128), f32),
        V((4, WIDE, 128), bf16),
        V((4, 128, 512), bf16),
        V((4, 512, 128), f32),
        V((2, 272, 1152), f32),
        V((4, 2, 256, 128), f32),
        V((3, 4, 2, 64, 128), f32),
        V((4, 2, 256, 128), bf16),
        V((4, 512, 1152), bf16),
        V((3, 2, 272, 128), f32),
        V((4, 512, 512), f32),
        V((3, 512, 512), bf16),
        V((3, 512, 512), bf16),
        V((3, 512, 512), bf16),
        V((3, 512, 512), bf16),
        V((4, WIDE, 512), bf16),
        V((3, 4, WIDE, 128), bf16),
        V((4, WIDE, 128), f32),
        V((4, BINS, 128), f32),
        V((4, BINS, 512), bf16),
        V((3, BINS, 512), bf16),
        V((2, 512, 1152), f32),
        V((512, 1152), f32),
        V((4, 512, 128), f32),
        V((4, 256, 128), f32),
        V((4, 256, 128), bf16),
        V((1, 24, 128), f32),
        V((4, 24, 128), f32),
        V((4, 24, 128), f32),
        V((3, 24, 128), f32),
        V((2, 24, 128), f32),
        V((2, 8, 128), f32),
        V((2, 3, 8, 128), f32),
        V((56, 128), f32),
        V((7, 56, 128), f32),
        V((4, WIDE, 128), f32),
        V((4, WIDE, 128), f32),
        V((2, 512, 128), f32),
        V((4, channels, 128), bf16),
        V((512, 512), f32),
        pltpu.SemaphoreType.DMA((SEMAPHORES,)),
    ]
    share = conv_weight.shape[2]
    logits_t, feature_grad, branch_grad, small, conv_grad = pl.pallas_call(
        head_kernel,
        out_shape=(
            jax.ShapeDtypeStruct((2, 24, 128), f32),
            jax.ShapeDtypeStruct((micros, pixels, channels), f32),
            jax.ShapeDtypeStruct((4, channels, share), bf16),
            jax.ShapeDtypeStruct((64, 128), f32),
            jax.ShapeDtypeStruct((TAPS, 512, share), f32),
        ),
        in_specs=[smem, vmem, vmem, hbm, vmem, hbm, hbm, vmem, vmem, vmem, vmem, vmem],
        out_specs=(vmem, hbm, hbm, vmem, hbm),
        scratch_shapes=scratch,
        compiler_params=pltpu.CompilerParams(
            collective_id=0, has_side_effects=True, vmem_limit_bytes=60 * 2**20
        ),
    )(
        region_boxes.reshape(-1), lane_table, row_table, features.reshape(micros, pixels, channels), seeds,
        conv_weight, branch_weight, branch_gain, branch_bias, norm_gain.reshape(1, -1), norm_bias.reshape(1, -1), cwt,
    )
    tile = lax.dynamic_slice_in_dim(logits_t, w * pixels, pixels, 2)[:, :classes]
    logits = (jnp.transpose(tile, (0, 2, 1)) + class_bias) * valid[:, :, None]
    return (
        logits.reshape(micros, tile_rows, tile_cols, classes),
        feature_grad.reshape(features.shape),
        branch_grad.astype(f32),
        small[56:60],
        small[60:64],
        conv_grad,
        small[49],
        small[48],
        small[:classes].T,
        small[24:24 + classes, 0],
    )


def extended(block, sides, width):
    for axis, dim in sides:
        count = lax.axis_size(axis)
        forward = [(i, i + 1) for i in range(count - 1)]
        backward = [(target, source) for source, target in forward]
        low = lax.ppermute(
            lax.slice_in_dim(block, block.shape[dim] - width, None, axis=dim), axis, forward
        )
        high = lax.ppermute(lax.slice_in_dim(block, 0, width, axis=dim), axis, backward)
        block = jnp.concatenate([low, block, high], axis=dim)
    return block


def interpolate(offset, extent, n, bin_ids):
    scaled = offset * (n - 1)
    lower_bin = scaled // (extent - 1)
    fraction = (scaled - lower_bin * (extent - 1)).astype(jnp.float32) / (extent - 1).astype(
        jnp.float32
    )
    upper_bin = jnp.minimum(lower_bin + 1, n - 1)
    lower_hit = (bin_ids[None, :] == lower_bin[:, None]).astype(jnp.float32)
    upper_hit = (bin_ids[None, :] == upper_bin[:, None]).astype(jnp.float32)
    return (1.0 - fraction)[:, None] * lower_hit + fraction[:, None] * upper_hit


def layout(region, row_ids, col_ids):
    member_cols = []
    count_cols = []
    weight_per_level = []
    validity = jnp.zeros(row_ids.shape, jnp.float32)
    for n in LEVELS:
        bin_ids = jnp.arange(n, dtype=jnp.int32)
        level_weights = []
        for k in range(region.shape[0]):
            row_start = region[k, 0]
            col_start = region[k, 1]
            height = region[k, 2] - row_start
            width = region[k, 3] - col_start
            row_offset = row_ids - row_start
            col_offset = col_ids - col_start
            inside = (
                (row_offset >= 0) & (row_offset < height) & (col_offset >= 0) & (col_offset < width)
            )
            row_low = bin_ids * height // n
            row_high = ((bin_ids + 1) * height + n - 1) // n
            col_low = bin_ids * width // n
            col_high = ((bin_ids + 1) * width + n - 1) // n
            row_in = (row_offset[:, None] >= row_low[None, :]) & (
                row_offset[:, None] < row_high[None, :]
            )
            col_in = (col_offset[:, None] >= col_low[None, :]) & (
                col_offset[:, None] < col_high[None, :]
            )
            member = row_in[:, :, None] & col_in[:, None, :] & inside[:, None, None]
            member_cols.append(member.reshape(-1, n * n).astype(jnp.float32))
            count_cols.append(
                ((row_high - row_low)[:, None] * (col_high - col_low)[None, :]).reshape(n * n)
            )
            row_weight = interpolate(row_offset, height, n, bin_ids)
            col_weight = interpolate(col_offset, width, n, bin_ids)
            bilinear = (
                row_weight[:, :, None]
                * col_weight[:, None, :]
                * inside.astype(jnp.float32)[:, None, None]
            )
            level_weights.append(bilinear.reshape(-1, n * n))
            if n == 1:
                validity = validity + inside.astype(jnp.float32)
        weight_per_level.append(jnp.concatenate(level_weights, 1))
    counts = jnp.concatenate(count_cols).astype(jnp.float32)
    return (jnp.concatenate(member_cols, 1), weight_per_level, counts, validity)


def silu_slope(inputs):
    logistic = jax.nn.sigmoid(inputs)
    return logistic * (1.0 + inputs * (1.0 - logistic))


def tiled_body(
    features,
    region_boxes,
    branch_weight,
    branch_gain,
    branch_bias,
    conv_weight,
    norm_gain,
    norm_bias,
    class_weight,
    class_bias,
    cotangent,
):
    micros, tile_rows, tile_cols, channels = features.shape
    groups = lax.axis_size("col")
    regions = region_boxes.shape[1]
    share = conv_weight.shape[2]
    width_out = share * groups
    pixels = tile_rows * tile_cols
    flat_rows = groups * pixels
    col_index = lax.axis_index("col")
    tile_row_ids = lax.axis_index("ha") * tile_rows + jnp.arange(tile_rows, dtype=jnp.int32)
    tile_col_ids = lax.axis_index("wa") * tile_cols + jnp.arange(tile_cols, dtype=jnp.int32)
    row_ids = jnp.repeat(tile_row_ids, tile_cols)
    col_ids = jnp.tile(tile_col_ids, tile_rows)
    conv_flat = conv_weight.reshape(-1, share)
    conv_back = jnp.transpose(conv_weight, (0, 2, 1)).reshape(-1, conv_weight.shape[1])
    spans = [regions * n * n for n in LEVELS]
    starts = [sum(spans[:level_number]) for level_number in range(len(LEVELS))]
    grouped_boxes = region_boxes.reshape(groups, micros, regions, 4)
    branch_float = branch_weight.astype(jnp.float32)
    branch_grads = [jnp.zeros((channels, share), jnp.float32) for level_number in range(4)]
    branch_gain_grads = [jnp.zeros((share,), jnp.float32) for level_number in range(4)]
    branch_bias_grads = [jnp.zeros((share,), jnp.float32) for level_number in range(4)]
    norm_gain_total = jnp.zeros((share,), jnp.float32)
    norm_bias_total = jnp.zeros((share,), jnp.float32)
    class_weight_total = jnp.zeros(class_weight.shape, jnp.float32)
    class_bias_total = jnp.zeros(class_bias.shape, jnp.float32)
    conv_total = jnp.zeros(conv_flat.shape, jnp.float32)
    logit_list = []
    feature_list = []
    for m in range(micros):
        boxes_now = grouped_boxes[:, m]
        member_pixels, weight_per_level, counts, validity = jax.vmap(
            lambda region: layout(region, row_ids, col_ids)
        )(boxes_now)
        own_members = lax.dynamic_index_in_dim(member_pixels, col_index, 0, False)
        own_counts = lax.dynamic_index_in_dim(counts, col_index, 0, False)
        own_valid = lax.dynamic_index_in_dim(validity, col_index, 0, False)
        areas = (boxes_now[:, :, 2] - boxes_now[:, :, 0]) * (
            boxes_now[:, :, 3] - boxes_now[:, :, 1]
        )
        valid_total = jnp.sum(areas.astype(jnp.float32))
        local_x = features[m].reshape(pixels, channels)
        partial_value = jnp.einsum(
            "pb,pd->bd",
            own_members.astype(jnp.bfloat16),
            local_x,
            preferred_element_type=jnp.float32,
        )
        bin_total = lax.psum(partial_value, ("ha", "wa"))
        pooled = (bin_total / own_counts[:, None]).astype(jnp.bfloat16)
        pooled_all = lax.all_gather(pooled[None], "col", axis=0, tiled=True)
        branch_norms = []
        branch_affines = []
        branch_inverse = []
        branch_outs = []
        for level_number in range(4):
            level_pooled = pooled_all[
                :, starts[level_number] : starts[level_number] + spans[level_number]
            ]
            pre = jnp.einsum(
                "cbd,de->cbe",
                level_pooled,
                branch_weight[level_number],
                preferred_element_type=jnp.float32,
            )
            average = jnp.mean(pre, (0, 1))
            spread = jnp.mean(pre * pre, (0, 1)) - average * average
            inverse = lax.rsqrt(spread + EPSILON)
            normed_branch = (pre - average) * inverse
            affine_branch = branch_gain[level_number] * normed_branch + branch_bias[level_number]
            branch_norms.append(normed_branch)
            branch_affines.append(affine_branch)
            branch_inverse.append(inverse)
            branch_outs.append(jax.nn.silu(affine_branch))
        branch_local = jnp.concatenate(branch_outs, 1).astype(jnp.bfloat16)
        branch_full = lax.all_gather(branch_local, "col", axis=2, tiled=True)
        enlarged_map = []
        for level_number in range(4):
            level_output = branch_full[
                :, starts[level_number] : starts[level_number] + spans[level_number]
            ].astype(jnp.float32)
            spread_out = jnp.einsum(
                "zdw,zwk->zdk",
                weight_per_level[level_number],
                level_output,
                precision=FULL_ACCURACY,
            )
            enlarged_map.append(
                spread_out.reshape(groups, tile_rows, tile_cols, width_out).astype(jnp.bfloat16)
            )
        x_all = lax.all_gather(features[m][None], "col", axis=0, tiled=True)
        masked_x = x_all * validity.reshape(groups, tile_rows, tile_cols, 1).astype(jnp.bfloat16)
        stacked = jnp.concatenate([masked_x] + enlarged_map, -1)
        padded = extended(stacked, (("ha", 1), ("wa", 2)), 1)
        columns = jnp.concatenate(
            [
                padded[:, row_tap : row_tap + tile_rows, col_tap : col_tap + tile_cols]
                for row_tap in range(3)
                for col_tap in range(3)
            ],
            -1,
        ).reshape(flat_rows, -1)
        convolved = jnp.dot(columns, conv_flat, preferred_element_type=jnp.float32)
        valid_flat = validity.reshape(flat_rows, 1)
        first_sum, second_sum = lax.psum(
            (jnp.sum(convolved * valid_flat, 0), jnp.sum(convolved * convolved * valid_flat, 0)),
            ("ha", "wa"),
        )
        average = first_sum / valid_total
        spread = second_sum / valid_total - average * average
        inverse = lax.rsqrt(spread + EPSILON)
        normed = (convolved - average) * inverse
        affine = norm_gain * normed + norm_bias
        hidden = jax.nn.silu(affine)
        part_logits = jnp.dot(hidden, class_weight, precision=FULL_ACCURACY).reshape(
            groups, tile_rows, tile_cols, -1
        )
        summed = lax.psum_scatter(part_logits, "col", scatter_dimension=0, tiled=True)
        own_valid_tile = own_valid.reshape(tile_rows, tile_cols, 1)
        logit_list.append((summed[0] + class_bias) * own_valid_tile)
        seed = (cotangent[m] * own_valid_tile)[None]
        seed_all = lax.all_gather(seed, "col", axis=0, tiled=True).reshape(flat_rows, -1)
        grad_hidden = jnp.dot(seed_all, class_weight.T, precision=FULL_ACCURACY)
        grad_affine = grad_hidden * silu_slope(affine)
        bias_sum, gain_sum, class_part, bias_part = lax.psum(
            (
                jnp.sum(grad_affine, 0),
                jnp.sum(grad_affine * normed, 0),
                jnp.dot(hidden.T, seed_all, precision=FULL_ACCURACY),
                jnp.sum(seed_all, 0),
            ),
            ("ha", "wa"),
        )
        norm_bias_total = norm_bias_total + bias_sum
        norm_gain_total = norm_gain_total + gain_sum
        class_weight_total = class_weight_total + class_part
        class_bias_total = class_bias_total + bias_part
        grad_conv = (
            valid_flat
            * inverse
            * (
                grad_affine * norm_gain
                - norm_gain * bias_sum / valid_total
                - normed * norm_gain * gain_sum / valid_total
            )
        )
        grad_low = grad_conv.astype(jnp.bfloat16)
        grad_pad = extended(
            grad_low.reshape(groups, tile_rows, tile_cols, share), (("ha", 1), ("wa", 2)), 1
        )
        grad_columns = jnp.concatenate(
            [
                grad_pad[
                    :, 2 - row_tap : 2 - row_tap + tile_rows, 2 - col_tap : 2 - col_tap + tile_cols
                ]
                for row_tap in range(3)
                for col_tap in range(3)
            ],
            -1,
        ).reshape(flat_rows, -1)
        grad_stacked = jnp.dot(grad_columns, conv_back, preferred_element_type=jnp.float32)
        conv_part = jnp.einsum("pk,pe->ke", columns, grad_low, preferred_element_type=jnp.float32)
        conv_total = conv_total + conv_part
        grad_x = grad_stacked[:, :channels]
        bin_parts = []
        for level_number in range(4):
            level_gradient = grad_stacked[
                :, channels + level_number * width_out : channels + (level_number + 1) * width_out
            ].reshape(groups, pixels, width_out)
            bin_parts.append(
                jnp.einsum(
                    "qkl,qko->qlo",
                    weight_per_level[level_number],
                    level_gradient,
                    precision=FULL_ACCURACY,
                )
            )
        bin_local = jnp.concatenate(bin_parts, 1)
        bin_grad = lax.psum(bin_local, ("ha", "wa", "col"))
        own_bin_grad = lax.dynamic_slice_in_dim(bin_grad, col_index * share, share, 2)
        grad_pres = []
        for level_number in range(4):
            grad_out = own_bin_grad[
                :, starts[level_number] : starts[level_number] + spans[level_number]
            ]
            grad_act = grad_out * silu_slope(branch_affines[level_number])
            act_sum = jnp.sum(grad_act, (0, 1))
            act_norm_sum = jnp.sum(grad_act * branch_norms[level_number], (0, 1))
            samples = float(groups * spans[level_number])
            branch_bias_grads[level_number] = branch_bias_grads[level_number] + act_sum
            branch_gain_grads[level_number] = branch_gain_grads[level_number] + act_norm_sum
            grad_pre = branch_inverse[level_number] * (
                branch_gain[level_number] * grad_act
                - branch_gain[level_number] * act_sum / samples
                - branch_norms[level_number] * branch_gain[level_number] * act_norm_sum / samples
            )
            level_pooled = pooled_all[
                :, starts[level_number] : starts[level_number] + spans[level_number]
            ].astype(jnp.float32)
            branch_grads[level_number] = branch_grads[level_number] + jnp.einsum(
                "cbd,cbe->de", level_pooled, grad_pre, precision=FULL_ACCURACY
            )
            grad_pres.append(grad_pre)
        pooled_grads = [
            jnp.einsum(
                "cbe,de->cbd",
                grad_pres[level_number],
                branch_float[level_number],
                precision=FULL_ACCURACY,
            )
            for level_number in range(4)
        ]
        grad_pooled = jnp.concatenate(pooled_grads, 1)
        back_x, back_pooled = (
            lax.psum_scatter(
                grad_x.reshape(groups, pixels, channels).astype(jnp.bfloat16),
                "col",
                scatter_dimension=0,
                tiled=True,
            ).astype(jnp.float32),
            lax.psum_scatter(
                grad_pooled.astype(jnp.bfloat16), "col", scatter_dimension=0, tiled=True
            ).astype(jnp.float32),
        )
        pooled_back = back_pooled[0]
        spread_back = jnp.dot(
            own_members, pooled_back / own_counts[:, None], precision=FULL_ACCURACY
        )
        feature_list.append(
            (back_x[0] * own_valid[:, None] + spread_back).reshape(tile_rows, tile_cols, channels)
        )
    conv_result = lax.psum_scatter(
        conv_total.reshape(9, -1, share), ("ha", "wa"), scatter_dimension=1, tiled=True
    )
    return (
        jnp.stack(logit_list),
        jnp.stack(feature_list),
        jnp.stack(branch_grads),
        jnp.stack(branch_gain_grads),
        jnp.stack(branch_bias_grads),
        conv_result,
        norm_gain_total,
        norm_bias_total,
        class_weight_total,
        class_bias_total,
    )


def solution(mesh):
    placed = (
        P("col", "ha", "wa", None),
        P(),
        P(None, None, "col"),
        P(None, "col"),
        P(None, "col"),
        P(None, None, "col"),
        P("col"),
        P("col"),
        P("col", None),
        P(),
        P("col", "ha", "wa", None),
    )
    return jax.shard_map(
        functools.partial(canvas_body, mesh) if whole_canvas_plan(mesh) else tiled_body,
        mesh=mesh,
        in_specs=placed,
        out_specs=(
            P("col", "ha", "wa", None),
            P("col", "ha", "wa", None),
            P(None, None, "col"),
            P(None, "col"),
            P(None, "col"),
            P(None, ("ha", "wa"), "col"),
            P("col"),
            P("col"),
            P("col", None),
            P(),
        ),
        check_vma=False,
    )
```

```python
import functools

import jax
import jax.numpy as jnp
import numpy as np
from jax import lax
from jax.experimental import pallas as pl
from jax.experimental.pallas import tpu as pltpu
from jax.sharding import PartitionSpec as P

EPSILON = 1e-05
LEVELS = (1, 2, 3, 6)
FULL_ACCURACY = lax.Precision.HIGHEST
MESH = pl.DeviceIdType.MESH


SPANS = (16, 16, 32, 112)
STARTS = (0, 16, 32, 64)
BINS = 176
WIDE = 112
TAPS = 9


def whole_canvas_plan(mesh):
    return mesh.shape["ha"] == 4 and mesh.shape["wa"] == 2 and mesh.shape["col"] == 4


def bin_tables():
    lanes = np.zeros((4, 8, 128), np.float32)
    rows = np.zeros((BINS, 8), np.float32)
    rows[:, 3] = 1.0
    for level, n in enumerate(LEVELS):
        lanes[level, 3, :] = n - 1
        for k in range(3):
            for i in range(n):
                for j in range(n):
                    b = (k * n + i) * n + j
                    lanes[level, :3, b] = (k, i, j)
                    lanes[level, 4, b] = 1.0
                    row = STARTS[level] + b
                    for at, value in enumerate((k, i, j, n, 1.0)):
                        rows[row, at] = value
    return lanes, rows


def dot(a, b, dims=((1,), (0,)), precision=None):
    return lax.dot_general(a, b, (dims, ((), ())), precision=precision, preferred_element_type=jnp.float32)


ROWS_T = ((0,), (0,))
BOTH_LAST = ((1,), (1,))


def halves(value):
    high = value.astype(jnp.bfloat16)
    return high, (value - high.astype(jnp.float32)).astype(jnp.bfloat16)


def pick3(index, values):
    return jnp.where(index == 0.0, values[0], jnp.where(index == 1.0, values[1], values[2]))


class Sems:
    def __init__(self):
        self.count = 0

    def take(self, n=1):
        at = self.count
        self.count += n
        return at


def head_kernel(
    boxes, lane_table, row_table, feat, cot, wconv, wbranch, bgain, bbias, ngain, nbias, cw_in, cb,
    logits_out, fgrad_out, bgrad_out, small_out, cgrad_out,
    x, lv, wall, wb2, u2, ut, mt, cnt, po, pre, prr, bos, bor, bo2, val, yp, p, cr, gc, g9, gp3, tb,
    dxf, sbu, sbd, rxu, rxd, gb, grr, gpre, gpa, gpx, gps, gpr, dw, dwr, bg, bgr, bgh, seed_in, sd, lt, ltr, lts,
    st, str_, small, smr, nb_s, af_s, cn_s, bga, fg, fgh, cwt, seeds, square, dwh, dwx, bi_s, sems, turn,
):
    f32, bf16 = jnp.float32, jnp.bfloat16
    q, w, z = lax.axis_index("ha"), lax.axis_index("wa"), lax.axis_index("col")
    xq, yq = lax.rem(q, 2), lax.div(q, 2)
    g = 2 * xq + yq
    classes = cb.shape[1]
    zm = lax.div(z, 2)
    zz = z * (1 - zm) + (3 - z) * zm
    names = Sems()
    finals = []
    due = {}

    def arrive(name):
        due.pop(name)()

    def each(copies, method):
        def run():
            for c in copies:
                getattr(c, method)()

        return run


    def peer(kx, ky, kw):
        px = xq + kx - 2 * kx * xq
        py = yq + ky - 2 * ky * yq
        return {"ha": 2 * py + px, "wa": w + kw - 2 * kw * w}, 2 * px + py

    def copy(src, dst, ss, rs, dev):
        return pltpu.make_async_remote_copy(
            src_ref=src, dst_ref=dst, send_sem=sems.at[ss], recv_sem=sems.at[rs], device_id=dev, device_id_type=MESH
        )

    def zpeer(j):
        return {"col": lax.rem(z + j, 4)}

    plane = [(kx, ky, kw) for kw in (0, 1) for ky in (0, 1) for kx in (0, 1) if kx + ky + kw]
    chips = [(1, 0), (0, 1), (1, 1)]

    barrier = pltpu.get_barrier_semaphore()
    for kx, ky, kw in plane:
        pl.semaphore_signal(barrier, 1, device_id=peer(kx, ky, kw)[0], device_id_type=MESH)
    for j in (1, 2, 3):
        pl.semaphore_signal(barrier, 1, device_id=zpeer(j), device_id_type=MESH)

    g512 = pl.multiple_of(g * 512, 512)
    weight_copies = []
    for t in range(TAPS):
        for part in range(2):
            s = names.take()
            weight_copies.append(
                pltpu.make_async_copy(
                    wconv.at[t, pl.ds(2048 * part + g512, 512), :],
                    wall.at[pl.ds(512 * part, 512), pl.ds(128 * t, 128)],
                    sems.at[s],
                )
            )
    for twice in range(2):
        s = names.take()
        weight_copies.append(
            pltpu.make_async_copy(
                wbranch.at[:, pl.ds(g512, 512), :], wb2.at[:, :, pl.ds(128 * twice, 128)], sems.at[s]
            )
        )
    for c in weight_copies:
        c.start()
    due["weights"] = each(weight_copies, "wait")

    for half in range(2):
        bo2[:, 128 * half + WIDE:128 * half + 128, :] = jnp.zeros((4, 128 - WIDE, 512), bf16)
    yp[:, 0:8, :] = jnp.zeros((2, 8, 1152), f32)
    yp[:, 264:272, :] = jnp.zeros((2, 8, 1152), f32)
    gp3[:, :, 0:8, :] = jnp.zeros((3, 2, 8, 128), f32)
    gp3[:, :, 264:272, :] = jnp.zeros((3, 2, 8, 128), f32)
    small[...] = jnp.zeros(small.shape, f32)
    st[...] = jnp.zeros(st.shape, f32)
    p[...] = jnp.zeros(p.shape, f32)
    nb_s[...] = jnp.zeros(nb_s.shape, f32)
    gpre[...] = jnp.zeros(gpre.shape, f32)
    cwt[...] = jnp.zeros(cwt.shape, f32)
    cwt[0:classes, :] = cw_in[...]
    pl.semaphore_wait(barrier, 10)

    q64 = pl.multiple_of(64 * q, 64)
    a_send, a_recv = names.take(8), names.take(8)
    own_row = pl.multiple_of(256 * w + 64 * q, 64)
    own = pltpu.make_async_copy(feat.at[w, :, pl.ds(g512, 512)], x.at[z, pl.ds(own_row, 64), :], sems.at[a_send])

    def tile_copy(t, kx, ky):
        n = 4 * (t + w - 2 * t * w) + 2 * ky + kx
        dev, block = peer(kx, ky, 0)
        return copy(
            feat.at[t, :, pl.ds(pl.multiple_of(512 * block, 512), 512)], x.at[z, pl.ds(own_row, 64), :],
            a_send + n, a_recv + n, {"ha": dev["ha"], "wa": t},
        )

    def tiles(t, method):
        for kx, ky in chips:
            getattr(tile_copy(t, kx, ky), method)()
        pl.when(w != t)(lambda: getattr(tile_copy(t, 0, 0), method)())

    def tiles_wait():
        for n, (kx, ky, kw) in enumerate(plane):
            at = 4 * kw + 2 * ky + kx
            copy(
                feat.at[0, :, pl.ds(0, 512)], x.at[z, pl.ds(own_row, 64), :], a_send + at, a_recv + at, peer(kx, ky, kw)[0]
            ).wait_recv()

    own.start()
    tiles(0, "start")

    def scalars(canvas, micro=None):
        index = 2 * canvas + (w if micro is None else micro)
        return [[boxes[k, e, index] for k in range(3)] for e in range(4)]

    def px(rows, lanes, axis, start=0):
        at = lax.broadcasted_iota(jnp.int32, (rows, lanes), axis) + start
        half = at // 256
        return (at // 8 % 32).astype(f32), (half * 8 + at % 8).astype(f32)

    def tile_valid(micro):
        at = lax.broadcasted_iota(jnp.int32, (64, 128), 0)
        y, xx = (8 * q + at // 8).astype(f32), (8 * w + at % 8).astype(f32)
        top, left, bottom, right = [[v.astype(f32) for v in values] for values in scalars(z, micro)]
        ok = jnp.zeros((64, 128), f32)
        for k in range(3):
            ok = jnp.where((y >= top[k]) & (y < bottom[k]) & (xx >= left[k]) & (xx < right[k]), 1.0, ok)
        return ok

    def layout(c):
        top, left, bottom, right = [[v.astype(f32) for v in values] for values in scalars(c)]
        y, xx = px(512, 128, 0)
        ok = jnp.zeros((512, 128), f32)
        for k in range(3):
            ok = jnp.where((y >= top[k]) & (y < bottom[k]) & (xx >= left[k]) & (xx < right[k]), 1.0, ok)
        val[c] = ok
        table = lane_table[g]
        box, bi, bj, n1, real = [table[e:e + 1] for e in range(5)]
        t_, l_, b_, r_ = [pick3(box, v) for v in (top, left, bottom, right)]
        h1, w1 = b_ - t_ - 1.0, r_ - l_ - 1.0
        rw = jnp.maximum(1.0 - jnp.abs((y - t_) * n1 - bi * h1) / h1, 0.0)
        cw = jnp.maximum(1.0 - jnp.abs((xx - l_) * n1 - bj * w1) / w1, 0.0)
        inside = (y >= t_) & (y < b_) & (xx >= l_) & (xx < r_) & (real > 0.0)
        weights = jnp.where(inside, rw * cw, 0.0)
        high, low = halves(weights)
        u2[c, :, 0:128] = high
        u2[c, :, 128:256] = low
        high, low = halves(weights.T)
        ut[c, 0:128, :] = high
        ut[c, 128:256, :] = low
        box, bi, bj, n, real = [jnp.broadcast_to(row_table[:, e:e + 1], (BINS, 128)) for e in range(5)]
        t_, l_, b_, r_ = [pick3(box, v) for v in (top, left, bottom, right)]
        h, wd = b_ - t_, r_ - l_
        row_low = jnp.floor((bi * h + 0.5) / n)
        row_high = jnp.floor(((bi + 1.0) * h + n - 0.5) / n)
        col_low = jnp.floor((bj * wd + 0.5) / n)
        col_high = jnp.floor(((bj + 1.0) * wd + n - 0.5) / n)
        cnt[c] = jnp.where(real > 0.0, (row_high - row_low) * (col_high - col_low), 1.0)
        for chunk in range(4):
            y, xx = px(BINS, 128, 1, 128 * chunk)
            u, v = y - t_, xx - l_
            member = (u >= row_low) & (u < row_high) & (v >= col_low) & (v < col_high) & (real > 0.0)
            mt[c, :, 128 * chunk:128 * chunk + 128] = jnp.where(member, 1.0, 0.0).astype(bf16)

    def combine():
        out = []
        zs = []
        for b in range(3):
            acc = [None, None]
            for h in range(2):
                for a in range(3):
                    t = 3 * a + b
                    piece = yp[h, 8 * a:8 * a + 256, 128 * t:128 * t + 128]
                    acc[h] = piece if acc[h] is None else acc[h] + piece
            zs.append(acc)
        col = lax.broadcasted_iota(jnp.int32, (256, 128), 0) % 8
        first, last = col == 0, col == 7
        out0 = zs[1][0] + jnp.where(first, 0.0, pltpu.roll(zs[0][0], 1, 0))
        out0 = out0 + jnp.where(last, pltpu.roll(zs[2][1], 7, 0), pltpu.roll(zs[2][0], 255, 0))
        out1 = zs[1][1] + jnp.where(first, pltpu.roll(zs[0][0], 249, 0), pltpu.roll(zs[0][1], 1, 0))
        out1 = out1 + jnp.where(last, 0.0, pltpu.roll(zs[2][1], 255, 0))
        return out0, out1

    def conv_part(operand, part):
        for h in range(2):
            yp[h, 8:264, :] = dot(operand[256 * h:256 * h + 256], wall[512 * part:512 * part + 512, :])
        return combine()

    e_send, e_recv = names.take(16), names.take(12)

    def pre_copy(level, c, kx, ky):
        slot = kx + 2 * ky - 1
        return copy(
            pre.at[c, pl.ds(STARTS[level], SPANS[level]), :],
            prr.at[slot, c, pl.ds(0, SPANS[level]), :],
            e_send + 4 * level + c, e_recv + 4 * slot + c, peer(kx, ky, 0)[0],
        )

    def to_level_owner(level, action):
        lx, ly = level // 2, level % 2
        for kx, ky in chips:
            wanted = (xq + kx - 2 * kx * xq == lx) & (yq + ky - 2 * ky * yq == ly)
            pl.when(wanted)(functools.partial(action, kx, ky))

    def pool(c):
        total = dot(mt[c], x[c])
        for chunk in range(4):
            cols = slice(128 * chunk, 128 * chunk + 128)
            po[c, :, cols] = (total[:, cols] / cnt[c]).astype(bf16)

    def branch_products(c):
        for level in range(4):
            rows = slice(STARTS[level], STARTS[level] + SPANS[level])
            pre[c, rows, :] = dot(po[c, rows, :], wb2[level, :, 0:128])
        for level in range(4):
            to_level_owner(level, lambda kx, ky, level=level: pre_copy(level, c, kx, ky).start())

    def conv_add(c, operand, part):
        out0, out1 = conv_part(operand, part)
        p[c, 0] = p[c, 0] + out0
        p[c, 1] = p[c, 1] + out1

    layout(z)
    for copy_out in (tiles,):
        copy_out(0, "wait_send")
        copy_out(1, "start")
    due["A"] = tiles_wait
    due["A own"] = own.wait
    finals.append(lambda: tiles(1, "wait_send"))

    w64 = pl.multiple_of(64 * w, 64)
    square[...] = jnp.zeros(square.shape, f32)
    for micro in range(2):
        square[pl.ds(w64, 64), 0:classes] = cot[micro] * tile_valid(micro)[:, 0:classes]
        seeds[micro] = square[...].T[0:24]
    sc_send, sc_recv = names.take(), names.take()
    seed_copy = copy(seeds.at[1 - w], seed_in.at[0], sc_send, sc_recv, peer(0, 0, 1)[0])
    seed_copy.start()
    due["seed"] = seed_copy.wait_recv
    finals.append(seed_copy.wait_send)

    arrive("weights")
    arrive("A")
    arrive("A own")
    ok = val[z]
    for chunk in range(4):
        cols = slice(128 * chunk, 128 * chunk + 128)
        x[z, :, cols] = (x[z, :, cols].astype(f32) * ok).astype(bf16)

    up_send, up_recv, dn_send, dn_recv = names.take(6), names.take(6), names.take(6), names.take(6)

    def half_of(c, h):
        return x.at[c, pl.ds(256 * h, 256), :]

    def up_copy(k, h):
        part = half_of(z - k, h)
        return copy(part, part, up_send + 2 * k + h, up_recv + 2 * k + h, {"col": z + 1})

    def dn_copy(k, h):
        part = half_of(z + k, h)
        return copy(part, part, dn_send + 2 * k + h, dn_recv + 2 * k + h, {"col": z - 1})

    def take_in(k, h):
        n = 2 * (k - 1) + h

        @pl.when(z >= k)
        def _():
            part = half_of(z - k, h)
            copy(part, part, up_send + n, up_recv + n, {"col": z}).wait_recv()

        @pl.when(z + k <= 3)
        def _():
            part = half_of(z + k, h)
            copy(part, part, dn_send + n, dn_recv + n, {"col": z}).wait_recv()

    other = peer(0, 0, 1)[0]

    def up_last(k):
        return (w == 0) & (z < 3) & (z == k)

    def dn_last(k):
        return (w == 0) & (z > 0) & (3 - z == k)

    def pass_on(k, h):
        pl.when((z >= k) & (z < 3))(lambda: up_copy(k, h).start())
        pl.when((z + k <= 3) & (z > 0))(lambda: dn_copy(k, h).start())
        if k == 2 and h == 1:
            give_turn(k)

    def passed_on():
        for k in range(3):
            for h in range(2):
                up_done, dn_done = (z >= k) & (z < 3), (z + k <= 3) & (z > 0)
                if h == 0 and k < 2:
                    up_done = up_done & jnp.logical_not(up_last(k))
                    dn_done = dn_done & jnp.logical_not(dn_last(k))
                pl.when(up_done)(lambda: up_copy(k, h).wait_send())
                pl.when(dn_done)(lambda: dn_copy(k, h).wait_send())

    finals.append(passed_on)

    def give_turn(k):
        @pl.when(up_last(k))
        def _():
            if k < 2:
                up_copy(k, 0).wait_send()
            pl.semaphore_signal(turn.at[0], 1, device_id=other, device_id_type=MESH)

        @pl.when(dn_last(k))
        def _():
            if k < 2:
                dn_copy(k, 0).wait_send()
            pl.semaphore_signal(turn.at[1], 1, device_id=other, device_id_type=MESH)

    def own_turn(up):
        def start():
            pl.semaphore_wait(turn.at[0 if up else 1], 1)
            for h in range(2):
                (up_copy(0, h) if up else dn_copy(0, h)).start()

        pl.when((z < 3) if up else (z > 0))(start)

    pool(z)
    h_send, h_recv = names.take(3), names.take(3)
    po_copies = [copy(po.at[z], po.at[z], h_send + j - 1, h_recv + j - 1, zpeer(j)) for j in (1, 2, 3)]

    @pl.when(w == 0)
    def _():
        each(po_copies, "start")()
        pass_on(0, 0)
        pass_on(0, 1)

    finals.append(lambda: pl.when(w == 0)(each(po_copies, "wait_send")))

    arrive("seed")
    sd[z] = seeds[w] + seed_in[0]
    sz_send, sz_recv = names.take(3), names.take(3)
    sd_copies = [copy(sd.at[z], sd.at[z], sz_send + j - 1, sz_recv + j - 1, zpeer(j)) for j in (1, 2, 3)]
    each(sd_copies, "start")()
    finals.append(each(sd_copies, "wait_send"))

    def sd_wait():
        for j in (1, 2, 3):
            src = lax.rem(z + 4 - j, 4)
            copy(sd.at[src], sd.at[src], sz_send + j - 1, sz_recv + j - 1, zpeer(j)).wait_recv()

    due["sd"] = sd_wait

    branch_products(z)
    conv_add(z, x[z], 0)

    def rest(i, carry):
        layout(lax.rem(z + i, 4))
        return carry

    lax.fori_loop(1, 4, rest, 0)

    def pre_wait():
        for c in range(4):
            for kx, ky in chips:
                slot = kx + 2 * ky - 1
                for level in range(4):

                    @pl.when(g == level)
                    def _():
                        copy(
                            pre.at[c, pl.ds(STARTS[level], SPANS[level]), :],
                            prr.at[slot, c, pl.ds(0, SPANS[level]), :],
                            e_send, e_recv + 4 * slot + c, peer(0, 0, 1)[0],
                        ).wait_recv()

    def pre_sent():
        for level in range(4):
            for c in range(4):
                to_level_owner(level, lambda kx, ky: pre_copy(level, c, kx, ky).wait_send())

    finals.append(pre_sent)
    level_n = jnp.where(g == 0, 1.0, jnp.where(g == 1, 2.0, jnp.where(g == 2, 3.0, 6.0)))
    samples = 12.0 * level_n * level_n

    def rows_of(value):
        return value.reshape(4 * WIDE, 128)

    def branch_norm():
        pre_wait()
        for level in range(4):

            @pl.when(g == level)
            def _():
                span = SPANS[level]
                for c in range(4):
                    total = pre[c, STARTS[level]:STARTS[level] + span, :]
                    for slot in range(3):
                        total = total + prr[slot, c, 0:span, :]
                    nb_s[c, 0:span, :] = total

        pre_all = rows_of(nb_s[...])
        average = jnp.sum(pre_all, 0, keepdims=True) / samples
        spread = jnp.sum(pre_all * pre_all, 0, keepdims=True) / samples - average * average
        b_inverse = lax.rsqrt(spread + EPSILON)
        b_norm = (pre_all - average) * b_inverse
        b_act = b_gain * b_norm + bbias[pl.ds(g, 1), :]
        nb_s[...] = b_norm.reshape(4, WIDE, 128)
        bi_s[0:1, :] = b_inverse
        logistic = jax.nn.sigmoid(b_act)
        af_s[...] = (logistic * (1.0 + b_act * (1.0 - logistic))).reshape(4, WIDE, 128)
        bos[...] = (b_act * logistic).astype(bf16).reshape(4, WIDE, 128)
        each(bo_copies, "start")()
        bor[z] = bos[...]

    b_gain = bgain[pl.ds(g, 1), :]
    f_send, f_recv = names.take(3), names.take(3)
    bo_copies = [copy(bos, bor.at[z], f_send + j - 1, f_recv + j - 1, zpeer(j)) for j in (1, 2, 3)]
    finals.append(each(bo_copies, "wait_send"))

    i_send, i_recv = names.take(12), names.take(12)

    def chip_rows(at):
        return pl.ds(pl.multiple_of(64 * at, 64), 64)

    def conv_copy(c, kx, ky):
        slot = kx + 2 * ky - 1
        dev, _ = peer(kx, ky, 0)
        return copy(p.at[c, :, chip_rows(dev["ha"]), :], cr.at[slot, c], i_send + 4 * slot + c, i_recv + 4 * slot + c, dev)

    def conv_send(c):
        for kx, ky in chips:
            conv_copy(c, kx, ky).start()

    def far(c):
        return (c + z == 3) & ((c == 0) | (c == 3))

    def levels(core):
        each(bo_copies, "wait_recv")()
        for part in range(4):
            for half in range(2):
                bo2[:, 128 * half:128 * half + WIDE, 128 * part:128 * part + 128] = bor[part]

        def level_conv(c, carry):
            lv[c] = dot(u2[c], bo2[c]).astype(bf16)
            conv_add(c, lv[c], 1)
            if core == 0:
                pl.when(jnp.logical_not(far(c)))(lambda: conv_send(c))
            else:
                conv_send(c)
            return carry

        lax.fori_loop(0, 4, level_conv, 0)

    @pl.when(w == 0)
    def _():
        def one(j, carry):
            src = lax.rem(z + 4 - j, 4)
            copy(po.at[src], po.at[src], h_send + j - 1, h_recv + j - 1, zpeer(j)).wait_recv()
            branch_products(src)
            return carry

        lax.fori_loop(1, 4, one, 0)

    @pl.when((w == 1) & (zm == 0))
    def _():
        own_turn(True)
        own_turn(False)

    @pl.when((w == 1) & (zm == 1))
    def _():
        own_turn(False)
        own_turn(True)

    def arrived(c):
        @pl.when(w == 1)
        def _():
            pool(c)
            branch_products(c)

        pl.when(w == 0)(lambda: conv_add(c, x[c], 0))

    for k in (1, 2, 3):
        if k < 3:
            give_turn(k - 1)
        for h in range(2):
            take_in(k, h)
            if k < 3:
                pass_on(k, h)
        pl.when(z >= k)(lambda: arrived(z - k))
        pl.when(z + k <= 3)(lambda: arrived(z + k))
        if k == 1:
            pl.when(w == 0)(branch_norm)
        if k == 2:
            pl.when(w == 0)(lambda: levels(0))

    pl.when((w == 0) & far(3 - z))(lambda: conv_send(3 - z))

    @pl.when(w == 1)
    def _():
        branch_norm()

        def late(j, carry):
            c = lax.rem(z + j, 4)
            conv_add(c, x[c], 0)
            return carry

        lax.fori_loop(1, 4, late, 0)
        levels(1)

    conv_copies = [conv_copy(c, kx, ky) for c in range(4) for kx, ky in chips]
    due["conv"] = each(conv_copies, "wait_recv")
    finals.append(each(conv_copies, "wait_send"))

    arrive("sd")
    for c in range(4):
        cn_s[0, 128 * c:128 * c + 128, :] = dot(sd[c], cwt[...], ROWS_T, FULL_ACCURACY)

    arrive("conv")
    convolved = (p[:, :, pl.ds(q64, 64), :] + cr[0] + cr[1] + cr[2]).reshape(512, 128)
    ok = val.at[...].reshape(4, 2, 256, 128)[:, :, pl.ds(q64, 64), :].reshape(512, 128)

    j_send, j_recv = names.take(6), names.take(6)

    def stat_copy(stage, kx, ky):
        slot = kx + 2 * ky - 1
        return copy(
            st.at[stage], str_.at[stage, slot], j_send + 3 * stage + slot, j_recv + 3 * stage + slot, peer(kx, ky, 0)[0]
        )

    def plane_sum(stage, first, second):
        st[stage, 0:1, :] = first
        st[stage, 1:2, :] = second
        copies = [stat_copy(stage, kx, ky) for kx, ky in chips]
        each(copies, "start")()
        each(copies, "wait_recv")()
        finals.append(each(copies, "wait_send"))
        total = st[stage] + str_[stage, 0] + str_[stage, 1] + str_[stage, 2]
        return total[0:1], total[1:2]

    masked = convolved * ok
    first, second = plane_sum(0, jnp.sum(masked, 0, keepdims=True), jnp.sum(convolved * masked, 0, keepdims=True))
    area = jnp.int32(0)
    for c in range(4):
        top, left, bottom, right = scalars(c)
        for k in range(3):
            area = area + (bottom[k] - top[k]) * (right[k] - left[k])
    valid_total = area.astype(f32)
    average = first / valid_total
    spread = second / valid_total - average * average
    inverse = lax.rsqrt(spread + EPSILON)
    normed = (convolved - average) * inverse
    gain = ngain[...]
    affine = gain * normed + nbias[...]
    logistic = jax.nn.sigmoid(affine)
    hidden = affine * logistic
    grad_affine = cn_s[0] * (logistic * (1.0 + affine * (1.0 - logistic)))
    part_bias = jnp.sum(grad_affine, 0, keepdims=True)
    part_gain = jnp.sum(grad_affine * normed, 0, keepdims=True)
    cn_s[1] = hidden
    small[48:49, :] = part_bias
    small[49:50, :] = part_gain
    bias_sum, gain_sum = plane_sum(1, part_bias, part_gain)
    grad_conv = ok * inverse * (
        grad_affine * gain - gain * bias_sum / valid_total - normed * gain * gain_sum / valid_total
    )
    gc[:, :, pl.ds(q64, 64), :] = grad_conv.astype(bf16).reshape(4, 2, 64, 128)
    k_send, k_recv = names.take(3), names.take(3)

    def gc_copy(kx, ky, at):
        slot = kx + 2 * ky - 1
        block = gc.at[:, :, chip_rows(at), :]
        return copy(block, block, k_send + slot, k_recv + slot, peer(kx, ky, 0)[0])

    gc_copies = [gc_copy(kx, ky, q) for kx, ky in chips]
    each(gc_copies, "start")()
    due["gc"] = each(gc_copies, "wait_recv")
    finals.append(each(gc_copies, "wait_send"))

    arrive("gc")

    def shifted(c):
        col = lax.broadcasted_iota(jnp.int32, (256, 128), 0) % 8
        first, last = col == 0, col == 7
        g0, g1 = gc[c, 0].astype(f32), gc[c, 1].astype(f32)
        gp3[1, 0, 8:264, :] = g0
        gp3[1, 1, 8:264, :] = g1
        gp3[0, 0, 8:264, :] = jnp.where(last, pltpu.roll(g1, 7, 0), pltpu.roll(g0, 255, 0))
        gp3[0, 1, 8:264, :] = jnp.where(last, 0.0, pltpu.roll(g1, 255, 0))
        gp3[2, 0, 8:264, :] = jnp.where(first, 0.0, pltpu.roll(g0, 1, 0))
        gp3[2, 1, 8:264, :] = jnp.where(first, pltpu.roll(g0, 249, 0), pltpu.roll(g1, 1, 0))
        for a in range(3):
            for b in range(3):
                t = 3 * a + b
                for h in range(2):
                    start = 8 * (2 - a)
                    g9[c, 256 * h:256 * h + 256, 128 * t:128 * t + 128] = gp3[b, h, start:start + 256, :].astype(bf16)

    def level_rows(c, carry):
        shifted(c)
        both = dot(ut[c], g9[c])
        high, low = halves(both[0:128] + both[128:256])
        tb[c, 0:128, :] = high
        tb[c, 128:256, :] = low
        return carry

    def data_grad(c):
        for h in range(2):
            dxf[c, 256 * h:256 * h + 256, :] = dot(g9[c, 256 * h:256 * h + 256, :], wall[0:512, :], BOTH_LAST)

    ru_send, ru_recv, rd_send, rd_recv = names.take(3), names.take(3), names.take(3), names.take(3)

    def ru_copy(k):
        return copy(sbu.at[k], rxu.at[k], ru_send + k, ru_recv + k, {"col": z + 1})

    def rd_copy(k):
        return copy(sbd.at[k], rxd.at[k], rd_send + k, rd_recv + k, {"col": z - 1})

    def up_on(k):
        return (z + 3 - k <= 3) & (z < 3)

    def dn_on(k):
        return (z - 3 + k >= 0) & (z > 0)

    def end_send(k):
        @pl.when(z == 0)
        def _():
            sbu[k] = dxf[3 - k].astype(bf16)
            ru_copy(k).start()

        @pl.when(z == 3)
        def _():
            sbd[k] = dxf[k].astype(bf16)
            rd_copy(k).start()

    def middle_send(k):
        @pl.when(up_on(k) & (z > 0))
        def _():
            ru_copy(k - 1).wait_recv()
            sbu[k] = (dxf[z + 3 - k] + rxu[k - 1].astype(f32)).astype(bf16)
            ru_copy(k).start()

        @pl.when(dn_on(k) & (z < 3))
        def _():
            rd_copy(k - 1).wait_recv()
            sbd[k] = (dxf[z - 3 + k] + rxd[k - 1].astype(f32)).astype(bf16)
            rd_copy(k).start()

    def scatter_sent():
        for k in range(3):
            pl.when(up_on(k))(lambda: ru_copy(k).wait_send())
            pl.when(dn_on(k))(lambda: rd_copy(k).wait_send())

    def canvas_at(i):
        low = (3 - i) if i < 2 else zz * (i - 2) + (1 - zz) * (3 - i)
        return (1 - zm) * low + zm * (3 - low)

    n_send, n_recv = names.take(3), names.take(3)

    def gb_copies(method):
        for level in range(4):

            @pl.when(g == level)
            def _():
                for j in (1, 2, 3):
                    item = copy(
                        gb.at[lax.rem(z + j, 4), :, pl.ds(0, SPANS[level]), :],
                        grr.at[j - 1, :, pl.ds(0, SPANS[level]), :],
                        n_send + j - 1, n_recv + j - 1, zpeer(j),
                    )
                    getattr(item, method)()

    lax.fori_loop(0, 4, level_rows, 0)

    def level_pair(n, carry):
        both = dot(tb[pl.ds(2 * n, 2)].reshape(512, 1152), wall[512:1024, :], BOTH_LAST)
        for c in range(2):
            total = both[256 * c:256 * c + WIDE] + both[256 * c + 128:256 * c + 128 + WIDE]
            for part in range(4):
                gb[part, 2 * n + c] = total[:, 128 * part:128 * part + 128].astype(bf16)
        return carry

    lax.fori_loop(0, 2, level_pair, 0)
    gb_copies("start")
    due["gb"] = lambda: gb_copies("wait_recv")
    finals.append(lambda: gb_copies("wait_send"))

    def weight_grad(part, slot):

        for tile in range(2):
            cols = slice(256 * tile, 256 * tile + 256)

            def of(operand):
                total = None
                for c in range(4):
                    piece = dot(operand[c, :, cols], g9[c], ROWS_T)
                    total = piece if total is None else total + piece
                dw[slot, cols, :] = total

            pl.when(part == 0)(lambda: of(x))
            pl.when(part == 1)(lambda: of(lv))

    w_send, w_recv = names.take(), names.take()
    dw_copy = copy(dw.at[0], dwr, w_send, w_recv, other)
    y_send, y_recv = names.take(), names.take()
    dw_y = copy(dwh, dwx, y_send, y_recv, {"ha": peer(0, 1, 0)[0]["ha"], "wa": yq})
    b_send, b_recv = names.take(), names.take()
    dw_back = copy(dw.at[1], dwr, b_send, b_recv, other)
    cg_sem = names.take()

    def cg_out(src):
        return pltpu.make_async_copy(src, cgrad_out, sems.at[cg_sem])

    weight_grad(1 - yq, w)
    pl.when(w == 0)(lambda: dw_copy.start())

    @pl.when(w == 1)
    def _():
        dw_copy.wait_recv()
        dwh[...] = (dw[1] + dwr[...]).astype(bf16)
        dw_y.start()

    for i in range(4):
        data_grad(canvas_at(i))
        if i < 3:
            end_send(i)

    arrive("gb")
    for level in range(4):

        @pl.when(g == level)
        def _():
            span = SPANS[level]
            total = gb[z, :, 0:span, :].astype(f32)
            for j in range(3):
                total = total + grr[j, :, 0:span, :].astype(f32)
            gpre[:, 0:span, :] = total

    grad_act = rows_of(gpre[...]) * rows_of(af_s[...])
    b_norm = rows_of(nb_s[...])
    act_sum = jnp.sum(grad_act, 0, keepdims=True)
    act_norm_sum = jnp.sum(grad_act * b_norm, 0, keepdims=True)
    small[50:51, :] = act_norm_sum
    small[51:52, :] = act_sum
    grad_pre = bi_s[0:1, :] * (
        b_gain * grad_act - b_gain * act_sum / samples - b_norm * b_gain * act_norm_sum / samples
    )
    gpre[...] = grad_pre.reshape(4, WIDE, 128)
    o_send, o_recv = names.take(3), names.take(12)

    def gpre_copies(method):
        for level in range(4):

            @pl.when(g == level)
            def _():
                rows = pl.ds(STARTS[level], SPANS[level])
                for kx, ky in chips:
                    slot = kx + 2 * ky - 1
                    c = copy(
                        gpre.at[:, pl.ds(0, SPANS[level]), :], gpa.at[:, rows, :],
                        o_send + slot, o_recv + 3 * level + slot, peer(kx, ky, 0)[0],
                    )
                    getattr(c, method)()

    def gpre_wait():
        for level in range(4):

            def wait(kx, ky):
                slot = kx + 2 * ky - 1
                copy(
                    gpre.at[:, pl.ds(0, SPANS[level]), :],
                    gpa.at[:, pl.ds(STARTS[level], SPANS[level]), :],
                    o_send + slot, o_recv + 3 * level + slot, peer(kx, ky, 0)[0],
                ).wait_recv()

            to_level_owner(level, wait)

    gpre_copies("start")
    for level in range(4):

        @pl.when(g == level)
        def _():
            gpa[:, STARTS[level]:STARTS[level] + SPANS[level], :] = gpre[:, 0:SPANS[level], :]

    due["gpre"] = gpre_wait
    finals.append(lambda: gpre_copies("wait_send"))

    middle_send(1)

    lt_send, lt_recv = names.take(3), names.take(3)
    weight_part = jnp.zeros((24, 128), f32)
    bias_part = jnp.zeros((24, 1), f32)
    for c in range(4):
        hidden_c = cn_s[1, 128 * c:128 * c + 128, :]
        lt[c] = dot(cwt[...], hidden_c, BOTH_LAST, FULL_ACCURACY)
        weight_part = weight_part + dot(sd[c], hidden_c, precision=FULL_ACCURACY)
        bias_part = bias_part + jnp.sum(sd[c], 1, keepdims=True)
    small[0:24, :] = weight_part
    small[24:48, :] = jnp.broadcast_to(bias_part, (24, 128))
    lt_copies = [
        copy(lt.at[lax.rem(z + j, 4)], ltr.at[j - 1], lt_send + j - 1, lt_recv + j - 1, zpeer(j)) for j in (1, 2, 3)
    ]
    each(lt_copies, "start")()
    due["lt"] = each(lt_copies, "wait_recv")
    finals.append(each(lt_copies, "wait_send"))

    arrive("gpre")

    def split_rows(c, carry):
        high, low = halves(gpa[c])
        gpx[c, :, 0:128] = high
        gpx[c, :, 128:256] = low
        return carry

    lax.fori_loop(0, 4, split_rows, 0)

    for level in range(4):
        rows = slice(STARTS[level], STARTS[level] + SPANS[level])
        total = None
        for c in range(4):
            piece = dot(po[c, rows, :], gpx[c, rows, :], ROWS_T)
            total = piece if total is None else total + piece
        bg[level] = total[:, 0:128] + total[:, 128:256]
    bc_send, bc_recv = names.take(), names.take()
    w256 = pl.multiple_of(256 * w, 256)
    v256 = pl.multiple_of(256 * (1 - w), 256)
    bg_copy = copy(bg.at[:, pl.ds(v256, 256), :], bgr, bc_send, bc_recv, peer(0, 0, 1)[0])
    bg_copy.start()
    due["bgc"] = bg_copy.wait_recv
    finals.append(bg_copy.wait_send)

    def pooled_grad(c, carry):
        for level in range(4):
            rows = slice(STARTS[level], STARTS[level] + SPANS[level])
            gps[c, rows, :] = dot(gpx[c, rows, :], wb2[level], BOTH_LAST).astype(bf16)
        return carry

    lax.fori_loop(0, 4, pooled_grad, 0)
    p_send, p_recv = names.take(3), names.take(3)
    gp_copies = [
        copy(gps.at[lax.rem(z + j, 4)], gpr.at[j - 1], p_send + j - 1, p_recv + j - 1, zpeer(j)) for j in (1, 2, 3)
    ]
    each(gp_copies, "start")()
    due["gp"] = each(gp_copies, "wait_recv")
    finals.append(each(gp_copies, "wait_send"))

    bg_wait = due.pop("bgc")
    own_channels = pl.ds(pl.multiple_of(512 * g + 256 * w, 256), 256)
    bx_send, bx_recv = names.take(3), names.take(3)
    by_send, by_recv = names.take(4), names.take(4)

    def bga_of(block, core):
        return bga.at[:, pl.ds(pl.multiple_of(512 * block + 256 * core, 256), 256), :]

    def bg_chip(kx, ky):
        slot = kx + 2 * ky - 1
        return copy(bgh, bga_of(g, w), bx_send + slot, bx_recv + slot, peer(kx, ky, 0)[0])

    def bg_core(n, block):
        return copy(bga_of(block, w), bga_of(block, w), by_send + n, by_recv + n, peer(0, 0, 1)[0])

    bg_copies = [bg_chip(kx, ky) for kx, ky in chips]
    due["bg"] = each(bg_copies, "wait_recv")
    finals.append(each(bg_copies, "wait_send"))
    bg_own = bg_core(3, g)
    finals.append(bg_own.wait_send)
    due["by", 3] = bg_own.wait_recv

    def bg_sum():
        bg_wait()
        bgh[...] = (bg[:, pl.ds(w256, 256), :] + bgr[...]).astype(bf16)
        each(bg_copies, "start")()
        bga[:, own_channels, :] = bgh[...]
        bg_own.start()

    pl.when(w == 1)(bg_sum)

    middle_send(2)
    finals.append(scatter_sent)

    weight_grad(yq, 1 - w)
    pl.when(w == 1)(lambda: dw_copy.start())

    def dw_sum():
        @pl.when(w == 0)
        def _():
            dw_copy.wait_recv()
            dw[1] = dw[1] + dwr[...]
            pl.when(yq == 0)(lambda: cg_out(dw.at[1]).start())
            pl.when(yq == 1)(lambda: dw_back.start())

    def dw_place():
        @pl.when((w == 1) & (yq == 1))
        def _():
            dw_back.wait_recv()
            cg_out(dwr).start()

        dw_copy.wait_send()

        @pl.when(w != yq)
        def _():
            dw_y.wait_recv()
            dw[0] = dwx[...].astype(f32)
            cg_out(dw.at[0]).start()

    due["dw"] = dw_sum
    due["dwy"] = dw_place
    finals.append(lambda: cg_out(dw.at[0]).wait())
    finals.append(lambda: pl.when(w == 1)(lambda: dw_y.wait_send()))
    finals.append(lambda: pl.when((w == 0) & (yq == 1))(lambda: dw_back.wait_send()))

    s_send, s_recv = names.take(7), names.take(7)

    def small_copy(n):
        return copy(small, smr.at[n], s_send + n, s_recv + n, peer(*plane[n])[0])

    small_copies = [small_copy(n) for n in range(7)]
    each(small_copies, "start")()
    due["small"] = each(small_copies, "wait_recv")
    finals.append(each(small_copies, "wait_send"))


    gp_wait = due.pop("gp")

    def ru_wait():
        pl.when(z > 0)(lambda: ru_copy(2).wait_recv())

    def rd_wait():
        pl.when(z < 3)(lambda: rd_copy(2).wait_recv())

    q_send, q_recv = names.take(8), names.take(8)

    def fg_copy(n):
        dev, _ = peer(*plane[n])
        rows = pl.ds(pl.multiple_of(256 * dev["wa"] + 64 * dev["ha"], 64), 64)
        return copy(fgh.at[rows, :], fgrad_out.at[w, :, pl.ds(g512, 512)], q_send + n, q_recv + n, dev)

    fg_copies = [fg_copy(n) for n in range(7)]
    finals.append(each(fg_copies, "wait_send"))
    fg_own = pltpu.make_async_copy(
        fgh.at[pl.ds(own_row, 64), :], fgrad_out.at[w, :, pl.ds(g512, 512)], sems.at[q_send + 7]
    )
    finals.append(fg_own.wait)

    def fg_wait():
        for n in range(7):
            dev, block = peer(*plane[n])
            copy(
                fgh.at[pl.ds(0, 64), :],
                fgrad_out.at[dev["wa"], :, pl.ds(pl.multiple_of(512 * block, 512), 512)],
                q_send + n, q_recv + n, dev,
            ).wait_recv()

    finals.append(fg_wait)

    def feature_grads():
        gp_wait()
        pooled_back = gps[z].astype(f32)
        for j in range(3):
            pooled_back = pooled_back + gpr[j].astype(f32)
        count = cnt[z]
        pieces = [pooled_back[:, 128 * chunk:128 * chunk + 128] / count for chunk in range(4)]
        high, low = halves(jnp.concatenate(pieces, 1))
        fg[...] = dot(mt[z], high, ROWS_T) + dot(mt[z], low, ROWS_T)
        ok = val[z]

        ru_wait()
        rd_wait()

        @pl.when(z > 0)
        def _():
            dxf[z] = dxf[z] + rxu[2].astype(f32)

        @pl.when(z < 3)
        def _():
            dxf[z] = dxf[z] + rxd[2].astype(f32)

        for chunk in range(4):
            cols = slice(128 * chunk, 128 * chunk + 128)
            fgh[:, cols] = (fg[:, cols] + dxf[z, :, cols] * ok).astype(bf16)
        each(fg_copies, "start")()
        fg_own.start()

    @pl.when(w == 0)
    def _():
        feature_grads()
        bg_sum()

    arrive("dw")

    arrive("lt")
    lts[w] = lt[z] + ltr[0] + ltr[1] + ltr[2]
    ls_send, ls_recv = names.take(), names.take()
    logits_copy = copy(lts.at[w], lts.at[w], ls_send, ls_recv, peer(0, 0, 1)[0])
    logits_copy.start()
    due["ls"] = logits_copy.wait_recv
    finals.append(logits_copy.wait_send)

    pl.when(w == 1)(feature_grads)

    arrive("bg")
    for n, (kx, ky) in enumerate(chips):
        item = bg_core(n, peer(kx, ky, 0)[1])
        item.start()
        finals.append(item.wait_send)
        due["by", n] = item.wait_recv

    arrive("small")
    total = small[...]
    for n in range(7):
        total = total + smr[n]
    small_out[0:48, :] = total[0:48]
    small_out[48:56, :] = total[48:56]
    for kx, ky in [(0, 0)] + chips:
        dev, block = peer(kx, ky, 0)
        mine = small[...] if kx + ky == 0 else smr[plane.index((kx, ky, 0))]
        both = mine + smr[plane.index((kx, ky, 1))]
        small_out[pl.ds(56 + block, 1), :] = both[50:51]
        small_out[pl.ds(60 + block, 1), :] = both[51:52]

    arrive("ls")
    for micro in range(2):
        square[:, 0:24] = lts[micro].T
        tile = square[pl.ds(w64, 64), 0:classes] + cb[...]
        logits_out[micro] = tile * tile_valid(micro)[:, 0:classes]

    for n in range(4):
        arrive(("by", n))
    out_sem = names.take()
    bg_out = pltpu.make_async_copy(bga, bgrad_out, sems.at[out_sem])
    bg_out.start()

    finals.append(bg_out.wait)

    arrive("dwy")

    for wait in finals:
        wait()
    assert not due
    assert names.count <= SEMAPHORES


SEMAPHORES = 256


def place_kernel(
    logits, fgrad, bgrad, small, cgrad,
    logits_out, fgrad_out, bgrad_out, gains_out, biases_out, cgrad_out, gain_out, bias_out, weight_out, class_out,
    low, wide, feats, feats_wide, taps, square, sems,
):
    levels, classes, micros = bgrad.shape[0], class_out.shape[1], fgrad.shape[0]
    half = bgrad.shape[1] // 2
    pieces = [(n, pl.ds(half * h, half)) for n in range(levels) for h in range(2)]
    count = len(pieces)
    loads = [pltpu.make_async_copy(bgrad.at[p], low.at[p], sems.at[n]) for n, p in enumerate(pieces)]
    loads += [pltpu.make_async_copy(fgrad.at[m], feats.at[m], sems.at[count + m]) for m in range(micros)]
    tap_load = pltpu.make_async_copy(cgrad, taps, sems.at[count + micros])
    for load in loads:
        load.start()
    tap_load.start()
    first = count + micros + 1
    stores = [pltpu.make_async_copy(wide.at[p], bgrad_out.at[p], sems.at[first + n]) for n, p in enumerate(pieces)]
    stores += [
        pltpu.make_async_copy(feats_wide.at[m], fgrad_out.at[m], sems.at[first + count + m]) for m in range(micros)
    ]
    tap_stores = [
        pltpu.make_async_copy(taps.at[:, pl.ds(128 * t, 128)], cgrad_out.at[t], sems.at[first + count + micros + t])
        for t in range(TAPS)
    ]
    for n, p in enumerate(pieces):
        loads[n].wait()
        wide[p] = low[p].astype(jnp.float32)
        stores[n].start()
    for m in range(micros):
        loads[count + m].wait()
        feats_wide[m] = feats[m].astype(jnp.float32)
        stores[count + m].start()
    tap_load.wait()
    for store in tap_stores:
        store.start()
    logits_out[...] = logits[...]
    gains_out[...] = small[56:60, :]
    biases_out[...] = small[60:64, :]
    gain_out[...] = small[49:50, :]
    bias_out[...] = small[48:49, :]
    weight_out[...] = small[0:classes, :]
    square[...] = small[...]
    class_out[...] = square[24:56, :].T[0:1, 0:classes]
    for store in stores + tap_stores:
        store.wait()


def canvas_body(
    mesh, features, region_boxes, branch_weight, branch_gain, branch_bias, conv_weight, norm_gain, norm_bias,
    class_weight, class_bias, cotangent,
):
    f32, bf16 = jnp.float32, jnp.bfloat16
    micros, tile_rows, tile_cols, channels = features.shape
    pixels = tile_rows * tile_cols
    classes = class_bias.shape[0]
    lane_table, row_table = bin_tables()

    vmem = pl.BlockSpec(memory_space=pltpu.VMEM)
    hbm = pl.BlockSpec(memory_space=pl.ANY)
    smem = pl.BlockSpec(memory_space=pltpu.SMEM)
    V = pltpu.VMEM
    scratch = [
        V((4, 512, 512), bf16),
        V((4, 512, 512), bf16),
        V((1024, 1152), bf16),
        V((4, 512, 256), bf16),
        V((4, 512, 256), bf16),
        V((4, 256, 512), bf16),
        V((4, BINS, 512), bf16),
        V((4, BINS, 128), f32),
        V((4, BINS, 512), bf16),
        V((4, BINS, 128), f32),
        V((3, 4, WIDE, 128), f32),
        V((4, WIDE, 128), bf16),
        V((4, 4, WIDE, 128), bf16),
        V((4, 256, 512), bf16),
        V((4, 512, 128), f32),
        V((2, 272, 1152), f32),
        V((4, 2, 256, 128), f32),
        V((3, 4, 2, 64, 128), f32),
        V((4, 2, 256, 128), bf16),
        V((4, 512, 1152), bf16),
        V((3, 2, 272, 128), f32),
        V((4, 256, 1152), bf16),
        V((4, 512, 512), f32),
        V((3, 512, 512), bf16),
        V((3, 512, 512), bf16),
        V((3, 512, 512), bf16),
        V((3, 512, 512), bf16),
        V((4, 4, WIDE, 128), bf16),
        V((3, 4, WIDE, 128), bf16),
        V((4, WIDE, 128), f32),
        V((4, BINS, 128), f32),
        V((4, BINS, 256), bf16),
        V((4, BINS, 512), bf16),
        V((3, BINS, 512), bf16),
        V((2, 512, 1152), f32),
        V((512, 1152), f32),
        V((4, 512, 128), f32),
        V((4, 256, 128), f32),
        V((4, 256, 128), bf16),
        V((1, 24, 128), f32),
        V((4, 24, 128), f32),
        V((4, 24, 128), f32),
        V((3, 24, 128), f32),
        V((2, 24, 128), f32),
        V((2, 8, 128), f32),
        V((2, 3, 8, 128), f32),
        V((56, 128), f32),
        V((7, 56, 128), f32),
        V((4, WIDE, 128), f32),
        V((4, WIDE, 128), f32),
        V((2, 512, 128), f32),
        V((4, channels, 128), bf16),
        V((512, 512), f32),
        V((512, 512), bf16),
        V((24, 128), f32),
        V((2, 24, 128), f32),
        V((128, 128), f32),
        V((512, 1152), bf16),
        V((512, 1152), bf16),
        V((8, 128), f32),
        pltpu.SemaphoreType.DMA((SEMAPHORES,)),
        pltpu.SemaphoreType.REGULAR((2,)),
    ]
    share = conv_weight.shape[2]
    parts = pl.pallas_call(
        head_kernel,
        out_shape=(
            jax.ShapeDtypeStruct((micros, pixels, classes), f32),
            jax.ShapeDtypeStruct((micros, pixels, channels), bf16),
            jax.ShapeDtypeStruct((4, channels, share), bf16),
            jax.ShapeDtypeStruct((64, 128), f32),
            jax.ShapeDtypeStruct((512, TAPS * share), f32),
        ),
        in_specs=[smem, vmem, vmem, hbm, vmem, hbm, hbm, vmem, vmem, vmem, vmem, vmem, vmem],
        out_specs=(vmem, hbm, hbm, vmem, hbm),
        scratch_shapes=scratch,
        compiler_params=pltpu.CompilerParams(
            collective_id=0, has_side_effects=True, vmem_limit_bytes=60 * 2**20
        ),
    )(
        jnp.transpose(region_boxes, (1, 2, 0)), lane_table, row_table, features.reshape(micros, pixels, channels),
        cotangent.reshape(micros, pixels, classes), conv_weight, branch_weight, branch_gain, branch_bias,
        norm_gain.reshape(1, -1), norm_bias.reshape(1, -1), class_weight.T, class_bias.reshape(1, -1),
    )
    logits, feature_grad, branch_grad, gains, biases, conv_grad, gain, bias, weight, class_grad = pl.pallas_call(
        place_kernel,
        out_shape=(
            jax.ShapeDtypeStruct((micros, pixels, classes), f32),
            jax.ShapeDtypeStruct((micros, pixels, channels), f32),
            jax.ShapeDtypeStruct((4, channels, share), f32),
            jax.ShapeDtypeStruct((4, share), f32),
            jax.ShapeDtypeStruct((4, share), f32),
            jax.ShapeDtypeStruct((TAPS, 512, share), f32),
            jax.ShapeDtypeStruct((1, share), f32),
            jax.ShapeDtypeStruct((1, share), f32),
            jax.ShapeDtypeStruct((classes, share), f32),
            jax.ShapeDtypeStruct((1, classes), f32),
        ),
        in_specs=[vmem, hbm, hbm, vmem, hbm],
        out_specs=(vmem, hbm, hbm, vmem, vmem, hbm, vmem, vmem, vmem, vmem),
        scratch_shapes=[
            V((4, channels, share), bf16), V((4, channels, share), f32), V((micros, pixels, channels), bf16),
            V((micros, pixels, channels), f32), V((512, TAPS * share), f32), V((64, 128), f32),
            pltpu.SemaphoreType.DMA((40,)),
        ],
        compiler_params=pltpu.CompilerParams(vmem_limit_bytes=60 * 2**20),
    )(*parts)
    return (
        logits.reshape(micros, tile_rows, tile_cols, classes),
        feature_grad.reshape(features.shape),
        branch_grad,
        gains,
        biases,
        conv_grad,
        gain.reshape(-1),
        bias.reshape(-1),
        weight.T,
        class_grad.reshape(-1),
    )


def extended(block, sides, width):
    for axis, dim in sides:
        count = lax.axis_size(axis)
        forward = [(i, i + 1) for i in range(count - 1)]
        backward = [(target, source) for source, target in forward]
        low = lax.ppermute(
            lax.slice_in_dim(block, block.shape[dim] - width, None, axis=dim), axis, forward
        )
        high = lax.ppermute(lax.slice_in_dim(block, 0, width, axis=dim), axis, backward)
        block = jnp.concatenate([low, block, high], axis=dim)
    return block


def interpolate(offset, extent, n, bin_ids):
    scaled = offset * (n - 1)
    lower_bin = scaled // (extent - 1)
    fraction = (scaled - lower_bin * (extent - 1)).astype(jnp.float32) / (extent - 1).astype(
        jnp.float32
    )
    upper_bin = jnp.minimum(lower_bin + 1, n - 1)
    lower_hit = (bin_ids[None, :] == lower_bin[:, None]).astype(jnp.float32)
    upper_hit = (bin_ids[None, :] == upper_bin[:, None]).astype(jnp.float32)
    return (1.0 - fraction)[:, None] * lower_hit + fraction[:, None] * upper_hit


def layout(region, row_ids, col_ids):
    member_cols = []
    count_cols = []
    weight_per_level = []
    validity = jnp.zeros(row_ids.shape, jnp.float32)
    for n in LEVELS:
        bin_ids = jnp.arange(n, dtype=jnp.int32)
        level_weights = []
        for k in range(region.shape[0]):
            row_start = region[k, 0]
            col_start = region[k, 1]
            height = region[k, 2] - row_start
            width = region[k, 3] - col_start
            row_offset = row_ids - row_start
            col_offset = col_ids - col_start
            inside = (
                (row_offset >= 0) & (row_offset < height) & (col_offset >= 0) & (col_offset < width)
            )
            row_low = bin_ids * height // n
            row_high = ((bin_ids + 1) * height + n - 1) // n
            col_low = bin_ids * width // n
            col_high = ((bin_ids + 1) * width + n - 1) // n
            row_in = (row_offset[:, None] >= row_low[None, :]) & (
                row_offset[:, None] < row_high[None, :]
            )
            col_in = (col_offset[:, None] >= col_low[None, :]) & (
                col_offset[:, None] < col_high[None, :]
            )
            member = row_in[:, :, None] & col_in[:, None, :] & inside[:, None, None]
            member_cols.append(member.reshape(-1, n * n).astype(jnp.float32))
            count_cols.append(
                ((row_high - row_low)[:, None] * (col_high - col_low)[None, :]).reshape(n * n)
            )
            row_weight = interpolate(row_offset, height, n, bin_ids)
            col_weight = interpolate(col_offset, width, n, bin_ids)
            bilinear = (
                row_weight[:, :, None]
                * col_weight[:, None, :]
                * inside.astype(jnp.float32)[:, None, None]
            )
            level_weights.append(bilinear.reshape(-1, n * n))
            if n == 1:
                validity = validity + inside.astype(jnp.float32)
        weight_per_level.append(jnp.concatenate(level_weights, 1))
    counts = jnp.concatenate(count_cols).astype(jnp.float32)
    return (jnp.concatenate(member_cols, 1), weight_per_level, counts, validity)


def silu_slope(inputs):
    logistic = jax.nn.sigmoid(inputs)
    return logistic * (1.0 + inputs * (1.0 - logistic))


def tiled_body(
    features,
    region_boxes,
    branch_weight,
    branch_gain,
    branch_bias,
    conv_weight,
    norm_gain,
    norm_bias,
    class_weight,
    class_bias,
    cotangent,
):
    micros, tile_rows, tile_cols, channels = features.shape
    groups = lax.axis_size("col")
    regions = region_boxes.shape[1]
    share = conv_weight.shape[2]
    width_out = share * groups
    pixels = tile_rows * tile_cols
    flat_rows = groups * pixels
    col_index = lax.axis_index("col")
    tile_row_ids = lax.axis_index("ha") * tile_rows + jnp.arange(tile_rows, dtype=jnp.int32)
    tile_col_ids = lax.axis_index("wa") * tile_cols + jnp.arange(tile_cols, dtype=jnp.int32)
    row_ids = jnp.repeat(tile_row_ids, tile_cols)
    col_ids = jnp.tile(tile_col_ids, tile_rows)
    conv_flat = conv_weight.reshape(-1, share)
    conv_back = jnp.transpose(conv_weight, (0, 2, 1)).reshape(-1, conv_weight.shape[1])
    spans = [regions * n * n for n in LEVELS]
    starts = [sum(spans[:level_number]) for level_number in range(len(LEVELS))]
    grouped_boxes = region_boxes.reshape(groups, micros, regions, 4)
    branch_float = branch_weight.astype(jnp.float32)
    branch_grads = [jnp.zeros((channels, share), jnp.float32) for level_number in range(4)]
    branch_gain_grads = [jnp.zeros((share,), jnp.float32) for level_number in range(4)]
    branch_bias_grads = [jnp.zeros((share,), jnp.float32) for level_number in range(4)]
    norm_gain_total = jnp.zeros((share,), jnp.float32)
    norm_bias_total = jnp.zeros((share,), jnp.float32)
    class_weight_total = jnp.zeros(class_weight.shape, jnp.float32)
    class_bias_total = jnp.zeros(class_bias.shape, jnp.float32)
    conv_total = jnp.zeros(conv_flat.shape, jnp.float32)
    logit_list = []
    feature_list = []
    for m in range(micros):
        boxes_now = grouped_boxes[:, m]
        member_pixels, weight_per_level, counts, validity = jax.vmap(
            lambda region: layout(region, row_ids, col_ids)
        )(boxes_now)
        own_members = lax.dynamic_index_in_dim(member_pixels, col_index, 0, False)
        own_counts = lax.dynamic_index_in_dim(counts, col_index, 0, False)
        own_valid = lax.dynamic_index_in_dim(validity, col_index, 0, False)
        areas = (boxes_now[:, :, 2] - boxes_now[:, :, 0]) * (
            boxes_now[:, :, 3] - boxes_now[:, :, 1]
        )
        valid_total = jnp.sum(areas.astype(jnp.float32))
        local_x = features[m].reshape(pixels, channels)
        partial_value = jnp.einsum(
            "pb,pd->bd",
            own_members.astype(jnp.bfloat16),
            local_x,
            preferred_element_type=jnp.float32,
        )
        bin_total = lax.psum(partial_value, ("ha", "wa"))
        pooled = (bin_total / own_counts[:, None]).astype(jnp.bfloat16)
        pooled_all = lax.all_gather(pooled[None], "col", axis=0, tiled=True)
        branch_norms = []
        branch_affines = []
        branch_inverse = []
        branch_outs = []
        for level_number in range(4):
            level_pooled = pooled_all[
                :, starts[level_number] : starts[level_number] + spans[level_number]
            ]
            pre = jnp.einsum(
                "cbd,de->cbe",
                level_pooled,
                branch_weight[level_number],
                preferred_element_type=jnp.float32,
            )
            average = jnp.mean(pre, (0, 1))
            spread = jnp.mean(pre * pre, (0, 1)) - average * average
            inverse = lax.rsqrt(spread + EPSILON)
            normed_branch = (pre - average) * inverse
            affine_branch = branch_gain[level_number] * normed_branch + branch_bias[level_number]
            branch_norms.append(normed_branch)
            branch_affines.append(affine_branch)
            branch_inverse.append(inverse)
            branch_outs.append(jax.nn.silu(affine_branch))
        branch_local = jnp.concatenate(branch_outs, 1).astype(jnp.bfloat16)
        branch_full = lax.all_gather(branch_local, "col", axis=2, tiled=True)
        enlarged_map = []
        for level_number in range(4):
            level_output = branch_full[
                :, starts[level_number] : starts[level_number] + spans[level_number]
            ].astype(jnp.float32)
            spread_out = jnp.einsum(
                "zdw,zwk->zdk",
                weight_per_level[level_number],
                level_output,
                precision=FULL_ACCURACY,
            )
            enlarged_map.append(
                spread_out.reshape(groups, tile_rows, tile_cols, width_out).astype(jnp.bfloat16)
            )
        x_all = lax.all_gather(features[m][None], "col", axis=0, tiled=True)
        masked_x = x_all * validity.reshape(groups, tile_rows, tile_cols, 1).astype(jnp.bfloat16)
        stacked = jnp.concatenate([masked_x] + enlarged_map, -1)
        padded = extended(stacked, (("ha", 1), ("wa", 2)), 1)
        columns = jnp.concatenate(
            [
                padded[:, row_tap : row_tap + tile_rows, col_tap : col_tap + tile_cols]
                for row_tap in range(3)
                for col_tap in range(3)
            ],
            -1,
        ).reshape(flat_rows, -1)
        convolved = jnp.dot(columns, conv_flat, preferred_element_type=jnp.float32)
        valid_flat = validity.reshape(flat_rows, 1)
        first_sum, second_sum = lax.psum(
            (jnp.sum(convolved * valid_flat, 0), jnp.sum(convolved * convolved * valid_flat, 0)),
            ("ha", "wa"),
        )
        average = first_sum / valid_total
        spread = second_sum / valid_total - average * average
        inverse = lax.rsqrt(spread + EPSILON)
        normed = (convolved - average) * inverse
        affine = norm_gain * normed + norm_bias
        hidden = jax.nn.silu(affine)
        part_logits = jnp.dot(hidden, class_weight, precision=FULL_ACCURACY).reshape(
            groups, tile_rows, tile_cols, -1
        )
        summed = lax.psum_scatter(part_logits, "col", scatter_dimension=0, tiled=True)
        own_valid_tile = own_valid.reshape(tile_rows, tile_cols, 1)
        logit_list.append((summed[0] + class_bias) * own_valid_tile)
        seed = (cotangent[m] * own_valid_tile)[None]
        seed_all = lax.all_gather(seed, "col", axis=0, tiled=True).reshape(flat_rows, -1)
        grad_hidden = jnp.dot(seed_all, class_weight.T, precision=FULL_ACCURACY)
        grad_affine = grad_hidden * silu_slope(affine)
        bias_sum, gain_sum, class_part, bias_part = lax.psum(
            (
                jnp.sum(grad_affine, 0),
                jnp.sum(grad_affine * normed, 0),
                jnp.dot(hidden.T, seed_all, precision=FULL_ACCURACY),
                jnp.sum(seed_all, 0),
            ),
            ("ha", "wa"),
        )
        norm_bias_total = norm_bias_total + bias_sum
        norm_gain_total = norm_gain_total + gain_sum
        class_weight_total = class_weight_total + class_part
        class_bias_total = class_bias_total + bias_part
        grad_conv = (
            valid_flat
            * inverse
            * (
                grad_affine * norm_gain
                - norm_gain * bias_sum / valid_total
                - normed * norm_gain * gain_sum / valid_total
            )
        )
        grad_low = grad_conv.astype(jnp.bfloat16)
        grad_pad = extended(
            grad_low.reshape(groups, tile_rows, tile_cols, share), (("ha", 1), ("wa", 2)), 1
        )
        grad_columns = jnp.concatenate(
            [
                grad_pad[
                    :, 2 - row_tap : 2 - row_tap + tile_rows, 2 - col_tap : 2 - col_tap + tile_cols
                ]
                for row_tap in range(3)
                for col_tap in range(3)
            ],
            -1,
        ).reshape(flat_rows, -1)
        grad_stacked = jnp.dot(grad_columns, conv_back, preferred_element_type=jnp.float32)
        conv_part = jnp.einsum("pk,pe->ke", columns, grad_low, preferred_element_type=jnp.float32)
        conv_total = conv_total + conv_part
        grad_x = grad_stacked[:, :channels]
        bin_parts = []
        for level_number in range(4):
            level_gradient = grad_stacked[
                :, channels + level_number * width_out : channels + (level_number + 1) * width_out
            ].reshape(groups, pixels, width_out)
            bin_parts.append(
                jnp.einsum(
                    "qkl,qko->qlo",
                    weight_per_level[level_number],
                    level_gradient,
                    precision=FULL_ACCURACY,
                )
            )
        bin_local = jnp.concatenate(bin_parts, 1)
        bin_grad = lax.psum(bin_local, ("ha", "wa", "col"))
        own_bin_grad = lax.dynamic_slice_in_dim(bin_grad, col_index * share, share, 2)
        grad_pres = []
        for level_number in range(4):
            grad_out = own_bin_grad[
                :, starts[level_number] : starts[level_number] + spans[level_number]
            ]
            grad_act = grad_out * silu_slope(branch_affines[level_number])
            act_sum = jnp.sum(grad_act, (0, 1))
            act_norm_sum = jnp.sum(grad_act * branch_norms[level_number], (0, 1))
            samples = float(groups * spans[level_number])
            branch_bias_grads[level_number] = branch_bias_grads[level_number] + act_sum
            branch_gain_grads[level_number] = branch_gain_grads[level_number] + act_norm_sum
            grad_pre = branch_inverse[level_number] * (
                branch_gain[level_number] * grad_act
                - branch_gain[level_number] * act_sum / samples
                - branch_norms[level_number] * branch_gain[level_number] * act_norm_sum / samples
            )
            level_pooled = pooled_all[
                :, starts[level_number] : starts[level_number] + spans[level_number]
            ].astype(jnp.float32)
            branch_grads[level_number] = branch_grads[level_number] + jnp.einsum(
                "cbd,cbe->de", level_pooled, grad_pre, precision=FULL_ACCURACY
            )
            grad_pres.append(grad_pre)
        pooled_grads = [
            jnp.einsum(
                "cbe,de->cbd",
                grad_pres[level_number],
                branch_float[level_number],
                precision=FULL_ACCURACY,
            )
            for level_number in range(4)
        ]
        grad_pooled = jnp.concatenate(pooled_grads, 1)
        back_x, back_pooled = (
            lax.psum_scatter(
                grad_x.reshape(groups, pixels, channels).astype(jnp.bfloat16),
                "col",
                scatter_dimension=0,
                tiled=True,
            ).astype(jnp.float32),
            lax.psum_scatter(
                grad_pooled.astype(jnp.bfloat16), "col", scatter_dimension=0, tiled=True
            ).astype(jnp.float32),
        )
        pooled_back = back_pooled[0]
        spread_back = jnp.dot(
            own_members, pooled_back / own_counts[:, None], precision=FULL_ACCURACY
        )
        feature_list.append(
            (back_x[0] * own_valid[:, None] + spread_back).reshape(tile_rows, tile_cols, channels)
        )
    conv_result = lax.psum_scatter(
        conv_total.reshape(9, -1, share), ("ha", "wa"), scatter_dimension=1, tiled=True
    )
    return (
        jnp.stack(logit_list),
        jnp.stack(feature_list),
        jnp.stack(branch_grads),
        jnp.stack(branch_gain_grads),
        jnp.stack(branch_bias_grads),
        conv_result,
        norm_gain_total,
        norm_bias_total,
        class_weight_total,
        class_bias_total,
    )


def solution(mesh):
    placed = (
        P("col", "ha", "wa", None),
        P(),
        P(None, None, "col"),
        P(None, "col"),
        P(None, "col"),
        P(None, None, "col"),
        P("col"),
        P("col"),
        P("col", None),
        P(),
        P("col", "ha", "wa", None),
    )
    return jax.shard_map(
        functools.partial(canvas_body, mesh) if whole_canvas_plan(mesh) else tiled_body,
        mesh=mesh,
        in_specs=placed,
        out_specs=(
            P("col", "ha", "wa", None),
            P("col", "ha", "wa", None),
            P(None, None, "col"),
            P(None, "col"),
            P(None, "col"),
            P(None, ("ha", "wa"), "col"),
            P("col"),
            P("col"),
            P("col", None),
            P(),
        ),
        check_vma=False,
    )
```

```python
import functools

import jax
import jax.numpy as jnp
import numpy as np
from jax import lax
from jax.experimental import pallas as pl
from jax.experimental.pallas import tpu as pltpu
from jax.sharding import PartitionSpec as P

EPSILON = 1e-05
LEVELS = (1, 2, 3, 6)
FULL_ACCURACY = lax.Precision.HIGHEST
MESH = pl.DeviceIdType.MESH


SPANS = (16, 16, 32, 112)
STARTS = (0, 16, 32, 64)
BINS = 176
WIDE = 112
TAPS = 9


def whole_canvas_plan(mesh):
    return mesh.shape["ha"] == 4 and mesh.shape["wa"] == 2 and mesh.shape["col"] == 4


def bin_tables():
    lanes = np.zeros((4, 8, 128), np.float32)
    rows = np.zeros((BINS, 8), np.float32)
    rows[:, 3] = 1.0
    for level, n in enumerate(LEVELS):
        lanes[level, 3, :] = n - 1
        for k in range(3):
            for i in range(n):
                for j in range(n):
                    b = (k * n + i) * n + j
                    lanes[level, :3, b] = (k, i, j)
                    lanes[level, 4, b] = 1.0
                    row = STARTS[level] + b
                    for at, value in enumerate((k, i, j, n, 1.0)):
                        rows[row, at] = value
    return lanes, rows


def dot(a, b, dims=((1,), (0,)), precision=None):
    return lax.dot_general(a, b, (dims, ((), ())), precision=precision, preferred_element_type=jnp.float32)


ROWS_T = ((0,), (0,))
BOTH_LAST = ((1,), (1,))


def halves(value):
    high = value.astype(jnp.bfloat16)
    return high, (value - high.astype(jnp.float32)).astype(jnp.bfloat16)


def pick3(index, values):
    return jnp.where(index == 0.0, values[0], jnp.where(index == 1.0, values[1], values[2]))


class Sems:
    def __init__(self):
        self.count = 0

    def take(self, n=1):
        at = self.count
        self.count += n
        return at


def head_kernel(
    boxes, lane_table, row_table, feat, cot, wconv, wbranch, bgain, bbias, ngain, nbias, cw_in, cb,
    logits_out, fgrad_out, bgrad_out, small_out, cgrad_out,
    x, lv, wall, wb2, u2, ut, mt, cnt, po, pre, prr, bos, bor, bo2, val, yp, p, cr, gc, g9, gp3, tb,
    dxf, sbu, sbd, rxu, rxd, gb, grr, gpre, gpa, gpx, gps, gpr, dw, dwr, bg, bgr, bgh, seed_in, sd, lt, ltr, lts,
    st, str_, small, smr, nb_s, af_s, cn_s, bga, fg, fgh, cwt, seeds, square, dwh, dwx, bi_s, sems, turn,
):
    f32, bf16 = jnp.float32, jnp.bfloat16
    q, w, z = lax.axis_index("ha"), lax.axis_index("wa"), lax.axis_index("col")
    xq, yq = lax.rem(q, 2), lax.div(q, 2)
    g = 2 * xq + yq
    classes = cb.shape[1]
    zm = lax.div(z, 2)
    zz = z * (1 - zm) + (3 - z) * zm
    names = Sems()
    finals = []
    due = {}

    def arrive(name):
        due.pop(name)()

    def each(copies, method):
        def run():
            for c in copies:
                getattr(c, method)()

        return run


    def peer(kx, ky, kw):
        px = xq + kx - 2 * kx * xq
        py = yq + ky - 2 * ky * yq
        return {"ha": 2 * py + px, "wa": w + kw - 2 * kw * w}, 2 * px + py

    def copy(src, dst, ss, rs, dev):
        return pltpu.make_async_remote_copy(
            src_ref=src, dst_ref=dst, send_sem=sems.at[ss], recv_sem=sems.at[rs], device_id=dev, device_id_type=MESH
        )

    def zpeer(j):
        return {"col": lax.rem(z + j, 4)}

    plane = [(kx, ky, kw) for kw in (0, 1) for ky in (0, 1) for kx in (0, 1) if kx + ky + kw]
    chips = [(1, 0), (0, 1), (1, 1)]

    barrier = pltpu.get_barrier_semaphore()
    for kx, ky, kw in plane:
        pl.semaphore_signal(barrier, 1, device_id=peer(kx, ky, kw)[0], device_id_type=MESH)
    for j in (1, 2, 3):
        pl.semaphore_signal(barrier, 1, device_id=zpeer(j), device_id_type=MESH)

    g512 = pl.multiple_of(g * 512, 512)
    weight_copies = []
    for t in range(TAPS):
        for part in range(2):
            s = names.take()
            weight_copies.append(
                pltpu.make_async_copy(
                    wconv.at[t, pl.ds(2048 * part + g512, 512), :],
                    wall.at[pl.ds(512 * part, 512), pl.ds(128 * t, 128)],
                    sems.at[s],
                )
            )
    for twice in range(2):
        s = names.take()
        weight_copies.append(
            pltpu.make_async_copy(
                wbranch.at[:, pl.ds(g512, 512), :], wb2.at[:, :, pl.ds(128 * twice, 128)], sems.at[s]
            )
        )
    for c in weight_copies:
        c.start()
    due["weights"] = each(weight_copies, "wait")

    for half in range(2):
        bo2[:, 128 * half + WIDE:128 * half + 128, :] = jnp.zeros((4, 128 - WIDE, 512), bf16)
    yp[:, 0:8, :] = jnp.zeros((2, 8, 1152), f32)
    yp[:, 264:272, :] = jnp.zeros((2, 8, 1152), f32)
    gp3[:, :, 0:8, :] = jnp.zeros((3, 2, 8, 128), f32)
    gp3[:, :, 264:272, :] = jnp.zeros((3, 2, 8, 128), f32)
    small[...] = jnp.zeros(small.shape, f32)
    st[...] = jnp.zeros(st.shape, f32)
    p[...] = jnp.zeros(p.shape, f32)
    nb_s[...] = jnp.zeros(nb_s.shape, f32)
    gpre[...] = jnp.zeros(gpre.shape, f32)
    cwt[...] = jnp.zeros(cwt.shape, f32)
    cwt[0:classes, :] = cw_in[...]
    pl.semaphore_wait(barrier, 10)

    q64 = pl.multiple_of(64 * q, 64)
    a_send, a_recv = names.take(8), names.take(8)
    own_row = pl.multiple_of(256 * w + 64 * q, 64)
    own = pltpu.make_async_copy(feat.at[w, :, pl.ds(g512, 512)], x.at[z, pl.ds(own_row, 64), :], sems.at[a_send])

    def tile_copy(t, kx, ky):
        n = 4 * (t + w - 2 * t * w) + 2 * ky + kx
        dev, block = peer(kx, ky, 0)
        return copy(
            feat.at[t, :, pl.ds(pl.multiple_of(512 * block, 512), 512)], x.at[z, pl.ds(own_row, 64), :],
            a_send + n, a_recv + n, {"ha": dev["ha"], "wa": t},
        )

    def tiles(t, method):
        for kx, ky in chips:
            getattr(tile_copy(t, kx, ky), method)()
        pl.when(w != t)(lambda: getattr(tile_copy(t, 0, 0), method)())

    def tiles_wait():
        for n, (kx, ky, kw) in enumerate(plane):
            at = 4 * kw + 2 * ky + kx
            copy(
                feat.at[0, :, pl.ds(0, 512)], x.at[z, pl.ds(own_row, 64), :], a_send + at, a_recv + at, peer(kx, ky, kw)[0]
            ).wait_recv()

    own.start()
    tiles(0, "start")

    def scalars(canvas, micro=None):
        index = 2 * canvas + (w if micro is None else micro)
        return [[boxes[k, e, index] for k in range(3)] for e in range(4)]

    def px(rows, lanes, axis, start=0):
        at = lax.broadcasted_iota(jnp.int32, (rows, lanes), axis) + start
        half = at // 256
        return (at // 8 % 32).astype(f32), (half * 8 + at % 8).astype(f32)

    def tile_valid(micro):
        at = lax.broadcasted_iota(jnp.int32, (64, 128), 0)
        y, xx = (8 * q + at // 8).astype(f32), (8 * w + at % 8).astype(f32)
        top, left, bottom, right = [[v.astype(f32) for v in values] for values in scalars(z, micro)]
        ok = jnp.zeros((64, 128), f32)
        for k in range(3):
            ok = jnp.where((y >= top[k]) & (y < bottom[k]) & (xx >= left[k]) & (xx < right[k]), 1.0, ok)
        return ok

    def layout(c):
        top, left, bottom, right = [[v.astype(f32) for v in values] for values in scalars(c)]
        y, xx = px(512, 128, 0)
        ok = jnp.zeros((512, 128), f32)
        for k in range(3):
            ok = jnp.where((y >= top[k]) & (y < bottom[k]) & (xx >= left[k]) & (xx < right[k]), 1.0, ok)
        val[c] = ok
        table = lane_table[g]
        box, bi, bj, n1, real = [table[e:e + 1] for e in range(5)]
        t_, l_, b_, r_ = [pick3(box, v) for v in (top, left, bottom, right)]
        h1, w1 = b_ - t_ - 1.0, r_ - l_ - 1.0
        rw = jnp.maximum(1.0 - jnp.abs((y - t_) * n1 - bi * h1) / h1, 0.0)
        cw = jnp.maximum(1.0 - jnp.abs((xx - l_) * n1 - bj * w1) / w1, 0.0)
        inside = (y >= t_) & (y < b_) & (xx >= l_) & (xx < r_) & (real > 0.0)
        weights = jnp.where(inside, rw * cw, 0.0)
        high, low = halves(weights)
        u2[c, :, 0:128] = high
        u2[c, :, 128:256] = low
        high, low = halves(weights.T)
        ut[c, 0:128, :] = high
        ut[c, 128:256, :] = low
        box, bi, bj, n, real = [jnp.broadcast_to(row_table[:, e:e + 1], (BINS, 128)) for e in range(5)]
        t_, l_, b_, r_ = [pick3(box, v) for v in (top, left, bottom, right)]
        h, wd = b_ - t_, r_ - l_
        row_low = jnp.floor((bi * h + 0.5) / n)
        row_high = jnp.floor(((bi + 1.0) * h + n - 0.5) / n)
        col_low = jnp.floor((bj * wd + 0.5) / n)
        col_high = jnp.floor(((bj + 1.0) * wd + n - 0.5) / n)
        cnt[c] = jnp.where(real > 0.0, (row_high - row_low) * (col_high - col_low), 1.0)
        for chunk in range(4):
            y, xx = px(BINS, 128, 1, 128 * chunk)
            u, v = y - t_, xx - l_
            member = (u >= row_low) & (u < row_high) & (v >= col_low) & (v < col_high) & (real > 0.0)
            mt[c, :, 128 * chunk:128 * chunk + 128] = jnp.where(member, 1.0, 0.0).astype(bf16)

    def combine():
        out = []
        zs = []
        for b in range(3):
            acc = [None, None]
            for h in range(2):
                for a in range(3):
                    t = 3 * a + b
                    piece = yp[h, 8 * a:8 * a + 256, 128 * t:128 * t + 128]
                    acc[h] = piece if acc[h] is None else acc[h] + piece
            zs.append(acc)
        col = lax.broadcasted_iota(jnp.int32, (256, 128), 0) % 8
        first, last = col == 0, col == 7
        out0 = zs[1][0] + jnp.where(first, 0.0, pltpu.roll(zs[0][0], 1, 0))
        out0 = out0 + jnp.where(last, pltpu.roll(zs[2][1], 7, 0), pltpu.roll(zs[2][0], 255, 0))
        out1 = zs[1][1] + jnp.where(first, pltpu.roll(zs[0][0], 249, 0), pltpu.roll(zs[0][1], 1, 0))
        out1 = out1 + jnp.where(last, 0.0, pltpu.roll(zs[2][1], 255, 0))
        return out0, out1

    def conv_part(operand, part):
        for h in range(2):
            yp[h, 8:264, :] = dot(operand[256 * h:256 * h + 256], wall[512 * part:512 * part + 512, :])
        return combine()

    e_send, e_recv = names.take(16), names.take(12)

    def pre_copy(level, c, kx, ky):
        slot = kx + 2 * ky - 1
        return copy(
            pre.at[c, pl.ds(STARTS[level], SPANS[level]), :],
            prr.at[slot, c, pl.ds(0, SPANS[level]), :],
            e_send + 4 * level + c, e_recv + 4 * slot + c, peer(kx, ky, 0)[0],
        )

    def to_level_owner(level, action):
        lx, ly = level // 2, level % 2
        for kx, ky in chips:
            wanted = (xq + kx - 2 * kx * xq == lx) & (yq + ky - 2 * ky * yq == ly)
            pl.when(wanted)(functools.partial(action, kx, ky))

    def pool(c):
        total = dot(mt[c], x[c])
        for chunk in range(4):
            cols = slice(128 * chunk, 128 * chunk + 128)
            po[c, :, cols] = (total[:, cols] / cnt[c]).astype(bf16)

    def branch_products(c):
        for level in range(4):
            rows = slice(STARTS[level], STARTS[level] + SPANS[level])
            pre[c, rows, :] = dot(po[c, rows, :], wb2[level, :, 0:128])
        for level in range(4):
            to_level_owner(level, lambda kx, ky, level=level: pre_copy(level, c, kx, ky).start())

    def conv_add(c, operand, part):
        out0, out1 = conv_part(operand, part)
        p[c, 0] = p[c, 0] + out0
        p[c, 1] = p[c, 1] + out1

    layout(z)
    for copy_out in (tiles,):
        copy_out(0, "wait_send")
        copy_out(1, "start")
    due["A"] = tiles_wait
    due["A own"] = own.wait
    finals.append(lambda: tiles(1, "wait_send"))

    w64 = pl.multiple_of(64 * w, 64)
    square[...] = jnp.zeros(square.shape, f32)
    for micro in range(2):
        square[pl.ds(w64, 64), 0:classes] = cot[micro] * tile_valid(micro)[:, 0:classes]
        seeds[micro] = square[...].T[0:24]
    sc_send, sc_recv = names.take(), names.take()
    seed_copy = copy(seeds.at[1 - w], seed_in.at[0], sc_send, sc_recv, peer(0, 0, 1)[0])
    seed_copy.start()
    due["seed"] = seed_copy.wait_recv
    finals.append(seed_copy.wait_send)

    arrive("weights")
    arrive("A")
    arrive("A own")
    ok = val[z]
    for chunk in range(4):
        cols = slice(128 * chunk, 128 * chunk + 128)
        x[z, :, cols] = (x[z, :, cols].astype(f32) * ok).astype(bf16)

    up_send, up_recv, dn_send, dn_recv = names.take(6), names.take(6), names.take(6), names.take(6)

    def half_of(c, h):
        return x.at[c, pl.ds(256 * h, 256), :]

    def up_copy(k, h):
        part = half_of(z - k, h)
        return copy(part, part, up_send + 2 * k + h, up_recv + 2 * k + h, {"col": z + 1})

    def dn_copy(k, h):
        part = half_of(z + k, h)
        return copy(part, part, dn_send + 2 * k + h, dn_recv + 2 * k + h, {"col": z - 1})

    def take_in(k, h):
        n = 2 * (k - 1) + h

        @pl.when(z >= k)
        def _():
            part = half_of(z - k, h)
            copy(part, part, up_send + n, up_recv + n, {"col": z}).wait_recv()

        @pl.when(z + k <= 3)
        def _():
            part = half_of(z + k, h)
            copy(part, part, dn_send + n, dn_recv + n, {"col": z}).wait_recv()

    other = peer(0, 0, 1)[0]

    def up_last(k):
        return (w == 0) & (z < 3) & (z == k)

    def dn_last(k):
        return (w == 0) & (z > 0) & (3 - z == k)

    def pass_on(k, h):
        pl.when((z >= k) & (z < 3))(lambda: up_copy(k, h).start())
        pl.when((z + k <= 3) & (z > 0))(lambda: dn_copy(k, h).start())
        if k == 2 and h == 1:
            give_turn(k)

    def passed_on():
        for k in range(3):
            for h in range(2):
                up_done, dn_done = (z >= k) & (z < 3), (z + k <= 3) & (z > 0)
                if h == 0 and k < 2:
                    up_done = up_done & jnp.logical_not(up_last(k))
                    dn_done = dn_done & jnp.logical_not(dn_last(k))
                pl.when(up_done)(lambda: up_copy(k, h).wait_send())
                pl.when(dn_done)(lambda: dn_copy(k, h).wait_send())

    finals.append(passed_on)

    def give_turn(k):
        @pl.when(up_last(k))
        def _():
            if k < 2:
                up_copy(k, 0).wait_send()
            pl.semaphore_signal(turn.at[0], 1, device_id=other, device_id_type=MESH)

        @pl.when(dn_last(k))
        def _():
            if k < 2:
                dn_copy(k, 0).wait_send()
            pl.semaphore_signal(turn.at[1], 1, device_id=other, device_id_type=MESH)

    def own_turn(up):
        def start():
            pl.semaphore_wait(turn.at[0 if up else 1], 1)
            for h in range(2):
                (up_copy(0, h) if up else dn_copy(0, h)).start()

        pl.when((z < 3) if up else (z > 0))(start)

    @pl.when(w == 0)
    def _():
        pass_on(0, 0)
        pass_on(0, 1)

    arrive("seed")
    sd[z] = seeds[w] + seed_in[0]
    sz_send, sz_recv = names.take(3), names.take(3)
    sd_copies = [copy(sd.at[z], sd.at[z], sz_send + j - 1, sz_recv + j - 1, zpeer(j)) for j in (1, 2, 3)]
    each(sd_copies, "start")()
    finals.append(each(sd_copies, "wait_send"))

    def sd_wait():
        for j in (1, 2, 3):
            src = lax.rem(z + 4 - j, 4)
            copy(sd.at[src], sd.at[src], sz_send + j - 1, sz_recv + j - 1, zpeer(j)).wait_recv()

    due["sd"] = sd_wait

    pool(z)
    branch_products(z)
    conv_add(z, x[z], 0)

    def rest(i, carry):
        layout(lax.rem(z + i, 4))
        return carry

    lax.fori_loop(1, 4, rest, 0)

    def pre_wait():
        for c in range(4):
            for kx, ky in chips:
                slot = kx + 2 * ky - 1
                for level in range(4):

                    @pl.when(g == level)
                    def _():
                        copy(
                            pre.at[c, pl.ds(STARTS[level], SPANS[level]), :],
                            prr.at[slot, c, pl.ds(0, SPANS[level]), :],
                            e_send, e_recv + 4 * slot + c, peer(0, 0, 1)[0],
                        ).wait_recv()

    def pre_sent():
        for level in range(4):
            for c in range(4):
                to_level_owner(level, lambda kx, ky: pre_copy(level, c, kx, ky).wait_send())

    finals.append(pre_sent)
    level_n = jnp.where(g == 0, 1.0, jnp.where(g == 1, 2.0, jnp.where(g == 2, 3.0, 6.0)))
    samples = 12.0 * level_n * level_n

    def rows_of(value):
        return value.reshape(4 * WIDE, 128)

    def branch_norm():
        pre_wait()
        for level in range(4):

            @pl.when(g == level)
            def _():
                span = SPANS[level]
                for c in range(4):
                    total = pre[c, STARTS[level]:STARTS[level] + span, :]
                    for slot in range(3):
                        total = total + prr[slot, c, 0:span, :]
                    nb_s[c, 0:span, :] = total

        pre_all = rows_of(nb_s[...])
        average = jnp.sum(pre_all, 0, keepdims=True) / samples
        spread = jnp.sum(pre_all * pre_all, 0, keepdims=True) / samples - average * average
        b_inverse = lax.rsqrt(spread + EPSILON)
        b_norm = (pre_all - average) * b_inverse
        b_act = b_gain * b_norm + bbias[pl.ds(g, 1), :]
        nb_s[...] = b_norm.reshape(4, WIDE, 128)
        bi_s[0:1, :] = b_inverse
        logistic = jax.nn.sigmoid(b_act)
        af_s[...] = (logistic * (1.0 + b_act * (1.0 - logistic))).reshape(4, WIDE, 128)
        bos[...] = (b_act * logistic).astype(bf16).reshape(4, WIDE, 128)
        each(bo_copies, "start")()
        bor[z] = bos[...]

    b_gain = bgain[pl.ds(g, 1), :]
    f_send, f_recv = names.take(3), names.take(3)
    bo_copies = [copy(bos, bor.at[z], f_send + j - 1, f_recv + j - 1, zpeer(j)) for j in (1, 2, 3)]
    finals.append(each(bo_copies, "wait_send"))

    i_send, i_recv = names.take(12), names.take(12)

    def chip_rows(at):
        return pl.ds(pl.multiple_of(64 * at, 64), 64)

    def conv_copy(c, kx, ky):
        slot = kx + 2 * ky - 1
        dev, _ = peer(kx, ky, 0)
        return copy(p.at[c, :, chip_rows(dev["ha"]), :], cr.at[slot, c], i_send + 4 * slot + c, i_recv + 4 * slot + c, dev)

    def conv_send(c):
        for kx, ky in chips:
            conv_copy(c, kx, ky).start()

    def levels():
        each(bo_copies, "wait_recv")()
        for part in range(4):
            for half in range(2):
                bo2[:, 128 * half:128 * half + WIDE, 128 * part:128 * part + 128] = bor[part]

        def level_conv(c, carry):
            lv[c] = dot(u2[c], bo2[c]).astype(bf16)
            conv_add(c, lv[c], 1)
            conv_send(c)
            return carry

        lax.fori_loop(0, 4, level_conv, 0)

    @pl.when((w == 1) & (zm == 0))
    def _():
        own_turn(True)
        own_turn(False)

    @pl.when((w == 1) & (zm == 1))
    def _():
        own_turn(False)
        own_turn(True)

    def arrived(c):
        pool(c)
        branch_products(c)

    for k in (1, 2, 3):
        if k < 3:
            give_turn(k - 1)
        for h in range(2):
            take_in(k, h)
            if k < 3:
                pass_on(k, h)
        pl.when(z >= k)(lambda: arrived(z - k))
        pl.when(z + k <= 3)(lambda: arrived(z + k))

    branch_norm()

    def late(j, carry):
        c = lax.rem(z + j, 4)
        conv_add(c, x[c], 0)
        return carry

    lax.fori_loop(1, 4, late, 0)
    levels()

    conv_copies = [conv_copy(c, kx, ky) for c in range(4) for kx, ky in chips]
    due["conv"] = each(conv_copies, "wait_recv")
    finals.append(each(conv_copies, "wait_send"))

    arrive("sd")
    for c in range(4):
        cn_s[0, 128 * c:128 * c + 128, :] = dot(sd[c], cwt[...], ROWS_T, FULL_ACCURACY)

    arrive("conv")
    convolved = (p[:, :, pl.ds(q64, 64), :] + cr[0] + cr[1] + cr[2]).reshape(512, 128)
    ok = val.at[...].reshape(4, 2, 256, 128)[:, :, pl.ds(q64, 64), :].reshape(512, 128)

    j_send, j_recv = names.take(6), names.take(6)

    def stat_copy(stage, kx, ky):
        slot = kx + 2 * ky - 1
        return copy(
            st.at[stage], str_.at[stage, slot], j_send + 3 * stage + slot, j_recv + 3 * stage + slot, peer(kx, ky, 0)[0]
        )

    def plane_sum(stage, first, second):
        st[stage, 0:1, :] = first
        st[stage, 1:2, :] = second
        copies = [stat_copy(stage, kx, ky) for kx, ky in chips]
        each(copies, "start")()
        each(copies, "wait_recv")()
        finals.append(each(copies, "wait_send"))
        total = st[stage] + str_[stage, 0] + str_[stage, 1] + str_[stage, 2]
        return total[0:1], total[1:2]

    masked = convolved * ok
    first, second = plane_sum(0, jnp.sum(masked, 0, keepdims=True), jnp.sum(convolved * masked, 0, keepdims=True))
    area = jnp.int32(0)
    for c in range(4):
        top, left, bottom, right = scalars(c)
        for k in range(3):
            area = area + (bottom[k] - top[k]) * (right[k] - left[k])
    valid_total = area.astype(f32)
    average = first / valid_total
    spread = second / valid_total - average * average
    inverse = lax.rsqrt(spread + EPSILON)
    normed = (convolved - average) * inverse
    gain = ngain[...]
    affine = gain * normed + nbias[...]
    logistic = jax.nn.sigmoid(affine)
    hidden = affine * logistic
    grad_affine = cn_s[0] * (logistic * (1.0 + affine * (1.0 - logistic)))
    part_bias = jnp.sum(grad_affine, 0, keepdims=True)
    part_gain = jnp.sum(grad_affine * normed, 0, keepdims=True)
    cn_s[1] = hidden
    small[48:49, :] = part_bias
    small[49:50, :] = part_gain
    bias_sum, gain_sum = plane_sum(1, part_bias, part_gain)
    grad_conv = ok * inverse * (
        grad_affine * gain - gain * bias_sum / valid_total - normed * gain * gain_sum / valid_total
    )
    gc[:, :, pl.ds(q64, 64), :] = grad_conv.astype(bf16).reshape(4, 2, 64, 128)
    k_send, k_recv = names.take(3), names.take(3)

    def gc_copy(kx, ky, at):
        slot = kx + 2 * ky - 1
        block = gc.at[:, :, chip_rows(at), :]
        return copy(block, block, k_send + slot, k_recv + slot, peer(kx, ky, 0)[0])

    gc_copies = [gc_copy(kx, ky, q) for kx, ky in chips]
    each(gc_copies, "start")()
    due["gc"] = each(gc_copies, "wait_recv")
    finals.append(each(gc_copies, "wait_send"))

    arrive("gc")

    def shifted(c):
        col = lax.broadcasted_iota(jnp.int32, (256, 128), 0) % 8
        first, last = col == 0, col == 7
        g0, g1 = gc[c, 0].astype(f32), gc[c, 1].astype(f32)
        gp3[1, 0, 8:264, :] = g0
        gp3[1, 1, 8:264, :] = g1
        gp3[0, 0, 8:264, :] = jnp.where(last, pltpu.roll(g1, 7, 0), pltpu.roll(g0, 255, 0))
        gp3[0, 1, 8:264, :] = jnp.where(last, 0.0, pltpu.roll(g1, 255, 0))
        gp3[2, 0, 8:264, :] = jnp.where(first, 0.0, pltpu.roll(g0, 1, 0))
        gp3[2, 1, 8:264, :] = jnp.where(first, pltpu.roll(g0, 249, 0), pltpu.roll(g1, 1, 0))
        for a in range(3):
            for b in range(3):
                t = 3 * a + b
                for h in range(2):
                    start = 8 * (2 - a)
                    g9[c, 256 * h:256 * h + 256, 128 * t:128 * t + 128] = gp3[b, h, start:start + 256, :].astype(bf16)

    def level_rows(c, carry):
        shifted(c)
        both = dot(ut[c], g9[c])
        high, low = halves(both[0:128] + both[128:256])
        tb[c, 0:128, :] = high
        tb[c, 128:256, :] = low
        return carry

    def data_grad(c):
        for h in range(2):
            dxf[c, 256 * h:256 * h + 256, :] = dot(g9[c, 256 * h:256 * h + 256, :], wall[0:512, :], BOTH_LAST)

    ru_send, ru_recv, rd_send, rd_recv = names.take(3), names.take(3), names.take(3), names.take(3)

    def ru_copy(k):
        return copy(sbu.at[k], rxu.at[k], ru_send + k, ru_recv + k, {"col": z + 1})

    def rd_copy(k):
        return copy(sbd.at[k], rxd.at[k], rd_send + k, rd_recv + k, {"col": z - 1})

    def up_on(k):
        return (z + 3 - k <= 3) & (z < 3)

    def dn_on(k):
        return (z - 3 + k >= 0) & (z > 0)

    def end_send(k):
        @pl.when(z == 0)
        def _():
            sbu[k] = dxf[3 - k].astype(bf16)
            ru_copy(k).start()

        @pl.when(z == 3)
        def _():
            sbd[k] = dxf[k].astype(bf16)
            rd_copy(k).start()

    def middle_send(k):
        @pl.when(up_on(k) & (z > 0))
        def _():
            ru_copy(k - 1).wait_recv()
            sbu[k] = (dxf[z + 3 - k] + rxu[k - 1].astype(f32)).astype(bf16)
            ru_copy(k).start()

        @pl.when(dn_on(k) & (z < 3))
        def _():
            rd_copy(k - 1).wait_recv()
            sbd[k] = (dxf[z - 3 + k] + rxd[k - 1].astype(f32)).astype(bf16)
            rd_copy(k).start()

    def scatter_sent():
        for k in range(3):
            pl.when(up_on(k))(lambda: ru_copy(k).wait_send())
            pl.when(dn_on(k))(lambda: rd_copy(k).wait_send())

    def canvas_at(i):
        low = (3 - i) if i < 2 else zz * (i - 2) + (1 - zz) * (3 - i)
        return (1 - zm) * low + zm * (3 - low)

    n_send, n_recv = names.take(3), names.take(3)

    def gb_copies(method):
        for level in range(4):

            @pl.when(g == level)
            def _():
                for j in (1, 2, 3):
                    item = copy(
                        gb.at[lax.rem(z + j, 4), :, pl.ds(0, SPANS[level]), :],
                        grr.at[j - 1, :, pl.ds(0, SPANS[level]), :],
                        n_send + j - 1, n_recv + j - 1, zpeer(j),
                    )
                    getattr(item, method)()

    lax.fori_loop(0, 4, level_rows, 0)

    def level_pair(n, carry):
        both = dot(tb[pl.ds(2 * n, 2)].reshape(512, 1152), wall[512:1024, :], BOTH_LAST)
        for c in range(2):
            total = both[256 * c:256 * c + WIDE] + both[256 * c + 128:256 * c + 128 + WIDE]
            for part in range(4):
                gb[part, 2 * n + c] = total[:, 128 * part:128 * part + 128].astype(bf16)
        return carry

    lax.fori_loop(0, 2, level_pair, 0)
    gb_copies("start")
    due["gb"] = lambda: gb_copies("wait_recv")
    finals.append(lambda: gb_copies("wait_send"))

    def weight_grad(part, slot):

        for tile in range(2):
            cols = slice(256 * tile, 256 * tile + 256)

            def of(operand):
                total = None
                for c in range(4):
                    piece = dot(operand[c, :, cols], g9[c], ROWS_T)
                    total = piece if total is None else total + piece
                dw[slot, cols, :] = total

            pl.when(part == 0)(lambda: of(x))
            pl.when(part == 1)(lambda: of(lv))

    w_send, w_recv = names.take(), names.take()
    dw_copy = copy(dw.at[0], dwr, w_send, w_recv, other)
    y_send, y_recv = names.take(), names.take()
    dw_y = copy(dwh, dwx, y_send, y_recv, {"ha": peer(0, 1, 0)[0]["ha"], "wa": yq})
    b_send, b_recv = names.take(), names.take()
    dw_back = copy(dw.at[1], dwr, b_send, b_recv, other)
    cg_sem = names.take()

    def cg_out(src):
        return pltpu.make_async_copy(src, cgrad_out, sems.at[cg_sem])

    weight_grad(1 - yq, w)
    pl.when(w == 0)(lambda: dw_copy.start())

    @pl.when(w == 1)
    def _():
        dw_copy.wait_recv()
        dwh[...] = (dw[1] + dwr[...]).astype(bf16)
        dw_y.start()

    for i in range(4):
        data_grad(canvas_at(i))
        if i < 3:
            end_send(i)

    arrive("gb")
    for level in range(4):

        @pl.when(g == level)
        def _():
            span = SPANS[level]
            total = gb[z, :, 0:span, :].astype(f32)
            for j in range(3):
                total = total + grr[j, :, 0:span, :].astype(f32)
            gpre[:, 0:span, :] = total

    grad_act = rows_of(gpre[...]) * rows_of(af_s[...])
    b_norm = rows_of(nb_s[...])
    act_sum = jnp.sum(grad_act, 0, keepdims=True)
    act_norm_sum = jnp.sum(grad_act * b_norm, 0, keepdims=True)
    small[50:51, :] = act_norm_sum
    small[51:52, :] = act_sum
    grad_pre = bi_s[0:1, :] * (
        b_gain * grad_act - b_gain * act_sum / samples - b_norm * b_gain * act_norm_sum / samples
    )
    gpre[...] = grad_pre.reshape(4, WIDE, 128)
    o_send, o_recv = names.take(3), names.take(12)

    def gpre_copies(method):
        for level in range(4):

            @pl.when(g == level)
            def _():
                rows = pl.ds(STARTS[level], SPANS[level])
                for kx, ky in chips:
                    slot = kx + 2 * ky - 1
                    c = copy(
                        gpre.at[:, pl.ds(0, SPANS[level]), :], gpa.at[:, rows, :],
                        o_send + slot, o_recv + 3 * level + slot, peer(kx, ky, 0)[0],
                    )
                    getattr(c, method)()

    def gpre_wait():
        for level in range(4):

            def wait(kx, ky):
                slot = kx + 2 * ky - 1
                copy(
                    gpre.at[:, pl.ds(0, SPANS[level]), :],
                    gpa.at[:, pl.ds(STARTS[level], SPANS[level]), :],
                    o_send + slot, o_recv + 3 * level + slot, peer(kx, ky, 0)[0],
                ).wait_recv()

            to_level_owner(level, wait)

    gpre_copies("start")
    for level in range(4):

        @pl.when(g == level)
        def _():
            gpa[:, STARTS[level]:STARTS[level] + SPANS[level], :] = gpre[:, 0:SPANS[level], :]

    due["gpre"] = gpre_wait
    finals.append(lambda: gpre_copies("wait_send"))

    middle_send(1)

    lt_send, lt_recv = names.take(3), names.take(3)
    weight_part = jnp.zeros((24, 128), f32)
    bias_part = jnp.zeros((24, 1), f32)
    for c in range(4):
        hidden_c = cn_s[1, 128 * c:128 * c + 128, :]
        lt[c] = dot(cwt[...], hidden_c, BOTH_LAST, FULL_ACCURACY)
        weight_part = weight_part + dot(sd[c], hidden_c, precision=FULL_ACCURACY)
        bias_part = bias_part + jnp.sum(sd[c], 1, keepdims=True)
    small[0:24, :] = weight_part
    small[24:48, :] = jnp.broadcast_to(bias_part, (24, 128))
    lt_copies = [
        copy(lt.at[lax.rem(z + j, 4)], ltr.at[j - 1], lt_send + j - 1, lt_recv + j - 1, zpeer(j)) for j in (1, 2, 3)
    ]
    each(lt_copies, "start")()
    due["lt"] = each(lt_copies, "wait_recv")
    finals.append(each(lt_copies, "wait_send"))

    arrive("gpre")

    def split_rows(c, carry):
        high, low = halves(gpa[c])
        gpx[c, :, 0:128] = high
        gpx[c, :, 128:256] = low
        return carry

    lax.fori_loop(0, 4, split_rows, 0)

    def pooled_grad(c, carry):
        for level in range(4):
            rows = slice(STARTS[level], STARTS[level] + SPANS[level])
            gps[c, rows, :] = dot(gpx[c, rows, :], wb2[level], BOTH_LAST).astype(bf16)
        return carry

    lax.fori_loop(0, 4, pooled_grad, 0)
    p_send, p_recv = names.take(3), names.take(3)
    gp_copies = [
        copy(gps.at[lax.rem(z + j, 4)], gpr.at[j - 1], p_send + j - 1, p_recv + j - 1, zpeer(j)) for j in (1, 2, 3)
    ]
    each(gp_copies, "start")()
    due["gp"] = each(gp_copies, "wait_recv")
    finals.append(each(gp_copies, "wait_send"))

    for level in range(4):
        rows = slice(STARTS[level], STARTS[level] + SPANS[level])
        total = None
        for c in range(4):
            piece = dot(po[c, rows, :], gpx[c, rows, :], ROWS_T)
            total = piece if total is None else total + piece
        bg[level] = total[:, 0:128] + total[:, 128:256]
    bc_send, bc_recv = names.take(), names.take()
    w256 = pl.multiple_of(256 * w, 256)
    v256 = pl.multiple_of(256 * (1 - w), 256)
    bg_copy = copy(bg.at[:, pl.ds(v256, 256), :], bgr, bc_send, bc_recv, peer(0, 0, 1)[0])
    bg_copy.start()
    due["bgc"] = bg_copy.wait_recv
    finals.append(bg_copy.wait_send)

    bg_wait = due.pop("bgc")
    own_channels = pl.ds(pl.multiple_of(512 * g + 256 * w, 256), 256)
    bx_send, bx_recv = names.take(3), names.take(3)
    by_send, by_recv = names.take(4), names.take(4)

    def bga_of(block, core):
        return bga.at[:, pl.ds(pl.multiple_of(512 * block + 256 * core, 256), 256), :]

    def bg_chip(kx, ky):
        slot = kx + 2 * ky - 1
        return copy(bgh, bga_of(g, w), bx_send + slot, bx_recv + slot, peer(kx, ky, 0)[0])

    def bg_core(n, block):
        return copy(bga_of(block, w), bga_of(block, w), by_send + n, by_recv + n, peer(0, 0, 1)[0])

    bg_copies = [bg_chip(kx, ky) for kx, ky in chips]
    due["bg"] = each(bg_copies, "wait_recv")
    finals.append(each(bg_copies, "wait_send"))
    bg_own = bg_core(3, g)
    finals.append(bg_own.wait_send)
    due["by", 3] = bg_own.wait_recv

    def bg_sum():
        bg_wait()
        bgh[...] = (bg[:, pl.ds(w256, 256), :] + bgr[...]).astype(bf16)
        each(bg_copies, "start")()
        bga[:, own_channels, :] = bgh[...]
        bg_own.start()

    pl.when(w == 1)(bg_sum)

    middle_send(2)
    finals.append(scatter_sent)

    weight_grad(yq, 1 - w)
    pl.when(w == 1)(lambda: dw_copy.start())

    def dw_sum():
        @pl.when(w == 0)
        def _():
            dw_copy.wait_recv()
            dw[1] = dw[1] + dwr[...]
            pl.when(yq == 0)(lambda: cg_out(dw.at[1]).start())
            pl.when(yq == 1)(lambda: dw_back.start())

    def dw_place():
        @pl.when((w == 1) & (yq == 1))
        def _():
            dw_back.wait_recv()
            cg_out(dwr).start()

        dw_copy.wait_send()

        @pl.when(w != yq)
        def _():
            dw_y.wait_recv()
            dw[0] = dwx[...].astype(f32)
            cg_out(dw.at[0]).start()

    due["dw"] = dw_sum
    due["dwy"] = dw_place
    finals.append(lambda: cg_out(dw.at[0]).wait())
    finals.append(lambda: pl.when(w == 1)(lambda: dw_y.wait_send()))
    finals.append(lambda: pl.when((w == 0) & (yq == 1))(lambda: dw_back.wait_send()))

    s_send, s_recv = names.take(7), names.take(7)

    def small_copy(n):
        return copy(small, smr.at[n], s_send + n, s_recv + n, peer(*plane[n])[0])

    small_copies = [small_copy(n) for n in range(7)]
    each(small_copies, "start")()
    due["small"] = each(small_copies, "wait_recv")
    finals.append(each(small_copies, "wait_send"))


    gp_wait = due.pop("gp")

    def ru_wait():
        pl.when(z > 0)(lambda: ru_copy(2).wait_recv())

    def rd_wait():
        pl.when(z < 3)(lambda: rd_copy(2).wait_recv())

    q_send, q_recv = names.take(8), names.take(8)

    def fg_copy(n):
        dev, _ = peer(*plane[n])
        rows = pl.ds(pl.multiple_of(256 * dev["wa"] + 64 * dev["ha"], 64), 64)
        return copy(fgh.at[rows, :], fgrad_out.at[w, :, pl.ds(g512, 512)], q_send + n, q_recv + n, dev)

    fg_copies = [fg_copy(n) for n in range(7)]
    finals.append(each(fg_copies, "wait_send"))
    fg_own = pltpu.make_async_copy(
        fgh.at[pl.ds(own_row, 64), :], fgrad_out.at[w, :, pl.ds(g512, 512)], sems.at[q_send + 7]
    )
    finals.append(fg_own.wait)

    def fg_wait():
        for n in range(7):
            dev, block = peer(*plane[n])
            copy(
                fgh.at[pl.ds(0, 64), :],
                fgrad_out.at[dev["wa"], :, pl.ds(pl.multiple_of(512 * block, 512), 512)],
                q_send + n, q_recv + n, dev,
            ).wait_recv()

    finals.append(fg_wait)

    def feature_grads():
        gp_wait()
        pooled_back = gps[z].astype(f32)
        for j in range(3):
            pooled_back = pooled_back + gpr[j].astype(f32)
        count = cnt[z]
        pieces = [pooled_back[:, 128 * chunk:128 * chunk + 128] / count for chunk in range(4)]
        high, low = halves(jnp.concatenate(pieces, 1))
        fg[...] = dot(mt[z], high, ROWS_T) + dot(mt[z], low, ROWS_T)
        ok = val[z]

        ru_wait()
        rd_wait()

        @pl.when(z > 0)
        def _():
            dxf[z] = dxf[z] + rxu[2].astype(f32)

        @pl.when(z < 3)
        def _():
            dxf[z] = dxf[z] + rxd[2].astype(f32)

        for chunk in range(4):
            cols = slice(128 * chunk, 128 * chunk + 128)
            fgh[:, cols] = (fg[:, cols] + dxf[z, :, cols] * ok).astype(bf16)
        each(fg_copies, "start")()
        fg_own.start()

    @pl.when(w == 0)
    def _():
        feature_grads()
        bg_sum()

    arrive("dw")

    arrive("lt")
    lts[w] = lt[z] + ltr[0] + ltr[1] + ltr[2]
    ls_send, ls_recv = names.take(), names.take()
    logits_copy = copy(lts.at[w], lts.at[w], ls_send, ls_recv, peer(0, 0, 1)[0])
    logits_copy.start()
    due["ls"] = logits_copy.wait_recv
    finals.append(logits_copy.wait_send)

    pl.when(w == 1)(feature_grads)

    arrive("bg")
    for n, (kx, ky) in enumerate(chips):
        item = bg_core(n, peer(kx, ky, 0)[1])
        item.start()
        finals.append(item.wait_send)
        due["by", n] = item.wait_recv

    arrive("small")
    total = small[...]
    for n in range(7):
        total = total + smr[n]
    small_out[0:48, :] = total[0:48]
    small_out[48:56, :] = total[48:56]
    for kx, ky in [(0, 0)] + chips:
        dev, block = peer(kx, ky, 0)
        mine = small[...] if kx + ky == 0 else smr[plane.index((kx, ky, 0))]
        both = mine + smr[plane.index((kx, ky, 1))]
        small_out[pl.ds(56 + block, 1), :] = both[50:51]
        small_out[pl.ds(60 + block, 1), :] = both[51:52]

    arrive("ls")
    for micro in range(2):
        square[:, 0:24] = lts[micro].T
        tile = square[pl.ds(w64, 64), 0:classes] + cb[...]
        logits_out[micro] = tile * tile_valid(micro)[:, 0:classes]

    for n in range(4):
        arrive(("by", n))
    out_sem = names.take()
    bg_out = pltpu.make_async_copy(bga, bgrad_out, sems.at[out_sem])
    bg_out.start()

    finals.append(bg_out.wait)

    arrive("dwy")

    for wait in finals:
        wait()
    assert not due
    assert names.count <= SEMAPHORES


SEMAPHORES = 256


def place_kernel(
    logits, fgrad, bgrad, small, cgrad,
    logits_out, fgrad_out, bgrad_out, gains_out, biases_out, cgrad_out, gain_out, bias_out, weight_out, class_out,
    low, wide, feats, feats_wide, taps, square, sems,
):
    levels, classes, micros = bgrad.shape[0], class_out.shape[1], fgrad.shape[0]
    half = bgrad.shape[1] // 2
    pieces = [(n, pl.ds(half * h, half)) for n in range(levels) for h in range(2)]
    count = len(pieces)
    loads = [pltpu.make_async_copy(bgrad.at[p], low.at[p], sems.at[n]) for n, p in enumerate(pieces)]
    loads += [pltpu.make_async_copy(fgrad.at[m], feats.at[m], sems.at[count + m]) for m in range(micros)]
    tap_load = pltpu.make_async_copy(cgrad, taps, sems.at[count + micros])
    for load in loads:
        load.start()
    tap_load.start()
    first = count + micros + 1
    stores = [pltpu.make_async_copy(wide.at[p], bgrad_out.at[p], sems.at[first + n]) for n, p in enumerate(pieces)]
    stores += [
        pltpu.make_async_copy(feats_wide.at[m], fgrad_out.at[m], sems.at[first + count + m]) for m in range(micros)
    ]
    tap_stores = [
        pltpu.make_async_copy(taps.at[:, pl.ds(128 * t, 128)], cgrad_out.at[t], sems.at[first + count + micros + t])
        for t in range(TAPS)
    ]
    for n, p in enumerate(pieces):
        loads[n].wait()
        wide[p] = low[p].astype(jnp.float32)
        stores[n].start()
    for m in range(micros):
        loads[count + m].wait()
        feats_wide[m] = feats[m].astype(jnp.float32)
        stores[count + m].start()
    tap_load.wait()
    for store in tap_stores:
        store.start()
    logits_out[...] = logits[...]
    gains_out[...] = small[56:60, :]
    biases_out[...] = small[60:64, :]
    gain_out[...] = small[49:50, :]
    bias_out[...] = small[48:49, :]
    weight_out[...] = small[0:classes, :]
    square[...] = small[...]
    class_out[...] = square[24:56, :].T[0:1, 0:classes]
    for store in stores + tap_stores:
        store.wait()


def canvas_body(
    mesh, features, region_boxes, branch_weight, branch_gain, branch_bias, conv_weight, norm_gain, norm_bias,
    class_weight, class_bias, cotangent,
):
    f32, bf16 = jnp.float32, jnp.bfloat16
    micros, tile_rows, tile_cols, channels = features.shape
    pixels = tile_rows * tile_cols
    classes = class_bias.shape[0]
    lane_table, row_table = bin_tables()

    vmem = pl.BlockSpec(memory_space=pltpu.VMEM)
    hbm = pl.BlockSpec(memory_space=pl.ANY)
    smem = pl.BlockSpec(memory_space=pltpu.SMEM)
    V = pltpu.VMEM
    scratch = [
        V((4, 512, 512), bf16),
        V((4, 512, 512), bf16),
        V((1024, 1152), bf16),
        V((4, 512, 256), bf16),
        V((4, 512, 256), bf16),
        V((4, 256, 512), bf16),
        V((4, BINS, 512), bf16),
        V((4, BINS, 128), f32),
        V((4, BINS, 512), bf16),
        V((4, BINS, 128), f32),
        V((3, 4, WIDE, 128), f32),
        V((4, WIDE, 128), bf16),
        V((4, 4, WIDE, 128), bf16),
        V((4, 256, 512), bf16),
        V((4, 512, 128), f32),
        V((2, 272, 1152), f32),
        V((4, 2, 256, 128), f32),
        V((3, 4, 2, 64, 128), f32),
        V((4, 2, 256, 128), bf16),
        V((4, 512, 1152), bf16),
        V((3, 2, 272, 128), f32),
        V((4, 256, 1152), bf16),
        V((4, 512, 512), f32),
        V((3, 512, 512), bf16),
        V((3, 512, 512), bf16),
        V((3, 512, 512), bf16),
        V((3, 512, 512), bf16),
        V((4, 4, WIDE, 128), bf16),
        V((3, 4, WIDE, 128), bf16),
        V((4, WIDE, 128), f32),
        V((4, BINS, 128), f32),
        V((4, BINS, 256), bf16),
        V((4, BINS, 512), bf16),
        V((3, BINS, 512), bf16),
        V((2, 512, 1152), f32),
        V((512, 1152), f32),
        V((4, 512, 128), f32),
        V((4, 256, 128), f32),
        V((4, 256, 128), bf16),
        V((1, 24, 128), f32),
        V((4, 24, 128), f32),
        V((4, 24, 128), f32),
        V((3, 24, 128), f32),
        V((2, 24, 128), f32),
        V((2, 8, 128), f32),
        V((2, 3, 8, 128), f32),
        V((56, 128), f32),
        V((7, 56, 128), f32),
        V((4, WIDE, 128), f32),
        V((4, WIDE, 128), f32),
        V((2, 512, 128), f32),
        V((4, channels, 128), bf16),
        V((512, 512), f32),
        V((512, 512), bf16),
        V((24, 128), f32),
        V((2, 24, 128), f32),
        V((128, 128), f32),
        V((512, 1152), bf16),
        V((512, 1152), bf16),
        V((8, 128), f32),
        pltpu.SemaphoreType.DMA((SEMAPHORES,)),
        pltpu.SemaphoreType.REGULAR((2,)),
    ]
    share = conv_weight.shape[2]
    parts = pl.pallas_call(
        head_kernel,
        out_shape=(
            jax.ShapeDtypeStruct((micros, pixels, classes), f32),
            jax.ShapeDtypeStruct((micros, pixels, channels), bf16),
            jax.ShapeDtypeStruct((4, channels, share), bf16),
            jax.ShapeDtypeStruct((64, 128), f32),
            jax.ShapeDtypeStruct((512, TAPS * share), f32),
        ),
        in_specs=[smem, vmem, vmem, hbm, vmem, hbm, hbm, vmem, vmem, vmem, vmem, vmem, vmem],
        out_specs=(vmem, hbm, hbm, vmem, hbm),
        scratch_shapes=scratch,
        compiler_params=pltpu.CompilerParams(
            collective_id=0, has_side_effects=True, vmem_limit_bytes=60 * 2**20
        ),
    )(
        jnp.transpose(region_boxes, (1, 2, 0)), lane_table, row_table, features.reshape(micros, pixels, channels),
        cotangent.reshape(micros, pixels, classes), conv_weight, branch_weight, branch_gain, branch_bias,
        norm_gain.reshape(1, -1), norm_bias.reshape(1, -1), class_weight.T, class_bias.reshape(1, -1),
    )
    logits, feature_grad, branch_grad, gains, biases, conv_grad, gain, bias, weight, class_grad = pl.pallas_call(
        place_kernel,
        out_shape=(
            jax.ShapeDtypeStruct((micros, pixels, classes), f32),
            jax.ShapeDtypeStruct((micros, pixels, channels), f32),
            jax.ShapeDtypeStruct((4, channels, share), f32),
            jax.ShapeDtypeStruct((4, share), f32),
            jax.ShapeDtypeStruct((4, share), f32),
            jax.ShapeDtypeStruct((TAPS, 512, share), f32),
            jax.ShapeDtypeStruct((1, share), f32),
            jax.ShapeDtypeStruct((1, share), f32),
            jax.ShapeDtypeStruct((classes, share), f32),
            jax.ShapeDtypeStruct((1, classes), f32),
        ),
        in_specs=[vmem, hbm, hbm, vmem, hbm],
        out_specs=(vmem, hbm, hbm, vmem, vmem, hbm, vmem, vmem, vmem, vmem),
        scratch_shapes=[
            V((4, channels, share), bf16), V((4, channels, share), f32), V((micros, pixels, channels), bf16),
            V((micros, pixels, channels), f32), V((512, TAPS * share), f32), V((64, 128), f32),
            pltpu.SemaphoreType.DMA((40,)),
        ],
        compiler_params=pltpu.CompilerParams(vmem_limit_bytes=60 * 2**20),
    )(*parts)
    return (
        logits.reshape(micros, tile_rows, tile_cols, classes),
        feature_grad.reshape(features.shape),
        branch_grad,
        gains,
        biases,
        conv_grad,
        gain.reshape(-1),
        bias.reshape(-1),
        weight.T,
        class_grad.reshape(-1),
    )


def extended(block, sides, width):
    for axis, dim in sides:
        count = lax.axis_size(axis)
        forward = [(i, i + 1) for i in range(count - 1)]
        backward = [(target, source) for source, target in forward]
        low = lax.ppermute(
            lax.slice_in_dim(block, block.shape[dim] - width, None, axis=dim), axis, forward
        )
        high = lax.ppermute(lax.slice_in_dim(block, 0, width, axis=dim), axis, backward)
        block = jnp.concatenate([low, block, high], axis=dim)
    return block


def interpolate(offset, extent, n, bin_ids):
    scaled = offset * (n - 1)
    lower_bin = scaled // (extent - 1)
    fraction = (scaled - lower_bin * (extent - 1)).astype(jnp.float32) / (extent - 1).astype(
        jnp.float32
    )
    upper_bin = jnp.minimum(lower_bin + 1, n - 1)
    lower_hit = (bin_ids[None, :] == lower_bin[:, None]).astype(jnp.float32)
    upper_hit = (bin_ids[None, :] == upper_bin[:, None]).astype(jnp.float32)
    return (1.0 - fraction)[:, None] * lower_hit + fraction[:, None] * upper_hit


def layout(region, row_ids, col_ids):
    member_cols = []
    count_cols = []
    weight_per_level = []
    validity = jnp.zeros(row_ids.shape, jnp.float32)
    for n in LEVELS:
        bin_ids = jnp.arange(n, dtype=jnp.int32)
        level_weights = []
        for k in range(region.shape[0]):
            row_start = region[k, 0]
            col_start = region[k, 1]
            height = region[k, 2] - row_start
            width = region[k, 3] - col_start
            row_offset = row_ids - row_start
            col_offset = col_ids - col_start
            inside = (
                (row_offset >= 0) & (row_offset < height) & (col_offset >= 0) & (col_offset < width)
            )
            row_low = bin_ids * height // n
            row_high = ((bin_ids + 1) * height + n - 1) // n
            col_low = bin_ids * width // n
            col_high = ((bin_ids + 1) * width + n - 1) // n
            row_in = (row_offset[:, None] >= row_low[None, :]) & (
                row_offset[:, None] < row_high[None, :]
            )
            col_in = (col_offset[:, None] >= col_low[None, :]) & (
                col_offset[:, None] < col_high[None, :]
            )
            member = row_in[:, :, None] & col_in[:, None, :] & inside[:, None, None]
            member_cols.append(member.reshape(-1, n * n).astype(jnp.float32))
            count_cols.append(
                ((row_high - row_low)[:, None] * (col_high - col_low)[None, :]).reshape(n * n)
            )
            row_weight = interpolate(row_offset, height, n, bin_ids)
            col_weight = interpolate(col_offset, width, n, bin_ids)
            bilinear = (
                row_weight[:, :, None]
                * col_weight[:, None, :]
                * inside.astype(jnp.float32)[:, None, None]
            )
            level_weights.append(bilinear.reshape(-1, n * n))
            if n == 1:
                validity = validity + inside.astype(jnp.float32)
        weight_per_level.append(jnp.concatenate(level_weights, 1))
    counts = jnp.concatenate(count_cols).astype(jnp.float32)
    return (jnp.concatenate(member_cols, 1), weight_per_level, counts, validity)


def silu_slope(inputs):
    logistic = jax.nn.sigmoid(inputs)
    return logistic * (1.0 + inputs * (1.0 - logistic))


def tiled_body(
    features,
    region_boxes,
    branch_weight,
    branch_gain,
    branch_bias,
    conv_weight,
    norm_gain,
    norm_bias,
    class_weight,
    class_bias,
    cotangent,
):
    micros, tile_rows, tile_cols, channels = features.shape
    groups = lax.axis_size("col")
    regions = region_boxes.shape[1]
    share = conv_weight.shape[2]
    width_out = share * groups
    pixels = tile_rows * tile_cols
    flat_rows = groups * pixels
    col_index = lax.axis_index("col")
    tile_row_ids = lax.axis_index("ha") * tile_rows + jnp.arange(tile_rows, dtype=jnp.int32)
    tile_col_ids = lax.axis_index("wa") * tile_cols + jnp.arange(tile_cols, dtype=jnp.int32)
    row_ids = jnp.repeat(tile_row_ids, tile_cols)
    col_ids = jnp.tile(tile_col_ids, tile_rows)
    conv_flat = conv_weight.reshape(-1, share)
    conv_back = jnp.transpose(conv_weight, (0, 2, 1)).reshape(-1, conv_weight.shape[1])
    spans = [regions * n * n for n in LEVELS]
    starts = [sum(spans[:level_number]) for level_number in range(len(LEVELS))]
    grouped_boxes = region_boxes.reshape(groups, micros, regions, 4)
    branch_float = branch_weight.astype(jnp.float32)
    branch_grads = [jnp.zeros((channels, share), jnp.float32) for level_number in range(4)]
    branch_gain_grads = [jnp.zeros((share,), jnp.float32) for level_number in range(4)]
    branch_bias_grads = [jnp.zeros((share,), jnp.float32) for level_number in range(4)]
    norm_gain_total = jnp.zeros((share,), jnp.float32)
    norm_bias_total = jnp.zeros((share,), jnp.float32)
    class_weight_total = jnp.zeros(class_weight.shape, jnp.float32)
    class_bias_total = jnp.zeros(class_bias.shape, jnp.float32)
    conv_total = jnp.zeros(conv_flat.shape, jnp.float32)
    logit_list = []
    feature_list = []
    for m in range(micros):
        boxes_now = grouped_boxes[:, m]
        member_pixels, weight_per_level, counts, validity = jax.vmap(
            lambda region: layout(region, row_ids, col_ids)
        )(boxes_now)
        own_members = lax.dynamic_index_in_dim(member_pixels, col_index, 0, False)
        own_counts = lax.dynamic_index_in_dim(counts, col_index, 0, False)
        own_valid = lax.dynamic_index_in_dim(validity, col_index, 0, False)
        areas = (boxes_now[:, :, 2] - boxes_now[:, :, 0]) * (
            boxes_now[:, :, 3] - boxes_now[:, :, 1]
        )
        valid_total = jnp.sum(areas.astype(jnp.float32))
        local_x = features[m].reshape(pixels, channels)
        partial_value = jnp.einsum(
            "pb,pd->bd",
            own_members.astype(jnp.bfloat16),
            local_x,
            preferred_element_type=jnp.float32,
        )
        bin_total = lax.psum(partial_value, ("ha", "wa"))
        pooled = (bin_total / own_counts[:, None]).astype(jnp.bfloat16)
        pooled_all = lax.all_gather(pooled[None], "col", axis=0, tiled=True)
        branch_norms = []
        branch_affines = []
        branch_inverse = []
        branch_outs = []
        for level_number in range(4):
            level_pooled = pooled_all[
                :, starts[level_number] : starts[level_number] + spans[level_number]
            ]
            pre = jnp.einsum(
                "cbd,de->cbe",
                level_pooled,
                branch_weight[level_number],
                preferred_element_type=jnp.float32,
            )
            average = jnp.mean(pre, (0, 1))
            spread = jnp.mean(pre * pre, (0, 1)) - average * average
            inverse = lax.rsqrt(spread + EPSILON)
            normed_branch = (pre - average) * inverse
            affine_branch = branch_gain[level_number] * normed_branch + branch_bias[level_number]
            branch_norms.append(normed_branch)
            branch_affines.append(affine_branch)
            branch_inverse.append(inverse)
            branch_outs.append(jax.nn.silu(affine_branch))
        branch_local = jnp.concatenate(branch_outs, 1).astype(jnp.bfloat16)
        branch_full = lax.all_gather(branch_local, "col", axis=2, tiled=True)
        enlarged_map = []
        for level_number in range(4):
            level_output = branch_full[
                :, starts[level_number] : starts[level_number] + spans[level_number]
            ].astype(jnp.float32)
            spread_out = jnp.einsum(
                "zdw,zwk->zdk",
                weight_per_level[level_number],
                level_output,
                precision=FULL_ACCURACY,
            )
            enlarged_map.append(
                spread_out.reshape(groups, tile_rows, tile_cols, width_out).astype(jnp.bfloat16)
            )
        x_all = lax.all_gather(features[m][None], "col", axis=0, tiled=True)
        masked_x = x_all * validity.reshape(groups, tile_rows, tile_cols, 1).astype(jnp.bfloat16)
        stacked = jnp.concatenate([masked_x] + enlarged_map, -1)
        padded = extended(stacked, (("ha", 1), ("wa", 2)), 1)
        columns = jnp.concatenate(
            [
                padded[:, row_tap : row_tap + tile_rows, col_tap : col_tap + tile_cols]
                for row_tap in range(3)
                for col_tap in range(3)
            ],
            -1,
        ).reshape(flat_rows, -1)
        convolved = jnp.dot(columns, conv_flat, preferred_element_type=jnp.float32)
        valid_flat = validity.reshape(flat_rows, 1)
        first_sum, second_sum = lax.psum(
            (jnp.sum(convolved * valid_flat, 0), jnp.sum(convolved * convolved * valid_flat, 0)),
            ("ha", "wa"),
        )
        average = first_sum / valid_total
        spread = second_sum / valid_total - average * average
        inverse = lax.rsqrt(spread + EPSILON)
        normed = (convolved - average) * inverse
        affine = norm_gain * normed + norm_bias
        hidden = jax.nn.silu(affine)
        part_logits = jnp.dot(hidden, class_weight, precision=FULL_ACCURACY).reshape(
            groups, tile_rows, tile_cols, -1
        )
        summed = lax.psum_scatter(part_logits, "col", scatter_dimension=0, tiled=True)
        own_valid_tile = own_valid.reshape(tile_rows, tile_cols, 1)
        logit_list.append((summed[0] + class_bias) * own_valid_tile)
        seed = (cotangent[m] * own_valid_tile)[None]
        seed_all = lax.all_gather(seed, "col", axis=0, tiled=True).reshape(flat_rows, -1)
        grad_hidden = jnp.dot(seed_all, class_weight.T, precision=FULL_ACCURACY)
        grad_affine = grad_hidden * silu_slope(affine)
        bias_sum, gain_sum, class_part, bias_part = lax.psum(
            (
                jnp.sum(grad_affine, 0),
                jnp.sum(grad_affine * normed, 0),
                jnp.dot(hidden.T, seed_all, precision=FULL_ACCURACY),
                jnp.sum(seed_all, 0),
            ),
            ("ha", "wa"),
        )
        norm_bias_total = norm_bias_total + bias_sum
        norm_gain_total = norm_gain_total + gain_sum
        class_weight_total = class_weight_total + class_part
        class_bias_total = class_bias_total + bias_part
        grad_conv = (
            valid_flat
            * inverse
            * (
                grad_affine * norm_gain
                - norm_gain * bias_sum / valid_total
                - normed * norm_gain * gain_sum / valid_total
            )
        )
        grad_low = grad_conv.astype(jnp.bfloat16)
        grad_pad = extended(
            grad_low.reshape(groups, tile_rows, tile_cols, share), (("ha", 1), ("wa", 2)), 1
        )
        grad_columns = jnp.concatenate(
            [
                grad_pad[
                    :, 2 - row_tap : 2 - row_tap + tile_rows, 2 - col_tap : 2 - col_tap + tile_cols
                ]
                for row_tap in range(3)
                for col_tap in range(3)
            ],
            -1,
        ).reshape(flat_rows, -1)
        grad_stacked = jnp.dot(grad_columns, conv_back, preferred_element_type=jnp.float32)
        conv_part = jnp.einsum("pk,pe->ke", columns, grad_low, preferred_element_type=jnp.float32)
        conv_total = conv_total + conv_part
        grad_x = grad_stacked[:, :channels]
        bin_parts = []
        for level_number in range(4):
            level_gradient = grad_stacked[
                :, channels + level_number * width_out : channels + (level_number + 1) * width_out
            ].reshape(groups, pixels, width_out)
            bin_parts.append(
                jnp.einsum(
                    "qkl,qko->qlo",
                    weight_per_level[level_number],
                    level_gradient,
                    precision=FULL_ACCURACY,
                )
            )
        bin_local = jnp.concatenate(bin_parts, 1)
        bin_grad = lax.psum(bin_local, ("ha", "wa", "col"))
        own_bin_grad = lax.dynamic_slice_in_dim(bin_grad, col_index * share, share, 2)
        grad_pres = []
        for level_number in range(4):
            grad_out = own_bin_grad[
                :, starts[level_number] : starts[level_number] + spans[level_number]
            ]
            grad_act = grad_out * silu_slope(branch_affines[level_number])
            act_sum = jnp.sum(grad_act, (0, 1))
            act_norm_sum = jnp.sum(grad_act * branch_norms[level_number], (0, 1))
            samples = float(groups * spans[level_number])
            branch_bias_grads[level_number] = branch_bias_grads[level_number] + act_sum
            branch_gain_grads[level_number] = branch_gain_grads[level_number] + act_norm_sum
            grad_pre = branch_inverse[level_number] * (
                branch_gain[level_number] * grad_act
                - branch_gain[level_number] * act_sum / samples
                - branch_norms[level_number] * branch_gain[level_number] * act_norm_sum / samples
            )
            level_pooled = pooled_all[
                :, starts[level_number] : starts[level_number] + spans[level_number]
            ].astype(jnp.float32)
            branch_grads[level_number] = branch_grads[level_number] + jnp.einsum(
                "cbd,cbe->de", level_pooled, grad_pre, precision=FULL_ACCURACY
            )
            grad_pres.append(grad_pre)
        pooled_grads = [
            jnp.einsum(
                "cbe,de->cbd",
                grad_pres[level_number],
                branch_float[level_number],
                precision=FULL_ACCURACY,
            )
            for level_number in range(4)
        ]
        grad_pooled = jnp.concatenate(pooled_grads, 1)
        back_x, back_pooled = (
            lax.psum_scatter(
                grad_x.reshape(groups, pixels, channels).astype(jnp.bfloat16),
                "col",
                scatter_dimension=0,
                tiled=True,
            ).astype(jnp.float32),
            lax.psum_scatter(
                grad_pooled.astype(jnp.bfloat16), "col", scatter_dimension=0, tiled=True
            ).astype(jnp.float32),
        )
        pooled_back = back_pooled[0]
        spread_back = jnp.dot(
            own_members, pooled_back / own_counts[:, None], precision=FULL_ACCURACY
        )
        feature_list.append(
            (back_x[0] * own_valid[:, None] + spread_back).reshape(tile_rows, tile_cols, channels)
        )
    conv_result = lax.psum_scatter(
        conv_total.reshape(9, -1, share), ("ha", "wa"), scatter_dimension=1, tiled=True
    )
    return (
        jnp.stack(logit_list),
        jnp.stack(feature_list),
        jnp.stack(branch_grads),
        jnp.stack(branch_gain_grads),
        jnp.stack(branch_bias_grads),
        conv_result,
        norm_gain_total,
        norm_bias_total,
        class_weight_total,
        class_bias_total,
    )


def solution(mesh):
    placed = (
        P("col", "ha", "wa", None),
        P(),
        P(None, None, "col"),
        P(None, "col"),
        P(None, "col"),
        P(None, None, "col"),
        P("col"),
        P("col"),
        P("col", None),
        P(),
        P("col", "ha", "wa", None),
    )
    return jax.shard_map(
        functools.partial(canvas_body, mesh) if whole_canvas_plan(mesh) else tiled_body,
        mesh=mesh,
        in_specs=placed,
        out_specs=(
            P("col", "ha", "wa", None),
            P("col", "ha", "wa", None),
            P(None, None, "col"),
            P(None, "col"),
            P(None, "col"),
            P(None, ("ha", "wa"), "col"),
            P("col"),
            P("col"),
            P("col", None),
            P(),
        ),
        check_vma=False,
    )
```

```python
import functools

import jax
import jax.numpy as jnp
import numpy as np
from jax import lax
from jax.experimental import pallas as pl
from jax.experimental.pallas import tpu as pltpu
from jax.sharding import PartitionSpec as P

EPSILON = 1e-05
LEVELS = (1, 2, 3, 6)
FULL_ACCURACY = lax.Precision.HIGHEST
MESH = pl.DeviceIdType.MESH


SPANS = (16, 16, 32, 112)
STARTS = (0, 16, 32, 64)
BINS = 176
WIDE = 112
TAPS = 9


def whole_canvas_plan(mesh):
    return mesh.shape["ha"] == 4 and mesh.shape["wa"] == 2 and mesh.shape["col"] == 4


def bin_tables():
    lanes = np.zeros((4, 8, 128), np.float32)
    rows = np.zeros((BINS, 8), np.float32)
    rows[:, 3] = 1.0
    for level, n in enumerate(LEVELS):
        lanes[level, 3, :] = n - 1
        for k in range(3):
            for i in range(n):
                for j in range(n):
                    b = (k * n + i) * n + j
                    lanes[level, :3, b] = (k, i, j)
                    lanes[level, 4, b] = 1.0
                    row = STARTS[level] + b
                    for at, value in enumerate((k, i, j, n, 1.0)):
                        rows[row, at] = value
    return lanes, rows


def dot(a, b, dims=((1,), (0,)), precision=None):
    return lax.dot_general(a, b, (dims, ((), ())), precision=precision, preferred_element_type=jnp.float32)


ROWS_T = ((0,), (0,))
BOTH_LAST = ((1,), (1,))


def halves(value):
    high = value.astype(jnp.bfloat16)
    return high, (value - high.astype(jnp.float32)).astype(jnp.bfloat16)


def pick3(index, values):
    return jnp.where(index == 0.0, values[0], jnp.where(index == 1.0, values[1], values[2]))


class Sems:
    def __init__(self):
        self.count = 0

    def take(self, n=1):
        at = self.count
        self.count += n
        return at


def head_kernel(
    boxes, lane_table, row_table, feat, cot, wconv, wbranch, bgain, bbias, ngain, nbias, cw_in, cb,
    logits_out, fgrad_out, bgrad_out, small_out, cgrad_out,
    x, lv, wall, wb2, u2, ut, mt, cnt, po, pre, prr, bos, bor, bo2, val, yp, p, cr, gc, g9, gp3, tb,
    dxf, sbu, sbd, rxu, rxd, gb, grr, gpre, gpa, gpx, gps, gpr, dw, dwr, bg, bgr, bgh, seed_in, sd, lt, ltr, lts,
    st, str_, small, smr, nb_s, af_s, cn_s, bga, fg, fgh, cwt, seeds, square, dwh, dwx, bi_s, sems, turn,
):
    f32, bf16 = jnp.float32, jnp.bfloat16
    q, w, z = lax.axis_index("ha"), lax.axis_index("wa"), lax.axis_index("col")
    xq, yq = lax.rem(q, 2), lax.div(q, 2)
    g = 2 * xq + yq
    classes = cb.shape[1]
    zm = lax.div(z, 2)
    zz = z * (1 - zm) + (3 - z) * zm
    names = Sems()
    finals = []
    due = {}

    def arrive(name):
        due.pop(name)()

    def each(copies, method):
        def run():
            for c in copies:
                getattr(c, method)()

        return run


    def peer(kx, ky, kw):
        px = xq + kx - 2 * kx * xq
        py = yq + ky - 2 * ky * yq
        return {"ha": 2 * py + px, "wa": w + kw - 2 * kw * w}, 2 * px + py

    def copy(src, dst, ss, rs, dev):
        return pltpu.make_async_remote_copy(
            src_ref=src, dst_ref=dst, send_sem=sems.at[ss], recv_sem=sems.at[rs], device_id=dev, device_id_type=MESH
        )

    def zpeer(j):
        return {"col": lax.rem(z + j, 4)}

    plane = [(kx, ky, kw) for kw in (0, 1) for ky in (0, 1) for kx in (0, 1) if kx + ky + kw]
    chips = [(1, 0), (0, 1), (1, 1)]

    barrier = pltpu.get_barrier_semaphore()
    for kx, ky, kw in plane:
        pl.semaphore_signal(barrier, 1, device_id=peer(kx, ky, kw)[0], device_id_type=MESH)
    for j in (1, 2, 3):
        pl.semaphore_signal(barrier, 1, device_id=zpeer(j), device_id_type=MESH)

    g512 = pl.multiple_of(g * 512, 512)
    weight_copies = []
    for t in range(TAPS):
        for part in range(2):
            s = names.take()
            weight_copies.append(
                pltpu.make_async_copy(
                    wconv.at[t, pl.ds(2048 * part + g512, 512), :],
                    wall.at[pl.ds(512 * part, 512), pl.ds(128 * t, 128)],
                    sems.at[s],
                )
            )
    for twice in range(2):
        s = names.take()
        weight_copies.append(
            pltpu.make_async_copy(
                wbranch.at[:, pl.ds(g512, 512), :], wb2.at[:, :, pl.ds(128 * twice, 128)], sems.at[s]
            )
        )
    for c in weight_copies:
        c.start()
    due["weights"] = each(weight_copies, "wait")

    for half in range(2):
        bo2[:, 128 * half + WIDE:128 * half + 128, :] = jnp.zeros((4, 128 - WIDE, 512), bf16)
    yp[:, 0:8, :] = jnp.zeros((2, 8, 1152), f32)
    yp[:, 264:272, :] = jnp.zeros((2, 8, 1152), f32)
    gp3[:, :, 0:8, :] = jnp.zeros((3, 2, 8, 128), f32)
    gp3[:, :, 264:272, :] = jnp.zeros((3, 2, 8, 128), f32)
    small[...] = jnp.zeros(small.shape, f32)
    st[...] = jnp.zeros(st.shape, f32)
    p[...] = jnp.zeros(p.shape, f32)
    nb_s[...] = jnp.zeros(nb_s.shape, f32)
    gpre[...] = jnp.zeros(gpre.shape, f32)
    cwt[...] = jnp.zeros(cwt.shape, f32)
    cwt[0:classes, :] = cw_in[...]
    pl.semaphore_wait(barrier, 10)

    q64 = pl.multiple_of(64 * q, 64)
    a_send, a_recv = names.take(8), names.take(8)
    own_row = pl.multiple_of(256 * w + 64 * q, 64)
    own = pltpu.make_async_copy(feat.at[w, :, pl.ds(g512, 512)], x.at[z, pl.ds(own_row, 64), :], sems.at[a_send])

    def tile_copy(t, kx, ky):
        n = 4 * (t + w - 2 * t * w) + 2 * ky + kx
        dev, block = peer(kx, ky, 0)
        return copy(
            feat.at[t, :, pl.ds(pl.multiple_of(512 * block, 512), 512)], x.at[z, pl.ds(own_row, 64), :],
            a_send + n, a_recv + n, {"ha": dev["ha"], "wa": t},
        )

    def tiles(t, method):
        for kx, ky in chips:
            getattr(tile_copy(t, kx, ky), method)()
        pl.when(w != t)(lambda: getattr(tile_copy(t, 0, 0), method)())

    def tiles_wait():
        for n, (kx, ky, kw) in enumerate(plane):
            at = 4 * kw + 2 * ky + kx
            copy(
                feat.at[0, :, pl.ds(0, 512)], x.at[z, pl.ds(own_row, 64), :], a_send + at, a_recv + at, peer(kx, ky, kw)[0]
            ).wait_recv()

    own.start()
    tiles(0, "start")

    def scalars(canvas, micro=None):
        index = 2 * canvas + (w if micro is None else micro)
        return [[boxes[k, e, index] for k in range(3)] for e in range(4)]

    def px(rows, lanes, axis, start=0):
        at = lax.broadcasted_iota(jnp.int32, (rows, lanes), axis) + start
        half = at // 256
        return (at // 8 % 32).astype(f32), (half * 8 + at % 8).astype(f32)

    def tile_valid(micro):
        at = lax.broadcasted_iota(jnp.int32, (64, 128), 0)
        y, xx = (8 * q + at // 8).astype(f32), (8 * w + at % 8).astype(f32)
        top, left, bottom, right = [[v.astype(f32) for v in values] for values in scalars(z, micro)]
        ok = jnp.zeros((64, 128), f32)
        for k in range(3):
            ok = jnp.where((y >= top[k]) & (y < bottom[k]) & (xx >= left[k]) & (xx < right[k]), 1.0, ok)
        return ok

    def layout(c):
        top, left, bottom, right = [[v.astype(f32) for v in values] for values in scalars(c)]
        y, xx = px(512, 128, 0)
        ok = jnp.zeros((512, 128), f32)
        for k in range(3):
            ok = jnp.where((y >= top[k]) & (y < bottom[k]) & (xx >= left[k]) & (xx < right[k]), 1.0, ok)
        val[c] = ok
        table = lane_table[g]
        box, bi, bj, n1, real = [table[e:e + 1] for e in range(5)]
        t_, l_, b_, r_ = [pick3(box, v) for v in (top, left, bottom, right)]
        h1, w1 = b_ - t_ - 1.0, r_ - l_ - 1.0
        rw = jnp.maximum(1.0 - jnp.abs((y - t_) * n1 - bi * h1) / h1, 0.0)
        cw = jnp.maximum(1.0 - jnp.abs((xx - l_) * n1 - bj * w1) / w1, 0.0)
        inside = (y >= t_) & (y < b_) & (xx >= l_) & (xx < r_) & (real > 0.0)
        weights = jnp.where(inside, rw * cw, 0.0)
        high, low = halves(weights)
        u2[c, :, 0:128] = high
        u2[c, :, 128:256] = low
        high, low = halves(weights.T)
        ut[c, 0:128, :] = high
        ut[c, 128:256, :] = low
        box, bi, bj, n, real = [jnp.broadcast_to(row_table[:, e:e + 1], (BINS, 128)) for e in range(5)]
        t_, l_, b_, r_ = [pick3(box, v) for v in (top, left, bottom, right)]
        h, wd = b_ - t_, r_ - l_
        row_low = jnp.floor((bi * h + 0.5) / n)
        row_high = jnp.floor(((bi + 1.0) * h + n - 0.5) / n)
        col_low = jnp.floor((bj * wd + 0.5) / n)
        col_high = jnp.floor(((bj + 1.0) * wd + n - 0.5) / n)
        cnt[c] = jnp.where(real > 0.0, (row_high - row_low) * (col_high - col_low), 1.0)
        for chunk in range(4):
            y, xx = px(BINS, 128, 1, 128 * chunk)
            u, v = y - t_, xx - l_
            member = (u >= row_low) & (u < row_high) & (v >= col_low) & (v < col_high) & (real > 0.0)
            mt[c, :, 128 * chunk:128 * chunk + 128] = jnp.where(member, 1.0, 0.0).astype(bf16)

    def combine():
        out = []
        zs = []
        for b in range(3):
            acc = [None, None]
            for h in range(2):
                for a in range(3):
                    t = 3 * a + b
                    piece = yp[h, 8 * a:8 * a + 256, 128 * t:128 * t + 128]
                    acc[h] = piece if acc[h] is None else acc[h] + piece
            zs.append(acc)
        col = lax.broadcasted_iota(jnp.int32, (256, 128), 0) % 8
        first, last = col == 0, col == 7
        out0 = zs[1][0] + jnp.where(first, 0.0, pltpu.roll(zs[0][0], 1, 0))
        out0 = out0 + jnp.where(last, pltpu.roll(zs[2][1], 7, 0), pltpu.roll(zs[2][0], 255, 0))
        out1 = zs[1][1] + jnp.where(first, pltpu.roll(zs[0][0], 249, 0), pltpu.roll(zs[0][1], 1, 0))
        out1 = out1 + jnp.where(last, 0.0, pltpu.roll(zs[2][1], 255, 0))
        return out0, out1

    def conv_part(operand, part):
        for h in range(2):
            yp[h, 8:264, :] = dot(operand[256 * h:256 * h + 256], wall[512 * part:512 * part + 512, :])
        return combine()

    e_send, e_recv = names.take(16), names.take(12)

    def pre_copy(level, c, kx, ky):
        slot = kx + 2 * ky - 1
        return copy(
            pre.at[c, pl.ds(STARTS[level], SPANS[level]), :],
            prr.at[slot, c, pl.ds(0, SPANS[level]), :],
            e_send + 4 * level + c, e_recv + 4 * slot + c, peer(kx, ky, 0)[0],
        )

    def to_level_owner(level, action):
        lx, ly = level // 2, level % 2
        for kx, ky in chips:
            wanted = (xq + kx - 2 * kx * xq == lx) & (yq + ky - 2 * ky * yq == ly)
            pl.when(wanted)(functools.partial(action, kx, ky))

    def pool(c):
        total = dot(mt[c], x[c])
        for chunk in range(4):
            cols = slice(128 * chunk, 128 * chunk + 128)
            po[c, :, cols] = (total[:, cols] / cnt[c]).astype(bf16)

    def branch_products(c):
        for level in range(4):
            rows = slice(STARTS[level], STARTS[level] + SPANS[level])
            pre[c, rows, :] = dot(po[c, rows, :], wb2[level, :, 0:128])
        for level in range(4):
            to_level_owner(level, lambda kx, ky, level=level: pre_copy(level, c, kx, ky).start())

    def conv_add(c, operand, part):
        out0, out1 = conv_part(operand, part)
        p[c, 0] = p[c, 0] + out0
        p[c, 1] = p[c, 1] + out1

    layout(z)
    for copy_out in (tiles,):
        copy_out(0, "wait_send")
        copy_out(1, "start")
    due["A"] = tiles_wait
    due["A own"] = own.wait
    finals.append(lambda: tiles(1, "wait_send"))

    w64 = pl.multiple_of(64 * w, 64)
    square[...] = jnp.zeros(square.shape, f32)
    for micro in range(2):
        square[pl.ds(w64, 64), 0:classes] = cot[micro] * tile_valid(micro)[:, 0:classes]
        seeds[micro] = square[...].T[0:24]
    sc_send, sc_recv = names.take(), names.take()
    seed_copy = copy(seeds.at[1 - w], seed_in.at[0], sc_send, sc_recv, peer(0, 0, 1)[0])
    seed_copy.start()
    due["seed"] = seed_copy.wait_recv
    finals.append(seed_copy.wait_send)

    arrive("weights")
    arrive("A")
    arrive("A own")
    ok = val[z]
    for chunk in range(4):
        cols = slice(128 * chunk, 128 * chunk + 128)
        x[z, :, cols] = (x[z, :, cols].astype(f32) * ok).astype(bf16)

    up_send, up_recv, dn_send, dn_recv = names.take(6), names.take(6), names.take(6), names.take(6)

    def half_of(c, h):
        return x.at[c, pl.ds(256 * h, 256), :]

    def up_copy(k, h):
        part = half_of(z - k, h)
        return copy(part, part, up_send + 2 * k + h, up_recv + 2 * k + h, {"col": z + 1})

    def dn_copy(k, h):
        part = half_of(z + k, h)
        return copy(part, part, dn_send + 2 * k + h, dn_recv + 2 * k + h, {"col": z - 1})

    def take_in(k, h):
        n = 2 * (k - 1) + h

        @pl.when(z >= k)
        def _():
            part = half_of(z - k, h)
            copy(part, part, up_send + n, up_recv + n, {"col": z}).wait_recv()

        @pl.when(z + k <= 3)
        def _():
            part = half_of(z + k, h)
            copy(part, part, dn_send + n, dn_recv + n, {"col": z}).wait_recv()

    other = peer(0, 0, 1)[0]

    def up_last(k):
        return (w == 0) & (z < 3) & (z == k)

    def dn_last(k):
        return (w == 0) & (z > 0) & (3 - z == k)

    def pass_on(k, h):
        pl.when((z >= k) & (z < 3))(lambda: up_copy(k, h).start())
        pl.when((z + k <= 3) & (z > 0))(lambda: dn_copy(k, h).start())
        if k == 2 and h == 1:
            give_turn(k)

    def passed_on():
        for k in range(3):
            for h in range(2):
                up_done, dn_done = (z >= k) & (z < 3), (z + k <= 3) & (z > 0)
                if h == 0 and k < 2:
                    up_done = up_done & jnp.logical_not(up_last(k))
                    dn_done = dn_done & jnp.logical_not(dn_last(k))
                pl.when(up_done)(lambda: up_copy(k, h).wait_send())
                pl.when(dn_done)(lambda: dn_copy(k, h).wait_send())

    finals.append(passed_on)

    def give_turn(k):
        @pl.when(up_last(k))
        def _():
            if k < 2:
                up_copy(k, 0).wait_send()
            pl.semaphore_signal(turn.at[0], 1, device_id=other, device_id_type=MESH)

        @pl.when(dn_last(k))
        def _():
            if k < 2:
                dn_copy(k, 0).wait_send()
            pl.semaphore_signal(turn.at[1], 1, device_id=other, device_id_type=MESH)

    def own_turn(up):
        def start():
            pl.semaphore_wait(turn.at[0 if up else 1], 1)
            for h in range(2):
                (up_copy(0, h) if up else dn_copy(0, h)).start()

        pl.when((z < 3) if up else (z > 0))(start)

    @pl.when(w == 0)
    def _():
        pass_on(0, 0)
        pass_on(0, 1)

    arrive("seed")
    sd[z] = seeds[w] + seed_in[0]
    sz_send, sz_recv = names.take(3), names.take(3)
    sd_copies = [copy(sd.at[z], sd.at[z], sz_send + j - 1, sz_recv + j - 1, zpeer(j)) for j in (1, 2, 3)]
    each(sd_copies, "start")()
    finals.append(each(sd_copies, "wait_send"))

    def sd_wait():
        for j in (1, 2, 3):
            src = lax.rem(z + 4 - j, 4)
            copy(sd.at[src], sd.at[src], sz_send + j - 1, sz_recv + j - 1, zpeer(j)).wait_recv()

    due["sd"] = sd_wait

    pool(z)
    branch_products(z)
    conv_add(z, x[z], 0)

    def rest(i, carry):
        layout(lax.rem(z + i, 4))
        return carry

    lax.fori_loop(1, 4, rest, 0)

    def pre_wait():
        for c in range(4):
            for kx, ky in chips:
                slot = kx + 2 * ky - 1
                for level in range(4):

                    @pl.when(g == level)
                    def _():
                        copy(
                            pre.at[c, pl.ds(STARTS[level], SPANS[level]), :],
                            prr.at[slot, c, pl.ds(0, SPANS[level]), :],
                            e_send, e_recv + 4 * slot + c, peer(0, 0, 1)[0],
                        ).wait_recv()

    def pre_sent():
        for level in range(4):
            for c in range(4):
                to_level_owner(level, lambda kx, ky: pre_copy(level, c, kx, ky).wait_send())

    finals.append(pre_sent)
    level_n = jnp.where(g == 0, 1.0, jnp.where(g == 1, 2.0, jnp.where(g == 2, 3.0, 6.0)))
    samples = 12.0 * level_n * level_n

    def rows_of(value):
        return value.reshape(4 * WIDE, 128)

    def branch_norm():
        pre_wait()
        for level in range(4):

            @pl.when(g == level)
            def _():
                span = SPANS[level]
                for c in range(4):
                    total = pre[c, STARTS[level]:STARTS[level] + span, :]
                    for slot in range(3):
                        total = total + prr[slot, c, 0:span, :]
                    nb_s[c, 0:span, :] = total

        pre_all = rows_of(nb_s[...])
        average = jnp.sum(pre_all, 0, keepdims=True) / samples
        spread = jnp.sum(pre_all * pre_all, 0, keepdims=True) / samples - average * average
        b_inverse = lax.rsqrt(spread + EPSILON)
        b_norm = (pre_all - average) * b_inverse
        b_act = b_gain * b_norm + bbias[pl.ds(g, 1), :]
        nb_s[...] = b_norm.reshape(4, WIDE, 128)
        bi_s[0:1, :] = b_inverse
        logistic = jax.nn.sigmoid(b_act)
        af_s[...] = (logistic * (1.0 + b_act * (1.0 - logistic))).reshape(4, WIDE, 128)
        bos[...] = (b_act * logistic).astype(bf16).reshape(4, WIDE, 128)
        each(bo_copies, "start")()
        bor[z] = bos[...]

    b_gain = bgain[pl.ds(g, 1), :]
    f_send, f_recv = names.take(3), names.take(3)
    bo_copies = [copy(bos, bor.at[z], f_send + j - 1, f_recv + j - 1, zpeer(j)) for j in (1, 2, 3)]
    finals.append(each(bo_copies, "wait_send"))

    i_send, i_recv = names.take(12), names.take(12)

    def chip_rows(at):
        return pl.ds(pl.multiple_of(64 * at, 64), 64)

    def conv_copy(c, kx, ky):
        slot = kx + 2 * ky - 1
        dev, _ = peer(kx, ky, 0)
        return copy(p.at[c, :, chip_rows(dev["ha"]), :], cr.at[slot, c], i_send + 4 * slot + c, i_recv + 4 * slot + c, dev)

    def conv_send(c):
        for kx, ky in chips:
            conv_copy(c, kx, ky).start()

    def levels():
        each(bo_copies, "wait_recv")()
        for part in range(4):
            for half in range(2):
                bo2[:, 128 * half:128 * half + WIDE, 128 * part:128 * part + 128] = bor[part]

        def level_conv(c, carry):
            lv[c] = dot(u2[c], bo2[c]).astype(bf16)
            conv_add(c, lv[c], 1)
            conv_send(c)
            return carry

        lax.fori_loop(0, 4, level_conv, 0)

    @pl.when((w == 1) & (zm == 0))
    def _():
        own_turn(True)
        own_turn(False)

    @pl.when((w == 1) & (zm == 1))
    def _():
        own_turn(False)
        own_turn(True)

    def arrived(c):
        pool(c)
        branch_products(c)

    for k in (1, 2, 3):
        if k < 3:
            give_turn(k - 1)
        for h in range(2):
            take_in(k, h)
            if k < 3:
                pass_on(k, h)
        pl.when(z >= k)(lambda: arrived(z - k))
        pl.when(z + k <= 3)(lambda: arrived(z + k))

    branch_norm()

    def late(j, carry):
        c = lax.rem(z + j, 4)
        conv_add(c, x[c], 0)
        return carry

    lax.fori_loop(1, 4, late, 0)
    levels()

    conv_copies = [conv_copy(c, kx, ky) for c in range(4) for kx, ky in chips]
    due["conv"] = each(conv_copies, "wait_recv")
    finals.append(each(conv_copies, "wait_send"))

    arrive("sd")
    for c in range(4):
        cn_s[0, 128 * c:128 * c + 128, :] = dot(sd[c], cwt[...], ROWS_T, FULL_ACCURACY)

    arrive("conv")
    convolved = (p[:, :, pl.ds(q64, 64), :] + cr[0] + cr[1] + cr[2]).reshape(512, 128)
    ok = val.at[...].reshape(4, 2, 256, 128)[:, :, pl.ds(q64, 64), :].reshape(512, 128)

    j_send, j_recv = names.take(6), names.take(6)

    def stat_copy(stage, kx, ky):
        slot = kx + 2 * ky - 1
        return copy(
            st.at[stage], str_.at[stage, slot], j_send + 3 * stage + slot, j_recv + 3 * stage + slot, peer(kx, ky, 0)[0]
        )

    def plane_sum(stage, first, second):
        st[stage, 0:1, :] = first
        st[stage, 1:2, :] = second
        copies = [stat_copy(stage, kx, ky) for kx, ky in chips]
        each(copies, "start")()
        each(copies, "wait_recv")()
        finals.append(each(copies, "wait_send"))
        total = st[stage] + str_[stage, 0] + str_[stage, 1] + str_[stage, 2]
        return total[0:1], total[1:2]

    masked = convolved * ok
    first, second = plane_sum(0, jnp.sum(masked, 0, keepdims=True), jnp.sum(convolved * masked, 0, keepdims=True))
    area = jnp.int32(0)
    for c in range(4):
        top, left, bottom, right = scalars(c)
        for k in range(3):
            area = area + (bottom[k] - top[k]) * (right[k] - left[k])
    valid_total = area.astype(f32)
    average = first / valid_total
    spread = second / valid_total - average * average
    inverse = lax.rsqrt(spread + EPSILON)
    normed = (convolved - average) * inverse
    gain = ngain[...]
    affine = gain * normed + nbias[...]
    logistic = jax.nn.sigmoid(affine)
    hidden = affine * logistic
    grad_affine = cn_s[0] * (logistic * (1.0 + affine * (1.0 - logistic)))
    part_bias = jnp.sum(grad_affine, 0, keepdims=True)
    part_gain = jnp.sum(grad_affine * normed, 0, keepdims=True)
    cn_s[1] = hidden
    small[48:49, :] = part_bias
    small[49:50, :] = part_gain
    bias_sum, gain_sum = plane_sum(1, part_bias, part_gain)
    grad_conv = ok * inverse * (
        grad_affine * gain - gain * bias_sum / valid_total - normed * gain * gain_sum / valid_total
    )
    gc[:, :, pl.ds(q64, 64), :] = grad_conv.astype(bf16).reshape(4, 2, 64, 128)
    k_send, k_recv = names.take(3), names.take(3)

    def gc_copy(kx, ky, at):
        slot = kx + 2 * ky - 1
        block = gc.at[:, :, chip_rows(at), :]
        return copy(block, block, k_send + slot, k_recv + slot, peer(kx, ky, 0)[0])

    gc_copies = [gc_copy(kx, ky, q) for kx, ky in chips]
    each(gc_copies, "start")()
    due["gc"] = each(gc_copies, "wait_recv")
    finals.append(each(gc_copies, "wait_send"))

    arrive("gc")

    def shifted(c):
        col = lax.broadcasted_iota(jnp.int32, (256, 128), 0) % 8
        first, last = col == 0, col == 7
        g0, g1 = gc[c, 0].astype(f32), gc[c, 1].astype(f32)
        gp3[1, 0, 8:264, :] = g0
        gp3[1, 1, 8:264, :] = g1
        gp3[0, 0, 8:264, :] = jnp.where(last, pltpu.roll(g1, 7, 0), pltpu.roll(g0, 255, 0))
        gp3[0, 1, 8:264, :] = jnp.where(last, 0.0, pltpu.roll(g1, 255, 0))
        gp3[2, 0, 8:264, :] = jnp.where(first, 0.0, pltpu.roll(g0, 1, 0))
        gp3[2, 1, 8:264, :] = jnp.where(first, pltpu.roll(g0, 249, 0), pltpu.roll(g1, 1, 0))
        for a in range(3):
            for b in range(3):
                t = 3 * a + b
                for h in range(2):
                    start = 8 * (2 - a)
                    g9[c, 256 * h:256 * h + 256, 128 * t:128 * t + 128] = gp3[b, h, start:start + 256, :].astype(bf16)

    def level_rows(c, carry):
        shifted(c)
        both = dot(ut[c], g9[c])
        high, low = halves(both[0:128] + both[128:256])
        tb[c, 0:128, :] = high
        tb[c, 128:256, :] = low
        return carry

    def data_grad(c):
        for h in range(2):
            dxf[c, 256 * h:256 * h + 256, :] = dot(g9[c, 256 * h:256 * h + 256, :], wall[0:512, :], BOTH_LAST)

    ru_send, ru_recv, rd_send, rd_recv = names.take(3), names.take(3), names.take(3), names.take(3)

    def ru_copy(k):
        return copy(sbu.at[k], rxu.at[k], ru_send + k, ru_recv + k, {"col": z + 1})

    def rd_copy(k):
        return copy(sbd.at[k], rxd.at[k], rd_send + k, rd_recv + k, {"col": z - 1})

    def up_on(k):
        return (z + 3 - k <= 3) & (z < 3)

    def dn_on(k):
        return (z - 3 + k >= 0) & (z > 0)

    def end_send(k):
        @pl.when(z == 0)
        def _():
            sbu[k] = dxf[3 - k].astype(bf16)
            ru_copy(k).start()

        @pl.when(z == 3)
        def _():
            sbd[k] = dxf[k].astype(bf16)
            rd_copy(k).start()

    def middle_send(k):
        @pl.when(up_on(k) & (z > 0))
        def _():
            ru_copy(k - 1).wait_recv()
            sbu[k] = (dxf[z + 3 - k] + rxu[k - 1].astype(f32)).astype(bf16)
            ru_copy(k).start()

        @pl.when(dn_on(k) & (z < 3))
        def _():
            rd_copy(k - 1).wait_recv()
            sbd[k] = (dxf[z - 3 + k] + rxd[k - 1].astype(f32)).astype(bf16)
            rd_copy(k).start()

    def scatter_sent():
        for k in range(3):
            pl.when(up_on(k))(lambda: ru_copy(k).wait_send())
            pl.when(dn_on(k))(lambda: rd_copy(k).wait_send())

    def canvas_at(i):
        low = (3 - i) if i < 2 else zz * (i - 2) + (1 - zz) * (3 - i)
        return (1 - zm) * low + zm * (3 - low)

    n_send, n_recv = names.take(3), names.take(3)

    def gb_copies(method):
        for level in range(4):

            @pl.when(g == level)
            def _():
                for j in (1, 2, 3):
                    item = copy(
                        gb.at[lax.rem(z + j, 4), :, pl.ds(0, SPANS[level]), :],
                        grr.at[j - 1, :, pl.ds(0, SPANS[level]), :],
                        n_send + j - 1, n_recv + j - 1, zpeer(j),
                    )
                    getattr(item, method)()

    lax.fori_loop(0, 4, level_rows, 0)

    def level_pair(n, carry):
        both = dot(tb[pl.ds(2 * n, 2)].reshape(512, 1152), wall[512:1024, :], BOTH_LAST)
        for c in range(2):
            total = both[256 * c:256 * c + WIDE] + both[256 * c + 128:256 * c + 128 + WIDE]
            for part in range(4):
                gb[part, 2 * n + c] = total[:, 128 * part:128 * part + 128].astype(bf16)
        return carry

    lax.fori_loop(0, 2, level_pair, 0)
    gb_copies("start")
    due["gb"] = lambda: gb_copies("wait_recv")
    finals.append(lambda: gb_copies("wait_send"))

    def weight_grad(part, slot):

        for tile in range(2):
            cols = slice(256 * tile, 256 * tile + 256)

            def of(operand):
                total = None
                for c in range(4):
                    piece = dot(operand[c, :, cols], g9[c], ROWS_T)
                    total = piece if total is None else total + piece
                dw[slot, cols, :] = total

            pl.when(part == 0)(lambda: of(x))
            pl.when(part == 1)(lambda: of(lv))

    w_send, w_recv = names.take(), names.take()
    dw_copy = copy(dw.at[0], dwr, w_send, w_recv, other)
    y_send, y_recv = names.take(), names.take()
    dw_y = copy(dwh, dwx, y_send, y_recv, {"ha": peer(0, 1, 0)[0]["ha"], "wa": yq})
    b_send, b_recv = names.take(), names.take()
    dw_back = copy(dw.at[1], dwr, b_send, b_recv, other)
    cg_sem = names.take()

    def cg_out(src):
        return pltpu.make_async_copy(src, cgrad_out, sems.at[cg_sem])

    weight_grad(1 - yq, w)
    pl.when(w == 0)(lambda: dw_copy.start())

    @pl.when(w == 1)
    def _():
        dw_copy.wait_recv()
        dwh[...] = (dw[1] + dwr[...]).astype(bf16)
        dw_y.start()

    for i in range(4):
        data_grad(canvas_at(i))
        if i < 3:
            end_send(i)

    arrive("gb")
    for level in range(4):

        @pl.when(g == level)
        def _():
            span = SPANS[level]
            total = gb[z, :, 0:span, :].astype(f32)
            for j in range(3):
                total = total + grr[j, :, 0:span, :].astype(f32)
            gpre[:, 0:span, :] = total

    grad_act = rows_of(gpre[...]) * rows_of(af_s[...])
    b_norm = rows_of(nb_s[...])
    act_sum = jnp.sum(grad_act, 0, keepdims=True)
    act_norm_sum = jnp.sum(grad_act * b_norm, 0, keepdims=True)
    small[50:51, :] = act_norm_sum
    small[51:52, :] = act_sum
    grad_pre = bi_s[0:1, :] * (
        b_gain * grad_act - b_gain * act_sum / samples - b_norm * b_gain * act_norm_sum / samples
    )
    gpre[...] = grad_pre.reshape(4, WIDE, 128)
    o_send, o_recv = names.take(3), names.take(12)

    def gpre_copies(method):
        for level in range(4):

            @pl.when(g == level)
            def _():
                rows = pl.ds(STARTS[level], SPANS[level])
                for kx, ky in chips:
                    slot = kx + 2 * ky - 1
                    c = copy(
                        gpre.at[:, pl.ds(0, SPANS[level]), :], gpa.at[:, rows, :],
                        o_send + slot, o_recv + 3 * level + slot, peer(kx, ky, 0)[0],
                    )
                    getattr(c, method)()

    def gpre_wait():
        for level in range(4):

            def wait(kx, ky):
                slot = kx + 2 * ky - 1
                copy(
                    gpre.at[:, pl.ds(0, SPANS[level]), :],
                    gpa.at[:, pl.ds(STARTS[level], SPANS[level]), :],
                    o_send + slot, o_recv + 3 * level + slot, peer(kx, ky, 0)[0],
                ).wait_recv()

            to_level_owner(level, wait)

    gpre_copies("start")
    for level in range(4):

        @pl.when(g == level)
        def _():
            gpa[:, STARTS[level]:STARTS[level] + SPANS[level], :] = gpre[:, 0:SPANS[level], :]

    due["gpre"] = gpre_wait
    finals.append(lambda: gpre_copies("wait_send"))

    middle_send(1)

    lt_send, lt_recv = names.take(3), names.take(3)
    weight_part = jnp.zeros((24, 128), f32)
    bias_part = jnp.zeros((24, 1), f32)
    for c in range(4):
        hidden_c = cn_s[1, 128 * c:128 * c + 128, :]
        lt[c] = dot(cwt[...], hidden_c, BOTH_LAST, FULL_ACCURACY)
        weight_part = weight_part + dot(sd[c], hidden_c, precision=FULL_ACCURACY)
        bias_part = bias_part + jnp.sum(sd[c], 1, keepdims=True)
    small[0:24, :] = weight_part
    small[24:48, :] = jnp.broadcast_to(bias_part, (24, 128))
    lt_copies = [
        copy(lt.at[lax.rem(z + j, 4)], ltr.at[j - 1], lt_send + j - 1, lt_recv + j - 1, zpeer(j)) for j in (1, 2, 3)
    ]
    each(lt_copies, "start")()
    due["lt"] = each(lt_copies, "wait_recv")
    finals.append(each(lt_copies, "wait_send"))

    weight_grad(yq, 1 - w)
    pl.when(w == 1)(lambda: dw_copy.start())

    def dw_sum():
        @pl.when(w == 0)
        def _():
            dw_copy.wait_recv()
            dw[1] = dw[1] + dwr[...]
            pl.when(yq == 0)(lambda: cg_out(dw.at[1]).start())
            pl.when(yq == 1)(lambda: dw_back.start())

    def dw_place():
        @pl.when((w == 1) & (yq == 1))
        def _():
            dw_back.wait_recv()
            cg_out(dwr).start()

        dw_copy.wait_send()

        @pl.when(w != yq)
        def _():
            dw_y.wait_recv()
            dw[0] = dwx[...].astype(f32)
            cg_out(dw.at[0]).start()

    due["dw"] = dw_sum
    due["dwy"] = dw_place
    finals.append(lambda: cg_out(dw.at[0]).wait())
    finals.append(lambda: pl.when(w == 1)(lambda: dw_y.wait_send()))
    finals.append(lambda: pl.when((w == 0) & (yq == 1))(lambda: dw_back.wait_send()))

    arrive("gpre")

    def split_rows(c, carry):
        high, low = halves(gpa[c])
        gpx[c, :, 0:128] = high
        gpx[c, :, 128:256] = low
        return carry

    lax.fori_loop(0, 4, split_rows, 0)

    def pooled_grad(c, carry):
        for level in range(4):
            rows = slice(STARTS[level], STARTS[level] + SPANS[level])
            gps[c, rows, :] = dot(gpx[c, rows, :], wb2[level], BOTH_LAST).astype(bf16)
        return carry

    lax.fori_loop(0, 4, pooled_grad, 0)
    p_send, p_recv = names.take(3), names.take(3)
    gp_copies = [
        copy(gps.at[lax.rem(z + j, 4)], gpr.at[j - 1], p_send + j - 1, p_recv + j - 1, zpeer(j)) for j in (1, 2, 3)
    ]
    each(gp_copies, "start")()
    due["gp"] = each(gp_copies, "wait_recv")
    finals.append(each(gp_copies, "wait_send"))

    for level in range(4):
        rows = slice(STARTS[level], STARTS[level] + SPANS[level])
        total = None
        for c in range(4):
            piece = dot(po[c, rows, :], gpx[c, rows, :], ROWS_T)
            total = piece if total is None else total + piece
        bg[level] = total[:, 0:128] + total[:, 128:256]
    bc_send, bc_recv = names.take(), names.take()
    w256 = pl.multiple_of(256 * w, 256)
    v256 = pl.multiple_of(256 * (1 - w), 256)
    bg_copy = copy(bg.at[:, pl.ds(v256, 256), :], bgr, bc_send, bc_recv, peer(0, 0, 1)[0])
    bg_copy.start()
    due["bgc"] = bg_copy.wait_recv
    finals.append(bg_copy.wait_send)

    bg_wait = due.pop("bgc")
    own_channels = pl.ds(pl.multiple_of(512 * g + 256 * w, 256), 256)
    bx_send, bx_recv = names.take(3), names.take(3)
    by_send, by_recv = names.take(4), names.take(4)

    def bga_of(block, core):
        return bga.at[:, pl.ds(pl.multiple_of(512 * block + 256 * core, 256), 256), :]

    def bg_chip(kx, ky):
        slot = kx + 2 * ky - 1
        return copy(bgh, bga_of(g, w), bx_send + slot, bx_recv + slot, peer(kx, ky, 0)[0])

    def bg_core(n, block):
        return copy(bga_of(block, w), bga_of(block, w), by_send + n, by_recv + n, peer(0, 0, 1)[0])

    bg_copies = [bg_chip(kx, ky) for kx, ky in chips]
    due["bg"] = each(bg_copies, "wait_recv")
    finals.append(each(bg_copies, "wait_send"))
    bg_own = bg_core(3, g)
    finals.append(bg_own.wait_send)
    due["by", 3] = bg_own.wait_recv

    def bg_sum():
        bg_wait()
        bgh[...] = (bg[:, pl.ds(w256, 256), :] + bgr[...]).astype(bf16)
        each(bg_copies, "start")()
        bga[:, own_channels, :] = bgh[...]
        bg_own.start()

    pl.when(w == 1)(bg_sum)

    middle_send(2)
    finals.append(scatter_sent)

    s_send, s_recv = names.take(7), names.take(7)

    def small_copy(n):
        return copy(small, smr.at[n], s_send + n, s_recv + n, peer(*plane[n])[0])

    small_copies = [small_copy(n) for n in range(7)]
    each(small_copies, "start")()
    due["small"] = each(small_copies, "wait_recv")
    finals.append(each(small_copies, "wait_send"))


    gp_wait = due.pop("gp")

    def ru_wait():
        pl.when(z > 0)(lambda: ru_copy(2).wait_recv())

    def rd_wait():
        pl.when(z < 3)(lambda: rd_copy(2).wait_recv())

    q_send, q_recv = names.take(8), names.take(8)

    def fg_copy(n):
        dev, _ = peer(*plane[n])
        rows = pl.ds(pl.multiple_of(256 * dev["wa"] + 64 * dev["ha"], 64), 64)
        return copy(fgh.at[rows, :], fgrad_out.at[w, :, pl.ds(g512, 512)], q_send + n, q_recv + n, dev)

    fg_copies = [fg_copy(n) for n in range(7)]
    finals.append(each(fg_copies, "wait_send"))
    fg_own = pltpu.make_async_copy(
        fgh.at[pl.ds(own_row, 64), :], fgrad_out.at[w, :, pl.ds(g512, 512)], sems.at[q_send + 7]
    )
    finals.append(fg_own.wait)

    def fg_wait():
        for n in range(7):
            dev, block = peer(*plane[n])
            copy(
                fgh.at[pl.ds(0, 64), :],
                fgrad_out.at[dev["wa"], :, pl.ds(pl.multiple_of(512 * block, 512), 512)],
                q_send + n, q_recv + n, dev,
            ).wait_recv()

    finals.append(fg_wait)

    def feature_grads():
        gp_wait()
        pooled_back = gps[z].astype(f32)
        for j in range(3):
            pooled_back = pooled_back + gpr[j].astype(f32)
        count = cnt[z]
        pieces = [pooled_back[:, 128 * chunk:128 * chunk + 128] / count for chunk in range(4)]
        high, low = halves(jnp.concatenate(pieces, 1))
        fg[...] = dot(mt[z], high, ROWS_T) + dot(mt[z], low, ROWS_T)
        ok = val[z]

        ru_wait()
        rd_wait()

        @pl.when(z > 0)
        def _():
            dxf[z] = dxf[z] + rxu[2].astype(f32)

        @pl.when(z < 3)
        def _():
            dxf[z] = dxf[z] + rxd[2].astype(f32)

        for chunk in range(4):
            cols = slice(128 * chunk, 128 * chunk + 128)
            fgh[:, cols] = (fg[:, cols] + dxf[z, :, cols] * ok).astype(bf16)
        each(fg_copies, "start")()
        fg_own.start()

    @pl.when(w == 0)
    def _():
        feature_grads()
        bg_sum()

    arrive("dw")

    arrive("lt")
    lts[w] = lt[z] + ltr[0] + ltr[1] + ltr[2]
    ls_send, ls_recv = names.take(), names.take()
    logits_copy = copy(lts.at[w], lts.at[w], ls_send, ls_recv, peer(0, 0, 1)[0])
    logits_copy.start()
    due["ls"] = logits_copy.wait_recv
    finals.append(logits_copy.wait_send)

    pl.when(w == 1)(feature_grads)

    arrive("bg")
    for n, (kx, ky) in enumerate(chips):
        item = bg_core(n, peer(kx, ky, 0)[1])
        item.start()
        finals.append(item.wait_send)
        due["by", n] = item.wait_recv

    arrive("small")
    total = small[...]
    for n in range(7):
        total = total + smr[n]
    small_out[0:48, :] = total[0:48]
    small_out[48:56, :] = total[48:56]
    for kx, ky in [(0, 0)] + chips:
        dev, block = peer(kx, ky, 0)
        mine = small[...] if kx + ky == 0 else smr[plane.index((kx, ky, 0))]
        both = mine + smr[plane.index((kx, ky, 1))]
        small_out[pl.ds(56 + block, 1), :] = both[50:51]
        small_out[pl.ds(60 + block, 1), :] = both[51:52]

    arrive("ls")
    for micro in range(2):
        square[:, 0:24] = lts[micro].T
        tile = square[pl.ds(w64, 64), 0:classes] + cb[...]
        logits_out[micro] = tile * tile_valid(micro)[:, 0:classes]

    for n in range(4):
        arrive(("by", n))
    out_sem = names.take()
    bg_out = pltpu.make_async_copy(bga, bgrad_out, sems.at[out_sem])
    bg_out.start()

    finals.append(bg_out.wait)

    arrive("dwy")

    for wait in finals:
        wait()
    assert not due
    assert names.count <= SEMAPHORES


SEMAPHORES = 256


def place_kernel(
    logits, fgrad, bgrad, small, cgrad,
    logits_out, fgrad_out, bgrad_out, gains_out, biases_out, cgrad_out, gain_out, bias_out, weight_out, class_out,
    low, wide, feats, feats_wide, taps, by_tap, square, sems,
):
    levels, classes, micros = bgrad.shape[0], class_out.shape[1], fgrad.shape[0]
    half = bgrad.shape[1] // 2
    pieces = [(n, pl.ds(half * h, half)) for n in range(levels) for h in range(2)]
    count = len(pieces)
    loads = [pltpu.make_async_copy(bgrad.at[p], low.at[p], sems.at[n]) for n, p in enumerate(pieces)]
    loads += [pltpu.make_async_copy(fgrad.at[m], feats.at[m], sems.at[count + m]) for m in range(micros)]
    tap_load = pltpu.make_async_copy(cgrad, taps, sems.at[count + micros])
    for load in loads:
        load.start()
    tap_load.start()
    first = count + micros + 1
    stores = [pltpu.make_async_copy(wide.at[p], bgrad_out.at[p], sems.at[first + n]) for n, p in enumerate(pieces)]
    stores += [
        pltpu.make_async_copy(feats_wide.at[m], fgrad_out.at[m], sems.at[first + count + m]) for m in range(micros)
    ]
    tap_stores = [
        pltpu.make_async_copy(by_tap.at[t], cgrad_out.at[t], sems.at[first + count + micros + t])
        for t in range(TAPS)
    ]
    for n, p in enumerate(pieces):
        loads[n].wait()
        wide[p] = low[p].astype(jnp.float32)
        stores[n].start()
    for m in range(micros):
        loads[count + m].wait()
        feats_wide[m] = feats[m].astype(jnp.float32)
        stores[count + m].start()
    tap_load.wait()
    for t, store in enumerate(tap_stores):
        by_tap[t] = taps[:, 128 * t:128 * t + 128]
        store.start()
    logits_out[...] = logits[...]
    gains_out[...] = small[56:60, :]
    biases_out[...] = small[60:64, :]
    gain_out[...] = small[49:50, :]
    bias_out[...] = small[48:49, :]
    weight_out[...] = small[0:classes, :]
    square[...] = small[...]
    class_out[...] = square[24:56, :].T[0:1, 0:classes]
    for store in stores + tap_stores:
        store.wait()


def canvas_body(
    mesh, features, region_boxes, branch_weight, branch_gain, branch_bias, conv_weight, norm_gain, norm_bias,
    class_weight, class_bias, cotangent,
):
    f32, bf16 = jnp.float32, jnp.bfloat16
    micros, tile_rows, tile_cols, channels = features.shape
    pixels = tile_rows * tile_cols
    classes = class_bias.shape[0]
    lane_table, row_table = bin_tables()

    vmem = pl.BlockSpec(memory_space=pltpu.VMEM)
    hbm = pl.BlockSpec(memory_space=pl.ANY)
    smem = pl.BlockSpec(memory_space=pltpu.SMEM)
    V = pltpu.VMEM
    scratch = [
        V((4, 512, 512), bf16),
        V((4, 512, 512), bf16),
        V((1024, 1152), bf16),
        V((4, 512, 256), bf16),
        V((4, 512, 256), bf16),
        V((4, 256, 512), bf16),
        V((4, BINS, 512), bf16),
        V((4, BINS, 128), f32),
        V((4, BINS, 512), bf16),
        V((4, BINS, 128), f32),
        V((3, 4, WIDE, 128), f32),
        V((4, WIDE, 128), bf16),
        V((4, 4, WIDE, 128), bf16),
        V((4, 256, 512), bf16),
        V((4, 512, 128), f32),
        V((2, 272, 1152), f32),
        V((4, 2, 256, 128), f32),
        V((3, 4, 2, 64, 128), f32),
        V((4, 2, 256, 128), bf16),
        V((4, 512, 1152), bf16),
        V((3, 2, 272, 128), f32),
        V((4, 256, 1152), bf16),
        V((4, 512, 512), f32),
        V((3, 512, 512), bf16),
        V((3, 512, 512), bf16),
        V((3, 512, 512), bf16),
        V((3, 512, 512), bf16),
        V((4, 4, WIDE, 128), bf16),
        V((3, 4, WIDE, 128), bf16),
        V((4, WIDE, 128), f32),
        V((4, BINS, 128), f32),
        V((4, BINS, 256), bf16),
        V((4, BINS, 512), bf16),
        V((3, BINS, 512), bf16),
        V((2, 512, 1152), f32),
        V((512, 1152), f32),
        V((4, 512, 128), f32),
        V((4, 256, 128), f32),
        V((4, 256, 128), bf16),
        V((1, 24, 128), f32),
        V((4, 24, 128), f32),
        V((4, 24, 128), f32),
        V((3, 24, 128), f32),
        V((2, 24, 128), f32),
        V((2, 8, 128), f32),
        V((2, 3, 8, 128), f32),
        V((56, 128), f32),
        V((7, 56, 128), f32),
        V((4, WIDE, 128), f32),
        V((4, WIDE, 128), f32),
        V((2, 512, 128), f32),
        V((4, channels, 128), bf16),
        V((512, 512), f32),
        V((512, 512), bf16),
        V((24, 128), f32),
        V((2, 24, 128), f32),
        V((128, 128), f32),
        V((512, 1152), bf16),
        V((512, 1152), bf16),
        V((8, 128), f32),
        pltpu.SemaphoreType.DMA((SEMAPHORES,)),
        pltpu.SemaphoreType.REGULAR((2,)),
    ]
    share = conv_weight.shape[2]
    parts = pl.pallas_call(
        head_kernel,
        out_shape=(
            jax.ShapeDtypeStruct((micros, pixels, classes), f32),
            jax.ShapeDtypeStruct((micros, pixels, channels), bf16),
            jax.ShapeDtypeStruct((4, channels, share), bf16),
            jax.ShapeDtypeStruct((64, 128), f32),
            jax.ShapeDtypeStruct((512, TAPS * share), f32),
        ),
        in_specs=[smem, vmem, vmem, hbm, vmem, hbm, hbm, vmem, vmem, vmem, vmem, vmem, vmem],
        out_specs=(vmem, hbm, hbm, vmem, hbm),
        scratch_shapes=scratch,
        compiler_params=pltpu.CompilerParams(
            collective_id=0, has_side_effects=True, vmem_limit_bytes=60 * 2**20
        ),
    )(
        jnp.transpose(region_boxes, (1, 2, 0)), lane_table, row_table, features.reshape(micros, pixels, channels),
        cotangent.reshape(micros, pixels, classes), conv_weight, branch_weight, branch_gain, branch_bias,
        norm_gain.reshape(1, -1), norm_bias.reshape(1, -1), class_weight.T, class_bias.reshape(1, -1),
    )
    logits, feature_grad, branch_grad, gains, biases, conv_grad, gain, bias, weight, class_grad = pl.pallas_call(
        place_kernel,
        out_shape=(
            jax.ShapeDtypeStruct((micros, pixels, classes), f32),
            jax.ShapeDtypeStruct((micros, pixels, channels), f32),
            jax.ShapeDtypeStruct((4, channels, share), f32),
            jax.ShapeDtypeStruct((4, share), f32),
            jax.ShapeDtypeStruct((4, share), f32),
            jax.ShapeDtypeStruct((TAPS, 512, share), f32),
            jax.ShapeDtypeStruct((1, share), f32),
            jax.ShapeDtypeStruct((1, share), f32),
            jax.ShapeDtypeStruct((classes, share), f32),
            jax.ShapeDtypeStruct((1, classes), f32),
        ),
        in_specs=[vmem, hbm, hbm, vmem, hbm],
        out_specs=(vmem, hbm, hbm, vmem, vmem, hbm, vmem, vmem, vmem, vmem),
        scratch_shapes=[
            V((4, channels, share), bf16), V((4, channels, share), f32), V((micros, pixels, channels), bf16),
            V((micros, pixels, channels), f32), V((512, TAPS * share), f32), V((TAPS, 512, share), f32), V((64, 128), f32),
            pltpu.SemaphoreType.DMA((40,)),
        ],
        compiler_params=pltpu.CompilerParams(vmem_limit_bytes=60 * 2**20),
    )(*parts)
    return (
        logits.reshape(micros, tile_rows, tile_cols, classes),
        feature_grad.reshape(features.shape),
        branch_grad,
        gains,
        biases,
        conv_grad,
        gain.reshape(-1),
        bias.reshape(-1),
        weight.T,
        class_grad.reshape(-1),
    )


def extended(block, sides, width):
    for axis, dim in sides:
        count = lax.axis_size(axis)
        forward = [(i, i + 1) for i in range(count - 1)]
        backward = [(target, source) for source, target in forward]
        low = lax.ppermute(
            lax.slice_in_dim(block, block.shape[dim] - width, None, axis=dim), axis, forward
        )
        high = lax.ppermute(lax.slice_in_dim(block, 0, width, axis=dim), axis, backward)
        block = jnp.concatenate([low, block, high], axis=dim)
    return block


def interpolate(offset, extent, n, bin_ids):
    scaled = offset * (n - 1)
    lower_bin = scaled // (extent - 1)
    fraction = (scaled - lower_bin * (extent - 1)).astype(jnp.float32) / (extent - 1).astype(
        jnp.float32
    )
    upper_bin = jnp.minimum(lower_bin + 1, n - 1)
    lower_hit = (bin_ids[None, :] == lower_bin[:, None]).astype(jnp.float32)
    upper_hit = (bin_ids[None, :] == upper_bin[:, None]).astype(jnp.float32)
    return (1.0 - fraction)[:, None] * lower_hit + fraction[:, None] * upper_hit


def layout(region, row_ids, col_ids):
    member_cols = []
    count_cols = []
    weight_per_level = []
    validity = jnp.zeros(row_ids.shape, jnp.float32)
    for n in LEVELS:
        bin_ids = jnp.arange(n, dtype=jnp.int32)
        level_weights = []
        for k in range(region.shape[0]):
            row_start = region[k, 0]
            col_start = region[k, 1]
            height = region[k, 2] - row_start
            width = region[k, 3] - col_start
            row_offset = row_ids - row_start
            col_offset = col_ids - col_start
            inside = (
                (row_offset >= 0) & (row_offset < height) & (col_offset >= 0) & (col_offset < width)
            )
            row_low = bin_ids * height // n
            row_high = ((bin_ids + 1) * height + n - 1) // n
            col_low = bin_ids * width // n
            col_high = ((bin_ids + 1) * width + n - 1) // n
            row_in = (row_offset[:, None] >= row_low[None, :]) & (
                row_offset[:, None] < row_high[None, :]
            )
            col_in = (col_offset[:, None] >= col_low[None, :]) & (
                col_offset[:, None] < col_high[None, :]
            )
            member = row_in[:, :, None] & col_in[:, None, :] & inside[:, None, None]
            member_cols.append(member.reshape(-1, n * n).astype(jnp.float32))
            count_cols.append(
                ((row_high - row_low)[:, None] * (col_high - col_low)[None, :]).reshape(n * n)
            )
            row_weight = interpolate(row_offset, height, n, bin_ids)
            col_weight = interpolate(col_offset, width, n, bin_ids)
            bilinear = (
                row_weight[:, :, None]
                * col_weight[:, None, :]
                * inside.astype(jnp.float32)[:, None, None]
            )
            level_weights.append(bilinear.reshape(-1, n * n))
            if n == 1:
                validity = validity + inside.astype(jnp.float32)
        weight_per_level.append(jnp.concatenate(level_weights, 1))
    counts = jnp.concatenate(count_cols).astype(jnp.float32)
    return (jnp.concatenate(member_cols, 1), weight_per_level, counts, validity)


def silu_slope(inputs):
    logistic = jax.nn.sigmoid(inputs)
    return logistic * (1.0 + inputs * (1.0 - logistic))


def tiled_body(
    features,
    region_boxes,
    branch_weight,
    branch_gain,
    branch_bias,
    conv_weight,
    norm_gain,
    norm_bias,
    class_weight,
    class_bias,
    cotangent,
):
    micros, tile_rows, tile_cols, channels = features.shape
    groups = lax.axis_size("col")
    regions = region_boxes.shape[1]
    share = conv_weight.shape[2]
    width_out = share * groups
    pixels = tile_rows * tile_cols
    flat_rows = groups * pixels
    col_index = lax.axis_index("col")
    tile_row_ids = lax.axis_index("ha") * tile_rows + jnp.arange(tile_rows, dtype=jnp.int32)
    tile_col_ids = lax.axis_index("wa") * tile_cols + jnp.arange(tile_cols, dtype=jnp.int32)
    row_ids = jnp.repeat(tile_row_ids, tile_cols)
    col_ids = jnp.tile(tile_col_ids, tile_rows)
    conv_flat = conv_weight.reshape(-1, share)
    conv_back = jnp.transpose(conv_weight, (0, 2, 1)).reshape(-1, conv_weight.shape[1])
    spans = [regions * n * n for n in LEVELS]
    starts = [sum(spans[:level_number]) for level_number in range(len(LEVELS))]
    grouped_boxes = region_boxes.reshape(groups, micros, regions, 4)
    branch_float = branch_weight.astype(jnp.float32)
    branch_grads = [jnp.zeros((channels, share), jnp.float32) for level_number in range(4)]
    branch_gain_grads = [jnp.zeros((share,), jnp.float32) for level_number in range(4)]
    branch_bias_grads = [jnp.zeros((share,), jnp.float32) for level_number in range(4)]
    norm_gain_total = jnp.zeros((share,), jnp.float32)
    norm_bias_total = jnp.zeros((share,), jnp.float32)
    class_weight_total = jnp.zeros(class_weight.shape, jnp.float32)
    class_bias_total = jnp.zeros(class_bias.shape, jnp.float32)
    conv_total = jnp.zeros(conv_flat.shape, jnp.float32)
    logit_list = []
    feature_list = []
    for m in range(micros):
        boxes_now = grouped_boxes[:, m]
        member_pixels, weight_per_level, counts, validity = jax.vmap(
            lambda region: layout(region, row_ids, col_ids)
        )(boxes_now)
        own_members = lax.dynamic_index_in_dim(member_pixels, col_index, 0, False)
        own_counts = lax.dynamic_index_in_dim(counts, col_index, 0, False)
        own_valid = lax.dynamic_index_in_dim(validity, col_index, 0, False)
        areas = (boxes_now[:, :, 2] - boxes_now[:, :, 0]) * (
            boxes_now[:, :, 3] - boxes_now[:, :, 1]
        )
        valid_total = jnp.sum(areas.astype(jnp.float32))
        local_x = features[m].reshape(pixels, channels)
        partial_value = jnp.einsum(
            "pb,pd->bd",
            own_members.astype(jnp.bfloat16),
            local_x,
            preferred_element_type=jnp.float32,
        )
        bin_total = lax.psum(partial_value, ("ha", "wa"))
        pooled = (bin_total / own_counts[:, None]).astype(jnp.bfloat16)
        pooled_all = lax.all_gather(pooled[None], "col", axis=0, tiled=True)
        branch_norms = []
        branch_affines = []
        branch_inverse = []
        branch_outs = []
        for level_number in range(4):
            level_pooled = pooled_all[
                :, starts[level_number] : starts[level_number] + spans[level_number]
            ]
            pre = jnp.einsum(
                "cbd,de->cbe",
                level_pooled,
                branch_weight[level_number],
                preferred_element_type=jnp.float32,
            )
            average = jnp.mean(pre, (0, 1))
            spread = jnp.mean(pre * pre, (0, 1)) - average * average
            inverse = lax.rsqrt(spread + EPSILON)
            normed_branch = (pre - average) * inverse
            affine_branch = branch_gain[level_number] * normed_branch + branch_bias[level_number]
            branch_norms.append(normed_branch)
            branch_affines.append(affine_branch)
            branch_inverse.append(inverse)
            branch_outs.append(jax.nn.silu(affine_branch))
        branch_local = jnp.concatenate(branch_outs, 1).astype(jnp.bfloat16)
        branch_full = lax.all_gather(branch_local, "col", axis=2, tiled=True)
        enlarged_map = []
        for level_number in range(4):
            level_output = branch_full[
                :, starts[level_number] : starts[level_number] + spans[level_number]
            ].astype(jnp.float32)
            spread_out = jnp.einsum(
                "zdw,zwk->zdk",
                weight_per_level[level_number],
                level_output,
                precision=FULL_ACCURACY,
            )
            enlarged_map.append(
                spread_out.reshape(groups, tile_rows, tile_cols, width_out).astype(jnp.bfloat16)
            )
        x_all = lax.all_gather(features[m][None], "col", axis=0, tiled=True)
        masked_x = x_all * validity.reshape(groups, tile_rows, tile_cols, 1).astype(jnp.bfloat16)
        stacked = jnp.concatenate([masked_x] + enlarged_map, -1)
        padded = extended(stacked, (("ha", 1), ("wa", 2)), 1)
        columns = jnp.concatenate(
            [
                padded[:, row_tap : row_tap + tile_rows, col_tap : col_tap + tile_cols]
                for row_tap in range(3)
                for col_tap in range(3)
            ],
            -1,
        ).reshape(flat_rows, -1)
        convolved = jnp.dot(columns, conv_flat, preferred_element_type=jnp.float32)
        valid_flat = validity.reshape(flat_rows, 1)
        first_sum, second_sum = lax.psum(
            (jnp.sum(convolved * valid_flat, 0), jnp.sum(convolved * convolved * valid_flat, 0)),
            ("ha", "wa"),
        )
        average = first_sum / valid_total
        spread = second_sum / valid_total - average * average
        inverse = lax.rsqrt(spread + EPSILON)
        normed = (convolved - average) * inverse
        affine = norm_gain * normed + norm_bias
        hidden = jax.nn.silu(affine)
        part_logits = jnp.dot(hidden, class_weight, precision=FULL_ACCURACY).reshape(
            groups, tile_rows, tile_cols, -1
        )
        summed = lax.psum_scatter(part_logits, "col", scatter_dimension=0, tiled=True)
        own_valid_tile = own_valid.reshape(tile_rows, tile_cols, 1)
        logit_list.append((summed[0] + class_bias) * own_valid_tile)
        seed = (cotangent[m] * own_valid_tile)[None]
        seed_all = lax.all_gather(seed, "col", axis=0, tiled=True).reshape(flat_rows, -1)
        grad_hidden = jnp.dot(seed_all, class_weight.T, precision=FULL_ACCURACY)
        grad_affine = grad_hidden * silu_slope(affine)
        bias_sum, gain_sum, class_part, bias_part = lax.psum(
            (
                jnp.sum(grad_affine, 0),
                jnp.sum(grad_affine * normed, 0),
                jnp.dot(hidden.T, seed_all, precision=FULL_ACCURACY),
                jnp.sum(seed_all, 0),
            ),
            ("ha", "wa"),
        )
        norm_bias_total = norm_bias_total + bias_sum
        norm_gain_total = norm_gain_total + gain_sum
        class_weight_total = class_weight_total + class_part
        class_bias_total = class_bias_total + bias_part
        grad_conv = (
            valid_flat
            * inverse
            * (
                grad_affine * norm_gain
                - norm_gain * bias_sum / valid_total
                - normed * norm_gain * gain_sum / valid_total
            )
        )
        grad_low = grad_conv.astype(jnp.bfloat16)
        grad_pad = extended(
            grad_low.reshape(groups, tile_rows, tile_cols, share), (("ha", 1), ("wa", 2)), 1
        )
        grad_columns = jnp.concatenate(
            [
                grad_pad[
                    :, 2 - row_tap : 2 - row_tap + tile_rows, 2 - col_tap : 2 - col_tap + tile_cols
                ]
                for row_tap in range(3)
                for col_tap in range(3)
            ],
            -1,
        ).reshape(flat_rows, -1)
        grad_stacked = jnp.dot(grad_columns, conv_back, preferred_element_type=jnp.float32)
        conv_part = jnp.einsum("pk,pe->ke", columns, grad_low, preferred_element_type=jnp.float32)
        conv_total = conv_total + conv_part
        grad_x = grad_stacked[:, :channels]
        bin_parts = []
        for level_number in range(4):
            level_gradient = grad_stacked[
                :, channels + level_number * width_out : channels + (level_number + 1) * width_out
            ].reshape(groups, pixels, width_out)
            bin_parts.append(
                jnp.einsum(
                    "qkl,qko->qlo",
                    weight_per_level[level_number],
                    level_gradient,
                    precision=FULL_ACCURACY,
                )
            )
        bin_local = jnp.concatenate(bin_parts, 1)
        bin_grad = lax.psum(bin_local, ("ha", "wa", "col"))
        own_bin_grad = lax.dynamic_slice_in_dim(bin_grad, col_index * share, share, 2)
        grad_pres = []
        for level_number in range(4):
            grad_out = own_bin_grad[
                :, starts[level_number] : starts[level_number] + spans[level_number]
            ]
            grad_act = grad_out * silu_slope(branch_affines[level_number])
            act_sum = jnp.sum(grad_act, (0, 1))
            act_norm_sum = jnp.sum(grad_act * branch_norms[level_number], (0, 1))
            samples = float(groups * spans[level_number])
            branch_bias_grads[level_number] = branch_bias_grads[level_number] + act_sum
            branch_gain_grads[level_number] = branch_gain_grads[level_number] + act_norm_sum
            grad_pre = branch_inverse[level_number] * (
                branch_gain[level_number] * grad_act
                - branch_gain[level_number] * act_sum / samples
                - branch_norms[level_number] * branch_gain[level_number] * act_norm_sum / samples
            )
            level_pooled = pooled_all[
                :, starts[level_number] : starts[level_number] + spans[level_number]
            ].astype(jnp.float32)
            branch_grads[level_number] = branch_grads[level_number] + jnp.einsum(
                "cbd,cbe->de", level_pooled, grad_pre, precision=FULL_ACCURACY
            )
            grad_pres.append(grad_pre)
        pooled_grads = [
            jnp.einsum(
                "cbe,de->cbd",
                grad_pres[level_number],
                branch_float[level_number],
                precision=FULL_ACCURACY,
            )
            for level_number in range(4)
        ]
        grad_pooled = jnp.concatenate(pooled_grads, 1)
        back_x, back_pooled = (
            lax.psum_scatter(
                grad_x.reshape(groups, pixels, channels).astype(jnp.bfloat16),
                "col",
                scatter_dimension=0,
                tiled=True,
            ).astype(jnp.float32),
            lax.psum_scatter(
                grad_pooled.astype(jnp.bfloat16), "col", scatter_dimension=0, tiled=True
            ).astype(jnp.float32),
        )
        pooled_back = back_pooled[0]
        spread_back = jnp.dot(
            own_members, pooled_back / own_counts[:, None], precision=FULL_ACCURACY
        )
        feature_list.append(
            (back_x[0] * own_valid[:, None] + spread_back).reshape(tile_rows, tile_cols, channels)
        )
    conv_result = lax.psum_scatter(
        conv_total.reshape(9, -1, share), ("ha", "wa"), scatter_dimension=1, tiled=True
    )
    return (
        jnp.stack(logit_list),
        jnp.stack(feature_list),
        jnp.stack(branch_grads),
        jnp.stack(branch_gain_grads),
        jnp.stack(branch_bias_grads),
        conv_result,
        norm_gain_total,
        norm_bias_total,
        class_weight_total,
        class_bias_total,
    )


def solution(mesh):
    placed = (
        P("col", "ha", "wa", None),
        P(),
        P(None, None, "col"),
        P(None, "col"),
        P(None, "col"),
        P(None, None, "col"),
        P("col"),
        P("col"),
        P("col", None),
        P(),
        P("col", "ha", "wa", None),
    )
    return jax.shard_map(
        functools.partial(canvas_body, mesh) if whole_canvas_plan(mesh) else tiled_body,
        mesh=mesh,
        in_specs=placed,
        out_specs=(
            P("col", "ha", "wa", None),
            P("col", "ha", "wa", None),
            P(None, None, "col"),
            P(None, "col"),
            P(None, "col"),
            P(None, ("ha", "wa"), "col"),
            P("col"),
            P("col"),
            P("col", None),
            P(),
        ),
        check_vma=False,
    )
```
